32 devices in a mesh: tilt: 4 (over x, core), tile: 8 (over z, y).
Axes of the slice: x: 2, y: 2, z: 4, core: 2. Of those that a mesh axis runs over, the one named last changes fastest.
Arguments:
- obj_re: float32 [4, 1024, 3072], P('tilt', None, 'tile'), may hold values from -6 to 6
- obj_im: float32 [4, 1024, 3072], P('tilt', None, 'tile'), may hold values from -6 to 6
- probe_re: float32 [256, 256], replicated, may hold values from -3 to 3
- probe_im: float32 [256, 256], replicated, may hold values from -3 to 3
- intensity: float32 [4, 64, 256, 256], P('tilt', 'tile'), may hold values from 0.25 to 4
- positions: int32 [4, 64, 2], P('tilt', 'tile'), may hold values from 0 to 768, as said below
- counts: int32 [4, 8], P('tilt', 'tile'), may hold values from 1 to 8, as said below
- row_shift: int32 [4], P('tilt'), may hold values from 0 to 1023
- slope: int32 [4], replicated, may hold values from -384 to 384
- volume: float32 [16, 1024, 3072], P(None, ('tilt', 'tile')), may hold values from -1.5 to 1.5
Outputs:
- volume_new: float32 [16, 1024, 3072], P(None, ('tilt', 'tile'))
- reprojection: float32 [4, 1024, 3072], P('tilt', None, 'tile')
- object_gradient: float32 [2, 4, 1024, 3072], P(None, 'tilt', None, 'tile')
The draws below stay inside these ranges and needn't reach their ends.
Inputs may be any that keep to these rules, and one draw needn't show every extreme that they name: `positions`: each slot's row lies in 0 to 768 and its column in 0 to 256; slots from counts on are unused. `counts`: at least one tile uses all 8 slots.
All inputs are finite; a program needn't handle non-finite values.
Results may differ from the reference program's by a relative error of at most 0.0003.
Values sent between devices are 32-bit elements; how exact they have to be, the bound alone decides.
No kernel may reach another device: no remote copies, remote signals or barrier semaphores. Data moves between devices by JAX's collectives and lax.ppermute only.
A program may use at most 128 MiB of HBM per device.

```python
import math
import jax
import jax.numpy as jnp
from jax import lax

TW = 384
PROBE_SIDE = 256
MG = 128
TH = 1024
NPMAX = 8
Z = 16
X = 3072
SLOTS = 64
N_TILT = 4
N_TILE = 8


def draw_positions(key, part):
    rows = jax.random.randint(jax.random.fold_in(key, 11), (N_TILT, SLOTS, 1), 0, TH - PROBE_SIDE + 1, dtype=jnp.int32)
    cols = jax.random.randint(jax.random.fold_in(key, 12), (N_TILT, SLOTS, 1), 0, TW + MG - PROBE_SIDE + 1, dtype=jnp.int32)
    return jnp.concatenate([rows, cols], axis=2)


def draw_counts(key, part):
    base = jax.random.randint(jax.random.fold_in(key, 21), (N_TILT, N_TILE), 1, min(3, NPMAX) + 1, dtype=jnp.int32)
    heavy = jax.random.randint(jax.random.fold_in(key, 22), (N_TILT, N_TILE), 0, 8, dtype=jnp.int32) == 0
    filled = jnp.where(heavy, NPMAX, base).reshape(-1)
    chosen = jax.random.randint(jax.random.fold_in(key, 23), (), 0, N_TILT * N_TILE, dtype=jnp.int32)
    filled = filled.at[chosen].set(NPMAX)
    return filled.reshape(N_TILT, N_TILE).astype(jnp.int32)


def place_ends(result, stream_key, least, top_value):
    longest = result.shape.index(max(result.shape))
    spots = []
    for shift in (0, 1):
        where = [jax.random.randint(jax.random.fold_in(stream_key, axis), (), 0, length) for axis, length in enumerate(result.shape)]
        where[longest] = (where[longest] + shift) % result.shape[longest]
        spots.append(tuple(where))
    return result.at[spots[0]].set(least).at[spots[1]].set(top_value)


def level_of(own_key, shape, cuts, smallest, high):
    loudness, own = 1.0, jax.random.fold_in(own_key, 6)
    for position, blocks in cuts:
        heights = jnp.exp(jax.random.uniform(jax.random.fold_in(own, position), (blocks,), jnp.float32, smallest / len(cuts), high / len(cuts)))
        loudness = loudness * jnp.repeat(heights, shape[position] // blocks).reshape([-1 if axis == position else 1 for axis in range(len(shape))])
    return loudness


def noise(stream_key, extent, width, limit, cuts=(), held_as=jnp.bfloat16):
    result = width * jax.random.normal(stream_key, extent, jnp.float32)
    if cuts:
        result = result * level_of(stream_key, extent, cuts, -0.22, 0.18)
    return jnp.clip(result, -limit, limit).astype(held_as)


def setup_inputs(seed: int = 0) -> dict:
    key_list = jax.random.split(jax.random.key(seed), 11)
    obj_re = noise(key_list[0], (N_TILT, TH, X), 1.0, 6.0, ((0, 4), (2, 8)), jnp.float32)
    obj_im = noise(key_list[1], (N_TILT, TH, X), 1.0, 6.0, ((0, 4), (2, 8)), jnp.float32)
    probe_re = noise(key_list[2], (PROBE_SIDE, PROBE_SIDE), 0.5, 3.0, (), jnp.float32)
    probe_im = noise(key_list[3], (PROBE_SIDE, PROBE_SIDE), 0.5, 3.0, (), jnp.float32)
    intensity = jnp.clip(jnp.exp(math.log(4.0) - 2.7725887 * jax.random.uniform(key_list[4], (N_TILT, SLOTS, PROBE_SIDE, PROBE_SIDE), jnp.float32) ** level_of(key_list[4], (N_TILT, SLOTS, PROBE_SIDE, PROBE_SIDE), ((0, 4), (1, 8)), -0.2, 0.2)), 0.25, 4.0)
    positions = draw_positions(jax.random.fold_in(key_list[10], 71), 0)
    counts = draw_counts(jax.random.fold_in(key_list[10], 71), 0)
    row_shift = place_ends(jax.random.randint(key_list[7], (N_TILT,), 0, TH), jax.random.fold_in(key_list[7], 1), 0, TH - 1).astype(jnp.int32)
    slope = place_ends(jax.random.randint(key_list[8], (N_TILT,), 0 - TW, TW + 1), jax.random.fold_in(key_list[8], 1), 0 - TW, TW).astype(jnp.int32)
    volume = noise(key_list[9], (Z, TH, X), Z ** -0.5, 1.5, ((1, 32),), jnp.float32)
    return dict(obj_re=obj_re, obj_im=obj_im, probe_re=probe_re, probe_im=probe_im, intensity=intensity, positions=positions, counts=counts, row_shift=row_shift, slope=slope, volume=volume)


def product(left, right):
    return jnp.dot(left, right, precision=lax.Precision.HIGHEST, preferred_element_type=jnp.float32)

def complex_product(ar, ai, br, bi):
    return (product(ar, br) - product(ai, bi), product(ar, bi) + product(ai, br))

def dft_tables(length):
    index = jnp.arange(length, dtype=jnp.int32)
    phase = index[:, None] * index[None, :] % length
    angle = phase.astype(jnp.float32) * (-2.0 * math.pi / length)
    factor = 1.0 / math.sqrt(length)
    return (jnp.cos(angle) * factor, jnp.sin(angle) * factor)

def probe_gradient(o_re, o_im, p_re, p_im, measured, w_re, w_im):
    psi_re = p_re * o_re - p_im * o_im
    psi_im = p_re * o_im + p_im * o_re
    half_re, half_im = complex_product(w_re, w_im, psi_re, psi_im)
    far_re, far_im = complex_product(half_re, half_im, w_re, w_im)
    excess = far_re * far_re + far_im * far_im - measured
    back_re, back_im = complex_product(w_re, -w_im, excess * far_re, excess * far_im)
    chi_re, chi_im = complex_product(back_re, back_im, w_re, -w_im)
    return (p_re * chi_re + p_im * chi_im, p_re * chi_im - p_im * chi_re)

def shift_weights(tilt_slope, depth):
    levels = jnp.arange(depth, dtype=jnp.int32)
    numer = levels * tilt_slope
    whole = jnp.floor_divide(numer, depth)
    frac = (numer - whole * depth).astype(jnp.float32) / depth
    return (whole, frac)

def roll_columns(field, amount):
    return jnp.roll(field, amount, axis=-1)

def volume_update(routed, volume, slope):
    tilts = routed.shape[0]
    depth = volume.shape[0]
    roll_one = jax.vmap(roll_columns, in_axes=(None, 0))
    roll_many = jax.vmap(roll_columns, in_axes=(0, 0))
    grand_total = jnp.zeros_like(volume)
    for tilt in range(tilts):
        whole, frac = shift_weights(slope[tilt], depth)
        near = roll_one(routed[tilt], -whole)
        further = roll_one(routed[tilt], -whole - 1)
        grand_total = grand_total + (1.0 - frac)[:, None, None] * near + frac[:, None, None] * further
    fresh = volume + grand_total / tilts
    projections = []
    for tilt in range(tilts):
        whole, frac = shift_weights(slope[tilt], depth)
        near = roll_many(fresh, whole)
        further = roll_many(fresh, whole + 1)
        projections.append(lax.optimization_barrier(jnp.sum((1.0 - frac)[:, None, None] * near + frac[:, None, None] * further, axis=0)))
    return (fresh, jnp.stack(projections))

def reference(obj_re, obj_im, probe_re, probe_im, intensity, positions, counts, row_shift, slope, volume):
    w_re, w_im = dft_tables(PROBE_SIDE)
    ext_re = jnp.pad(obj_re, ((0, 0), (0, 0), (0, MG)))
    ext_im = jnp.pad(obj_im, ((0, 0), (0, 0), (0, MG)))
    grand_total = N_TILT * SLOTS
    order = jnp.arange(grand_total, dtype=jnp.int32)
    tilt_lookup = order // SLOTS
    tile_lookup = order % SLOTS // NPMAX
    slot_lookup = order % NPMAX
    flattened_scan_points = positions.reshape(grand_total, 2)
    flattened_measurements = intensity.reshape(grand_total, PROBE_SIDE, PROBE_SIDE)

    def visit_order(carry, item):
        running_real, running_imaginary = carry
        tilt, tile, slot, place, measured = item
        row = place[0].astype(jnp.int32)
        col = (place[1] + tile * TW).astype(jnp.int32)
        start = (tilt.astype(jnp.int32), row, col)
        o_re = lax.dynamic_slice(ext_re, start, (1, PROBE_SIDE, PROBE_SIDE))[0]
        o_im = lax.dynamic_slice(ext_im, start, (1, PROBE_SIDE, PROBE_SIDE))[0]
        g_re, g_im = probe_gradient(o_re, o_im, probe_re, probe_im, measured, w_re, w_im)
        live = (slot < counts[tilt, tile]).astype(jnp.float32)
        old_re = lax.dynamic_slice(running_real, start, (1, PROBE_SIDE, PROBE_SIDE))
        old_im = lax.dynamic_slice(running_imaginary, start, (1, PROBE_SIDE, PROBE_SIDE))
        running_real = lax.dynamic_update_slice(running_real, old_re + live * g_re[None], start)
        running_imaginary = lax.dynamic_update_slice(running_imaginary, old_im + live * g_im[None], start)
        return ((running_real, running_imaginary), None)
    vacant_marker = jnp.zeros((N_TILT, TH, X + MG), jnp.float32)
    (running_real, running_imaginary), ignored_item = lax.scan(visit_order, (vacant_marker, vacant_marker), (tilt_lookup, tile_lookup, slot_lookup, flattened_scan_points, flattened_measurements))
    grad_re = running_real[:, :, :X]
    grad_im = running_imaginary[:, :, :X]
    residual = obj_re * grad_im - obj_im * grad_re
    roll_rows = jax.vmap(lambda field, amount: jnp.roll(field, amount, axis=0))
    routed = roll_rows(residual, row_shift)
    rows_block = 128 if TH % 128 == 0 else TH
    blocks = TH // rows_block
    routed_blocks = routed.reshape(N_TILT, blocks, rows_block, X).transpose(1, 0, 2, 3)
    volume_blocks = volume.reshape(Z, blocks, rows_block, X).transpose(1, 0, 2, 3)
    fresh_blocks, proj_blocks = lax.map(lambda pair: volume_update(pair[0], pair[1], slope), (routed_blocks, volume_blocks))
    fresh = fresh_blocks.transpose(1, 0, 2, 3).reshape(Z, TH, X)
    proj = proj_blocks.transpose(1, 0, 2, 3).reshape(N_TILT, TH, X)
    reprojection = roll_rows(proj, -row_shift)
    return (fresh, reprojection, jnp.stack([grad_re, grad_im]))
```

```python
import functools
import math

import jax
import jax.numpy as jnp
import ml_dtypes
import numpy as np
from jax import lax
from jax.experimental import pallas as pl
from jax.experimental.pallas import tpu as pltpu
from jax.sharding import PartitionSpec as P

LANES = 128
SUBLANES = 8
VMEM_BYTES = 60 * 1024 * 1024
SPLIT = jnp.bfloat16
ANY = pl.BlockSpec(memory_space=pl.ANY)
SMEM = pl.BlockSpec(memory_space=pltpu.SMEM)
VMEM = pl.BlockSpec(memory_space=pltpu.VMEM)


def passed_along(block, axis, distance):
    devices = range(lax.axis_size(axis))
    route = [(i - distance, i) for i in devices if i - distance in devices]
    return lax.ppermute(block, axis, route)


def halves(table):
    high = table.astype(ml_dtypes.bfloat16)
    low = (table - high.astype(np.float64)).astype(ml_dtypes.bfloat16)
    return high, low


def dft_tables(length):
    half = length // 2
    index = np.arange(length)
    angle = (index[:, None] * index[None, :] % length) * (-2.0 * math.pi / length)
    wave = (np.cos(angle) + 1j * np.sin(angle)) / math.sqrt(length)
    tables = []
    for parity in (0, 1):
        part = wave[parity::2, :half]
        pair = np.block([[part.real, -part.imag], [part.imag, part.real]])
        tables += [*halves(pair), *halves(pair.T)]
    order = np.concatenate([index[0::2], index[1::2]])
    spread = np.zeros((length, length))
    spread[order, index] = 1.0
    return np.stack(tables), spread.astype(ml_dtypes.bfloat16)


def split(x):
    high = x.astype(SPLIT)
    return high, (x - high.astype(jnp.float32)).astype(SPLIT)


def dot(a, b):
    return jnp.dot(a, b, preferred_element_type=jnp.float32)


def dot3(ah, al, bh, bl):
    return dot(ah, bh) + dot(ah, bl) + dot(al, bh)


def lanes_of(shape):
    return lax.broadcasted_iota(jnp.int32, shape, len(shape) - 1)


def rows_of(shape):
    return lax.broadcasted_iota(jnp.int32, shape, len(shape) - 2)


def rolled(x, row, lane):
    size = x.shape[0]
    tiles = x.shape[1] // LANES
    cut = []
    for tile in range(tiles):
        part = x[:, tile * LANES : (tile + 1) * LANES].reshape(-1, SUBLANES, LANES)
        turned = pltpu.roll(part, row, axis=1)
        before = jnp.concatenate([turned[-1:], turned[:-1]], axis=0)
        part = jnp.where(rows_of(part.shape) < row, before, turned).reshape(size, LANES)
        cut.append(pltpu.roll(part, lane, axis=1))
    keep = lanes_of(cut[0].shape) >= lane
    return [jnp.where(keep, cut[tile], cut[tile - 1]) for tile in range(tiles)]


def probe_kernel(
    used_ref, positions_ref, shift_ref,
    tile_re, tile_im, edge_re, edge_im, probe_re, probe_im, intensity, tables, spread,
    grad_ref, spill_ref, routed_ref,
    ext, acc, measured, turned, uh, ul, vh, vl, residual, sems, slot_sems,
):
    height = ext.shape[2]
    tiles = ext.shape[1] - 1
    size = probe_re.shape[0]
    half = size // 2
    used = used_ref[0, 0]
    copies = []
    for part, (tile, edge) in enumerate(((tile_re, edge_re), (tile_im, edge_im))):
        for column in range(tiles):
            copies.append(
                pltpu.make_async_copy(
                    tile.at[:, pl.ds(column * LANES, LANES)],
                    ext.at[part, column],
                    sems.at[part * (tiles + 1) + column],
                )
            )
        copies.append(
            pltpu.make_async_copy(edge, ext.at[part, tiles], sems.at[part * (tiles + 1) + tiles])
        )
    for copy in copies:
        copy.start()

    def fetch(slot):
        return [
            pltpu.make_async_copy(
                intensity.at[slot, :, pl.ds(tile * LANES, LANES)],
                measured.at[slot, tile],
                slot_sems.at[slot, tile],
            )
            for tile in range(2)
        ]

    slots = measured.shape[0]
    for slot in range(slots):
        @pl.when(slot < used)
        def _():
            for copy in fetch(slot):
                copy.start()

    @pl.loop(0, height // size)
    def _(chunk):
        rows = pl.ds(chunk * size, size)
        for part in range(2):
            for column in range(tiles + 1):
                acc[part, column, rows, :] = jnp.zeros((size, LANES), jnp.float32)

    for copy in copies:
        copy.wait()

    le, let, lo, lot = 0, 2, 4, 6

    def table(which):
        return tables[which], tables[which + 1]

    @pl.loop(0, used)
    def _(slot):
        row = positions_ref[slot, 0]
        col = positions_ref[slot, 1]
        first = pl.multiple_of(row // SUBLANES * SUBLANES, SUBLANES)
        row_rest = row - first
        wrap = pl.multiple_of(jnp.minimum(first + size, height - SUBLANES), SUBLANES)
        column = col // LANES
        lane_rest = col - column * LANES
        wrap_column = jnp.minimum(column + 2, tiles)
        body = pl.ds(first, size)
        tail = pl.ds(wrap, SUBLANES)
        low_rows = rows_of((SUBLANES, LANES)) < row_rest
        low_lanes = lanes_of((size, LANES)) < lane_rest

        for part, probe in enumerate((probe_re, probe_im)):
            for tile, piece in enumerate(rolled(probe[...], row_rest, lane_rest)):
                turned[part, tile] = piece

        def window(part, at):
            block = ext[part, at, body, :]
            top = jnp.where(low_rows, ext[part, at, tail, :], block[:SUBLANES])
            return jnp.concatenate([top, block[SUBLANES:]], axis=0)

        psi = []
        for tile in range(2):
            if tile == 0:
                o_re, o_im = (
                    jnp.where(low_lanes, window(part, wrap_column), window(part, column))
                    for part in range(2)
                )
            else:
                o_re, o_im = (window(part, column + 1) for part in range(2))
            p_re, p_im = turned[0, tile], turned[1, tile]
            psi.append((p_re * o_re - p_im * o_im, p_re * o_im + p_im * o_re))
        for part in range(2):
            lanes = slice(part * LANES, (part + 1) * LANES)
            uh[:, lanes], ul[:, lanes] = split(psi[0][part] + psi[1][part])
            vh[:, lanes], vl[:, lanes] = split(psi[0][part] - psi[1][part])
        even = dot3(uh[...], ul[...], *table(let))
        odd = dot3(vh[...], vl[...], *table(lot))
        for part in range(2):
            rows = slice(part * half, (part + 1) * half)
            for tile, y in enumerate((even, odd)):
                lanes = slice(tile * LANES, (tile + 1) * LANES)
                y = y[:, part * LANES : (part + 1) * LANES]
                uh[rows, lanes], ul[rows, lanes] = split(y[:half] + y[half:])
                vh[rows, lanes], vl[rows, lanes] = split(y[:half] - y[half:])
        for copy in fetch(slot):
            copy.wait()
        for parity, (h, l, which) in enumerate(((uh, ul, le), (vh, vl, lo))):
            th, tl = table(which)
            far = dot(th, h[...]) + dot(tl, h[...]) + dot(th, l[...])
            f_re, f_im = far[:half], far[half:]
            m = [measured[slot, tile, pl.ds(parity, half, stride=2), :] for tile in range(2)]
            mh, ml = split(jnp.concatenate(m, axis=1))
            excess = f_re * f_re + f_im * f_im - (dot(mh, spread[...]) + dot(ml, spread[...]))
            h[:half, :], l[:half, :] = split(excess * f_re)
            h[half:, :], l[half:, :] = split(excess * f_im)
        th, tl = table(let)
        even = dot(th, uh[...]) + dot(tl, uh[...]) + dot(th, ul[...])
        th, tl = table(lot)
        odd = dot(th, vh[...]) + dot(tl, vh[...]) + dot(th, vl[...])
        for part in range(2):
            rows = slice(part * half, (part + 1) * half)
            lanes = slice(part * LANES, (part + 1) * LANES)
            for sign in range(2):
                out = slice(sign * half, (sign + 1) * half)
                t = even[rows] + odd[rows] if sign == 0 else even[rows] - odd[rows]
                uh[out, lanes], ul[out, lanes] = split(t[:, :LANES])
                vh[out, lanes], vl[out, lanes] = split(t[:, LANES:])
        even = dot3(uh[...], ul[...], *table(le))
        odd = dot3(vh[...], vl[...], *table(lo))
        for tile in range(2):
            chi = even + odd if tile == 0 else even - odd
            c_re, c_im = chi[:, :LANES], chi[:, LANES:]
            p_re, p_im = turned[0, tile], turned[1, tile]
            for part, g in enumerate((p_re * c_re + p_im * c_im, p_re * c_im - p_im * c_re)):
                if tile == 0:
                    places = (
                        (column, jnp.where(low_lanes, 0.0, g)),
                        (wrap_column, jnp.where(low_lanes, g, 0.0)),
                    )
                else:
                    places = ((column + 1, g),)
                for at, value in places:
                    top = value[:SUBLANES]
                    kept = jnp.where(low_rows, 0.0, top)
                    acc[part, at, body, :] += jnp.concatenate([kept, value[SUBLANES:]], axis=0)
                    acc[part, at, tail, :] += jnp.where(low_rows, top, 0.0)

    @pl.loop(0, height // size)
    def _(chunk):
        rows = pl.ds(chunk * size, size)
        for part in range(2):
            for column in range(tiles):
                grad_ref[part, 0, rows, column * LANES : (column + 1) * LANES] = acc[
                    part, column, rows, :
                ]
            spill_ref[part, rows, :] = acc[part, tiles, rows, :]


def probe_phase(used, positions, shift, tile_re, tile_im, edge_re, edge_im, probe_re, probe_im, intensity):
    height, width = tile_re.shape
    size = probe_re.shape[0]
    slots = intensity.shape[0]
    columns = width // LANES
    tables, spread = dft_tables(size)
    plane = pltpu.VMEM((size, size), SPLIT)
    passes = 26 * slots
    return pl.pallas_call(
        probe_kernel,
        out_shape=(
            jax.ShapeDtypeStruct((2, 1, height, width), jnp.float32),
            jax.ShapeDtypeStruct((2, height, LANES), jnp.float32),
            jax.ShapeDtypeStruct((SUBLANES, LANES), jnp.float32),
        ),
        in_specs=[SMEM, SMEM, SMEM, ANY, ANY, ANY, ANY, VMEM, VMEM, ANY, VMEM, VMEM],
        out_specs=(VMEM, VMEM, VMEM),
        scratch_shapes=[
            pltpu.VMEM((2, columns + 1, height, LANES), jnp.float32),
            pltpu.VMEM((2, columns + 1, height, LANES), jnp.float32),
            pltpu.VMEM((slots, 2, size, LANES), jnp.float32),
            pltpu.VMEM((2, 2, size, LANES), jnp.float32),
            plane, plane, plane, plane,
            pltpu.VMEM((SUBLANES, LANES), jnp.float32),
            pltpu.SemaphoreType.DMA((2 * (columns + 1),)),
            pltpu.SemaphoreType.DMA((slots, 2)),
        ],
        compiler_params=pltpu.CompilerParams(vmem_limit_bytes=VMEM_BYTES),
        cost_estimate=pl.CostEstimate(
            flops=passes * 2 * size**3, bytes_accessed=16 * height * width, transcendentals=0
        ),
        name="probes",
    )(used, positions, shift, tile_re, tile_im, edge_re, edge_im, probe_re, probe_im, intensity,
      jnp.asarray(tables), jnp.asarray(spread))


def moved(values, steps, weight, lead, amount, base, count):
    tile = jnp.floor_divide(amount, LANES)
    rest = amount - tile * LANES
    at = pl.ds(base + tile, count + 1)
    x = values[lead, at] + weight * steps[lead, at]
    x = x.reshape((count + 1) * SUBLANES, LANES)
    x = pltpu.roll(x, jnp.where(rest == 0, 0, LANES - rest), axis=1)
    keep = lanes_of((count * SUBLANES, LANES)) < LANES - rest
    return jnp.where(keep, x[: count * SUBLANES], x[SUBLANES:])


def volume_kernel(slope_ref, pieces, volume, fresh, parts, near, slope_near, cells, slope_cells):
    depth = volume.shape[0]
    columns = volume.shape[2]
    count = columns // LANES
    margin = (near.shape[1] - count) // 2
    tilts = near.shape[0]
    per_tile = pieces.shape[2] // LANES
    tiles = pieces.shape[0] // tilts
    last = lanes_of((SUBLANES, LANES)) == LANES - 1
    first = lanes_of((SUBLANES, LANES)) == 0

    def place(ref, lead, tile, value):
        ref[lead, margin + tile] = value
        if tile < margin:
            ref[lead, margin + tile + count] = value
        if tile >= count - margin:
            ref[lead, margin + tile - count] = value

    for tilt in range(tilts):
        row = []
        for tile in range(count):
            lanes = slice(tile % per_tile * LANES, (tile % per_tile + 1) * LANES)
            row.append(pieces[tilt * tiles + tile // per_tile, :, lanes])
        back = [pltpu.roll(x, LANES - 1, axis=1) for x in row]
        for tile in range(count):
            place(near, tilt, tile, row[tile])
            further = jnp.where(last, back[(tile + 1) % count], back[tile])
            place(slope_near, tilt, tile, further - row[tile])

    def weights(tilt, level):
        numer = level * slope_ref[tilt]
        whole = jnp.floor_divide(numer, depth)
        return whole, (numer - whole * depth).astype(jnp.float32) / depth

    @pl.loop(0, depth)
    def _(level):
        total = None
        for tilt in range(tilts):
            whole, frac = weights(tilt, level)
            term = moved(near, slope_near, frac, tilt, whole, margin, count)
            total = term if total is None else total + term
        total = total / tilts
        row = []
        for tile in range(count):
            lanes = slice(tile * LANES, (tile + 1) * LANES)
            value = volume[level, :, lanes] + total[tile * SUBLANES : (tile + 1) * SUBLANES]
            fresh[level, :, lanes] = value
            row.append(value)
        ahead = [pltpu.roll(x, 1, axis=1) for x in row]
        for tile in range(count):
            place(cells, level, tile, row[tile])
            further = jnp.where(first, ahead[tile - 1], ahead[tile])
            place(slope_cells, level, tile, further - row[tile])

    for tilt in range(tilts):
        def add_level(level, total):
            whole, frac = weights(tilt, level)
            return total + moved(cells, slope_cells, frac, level, -whole, margin, count)

        total = lax.fori_loop(
            0, depth, add_level, jnp.zeros((count * SUBLANES, LANES), jnp.float32)
        )
        for tile in range(count):
            lanes = slice(tile % per_tile * LANES, (tile % per_tile + 1) * LANES)
            parts[tilt * tiles + tile // per_tile, :, lanes] = total[
                tile * SUBLANES : (tile + 1) * SUBLANES
            ]


def volume_phase(slope, pieces, volume):
    depth, band, columns = volume.shape
    tilts = slope.shape[0]
    width = pieces.shape[2]
    margin = width // LANES + 1
    count = columns // LANES + 2 * margin
    near = pltpu.VMEM((tilts, count, SUBLANES, LANES), jnp.float32)
    cells = pltpu.VMEM((depth, count, SUBLANES, LANES), jnp.float32)

    def rows(shape):
        return pl.BlockSpec((shape[0], SUBLANES, shape[2]), lambda i: (0, i, 0))

    return pl.pallas_call(
        volume_kernel,
        grid=(band // SUBLANES,),
        out_shape=(
            jax.ShapeDtypeStruct(volume.shape, jnp.float32),
            jax.ShapeDtypeStruct(pieces.shape, jnp.float32),
        ),
        in_specs=[SMEM, rows(pieces.shape), rows(volume.shape)],
        out_specs=(rows(volume.shape), rows(pieces.shape)),
        scratch_shapes=[near, near, cells, cells],
        compiler_params=pltpu.CompilerParams(vmem_limit_bytes=VMEM_BYTES),
        cost_estimate=pl.CostEstimate(
            flops=8 * tilts * volume.size, bytes_accessed=8 * volume.size, transcendentals=0
        ),
        name="volume",
    )(slope, pieces, volume)


def local(
    obj_re, obj_im, probe_re, probe_im, intensity, positions, counts, row_shift, slope, volume
):
    tile_re = obj_re[0]
    tile_im = obj_im[0]
    height, width = tile_re.shape
    margin = LANES
    edge_re = passed_along(tile_re[:, :margin], "tile", -1)
    edge_im = passed_along(tile_im[:, :margin], "tile", -1)
    grad, spill, _ = probe_phase(
        counts, positions[0], row_shift, tile_re, tile_im, edge_re, edge_im,
        probe_re, probe_im, intensity[0],
    )
    spill = passed_along(spill, "tile", 1)
    grad = grad.at[:, 0, :, :margin].add(spill)
    residual = tile_re * grad[1, 0] - tile_im * grad[0, 0]
    routed = jnp.roll(residual, row_shift[0], axis=0)
    axes = ("tilt", "tile")
    devices = lax.axis_size("tilt") * lax.axis_size("tile")
    routed = routed.reshape(devices, height // devices, width)
    pieces = lax.all_to_all(routed, axes, split_axis=0, concat_axis=0, tiled=True)
    fresh, parts = volume_phase(slope, pieces, volume)
    returned = lax.all_to_all(parts, axes, split_axis=0, concat_axis=0, tiled=True)
    reprojection = jnp.roll(returned.reshape(height, width), -row_shift[0], axis=0)[None]
    return (fresh, reprojection, grad)


def solution(mesh):
    placed = (
        P("tilt", None, "tile"),
        P("tilt", None, "tile"),
        P(),
        P(),
        P("tilt", "tile", None, None),
        P("tilt", "tile", None),
        P("tilt", "tile"),
        P("tilt"),
        P(),
        P(None, ("tilt", "tile"), None),
    )
    return jax.shard_map(
        local,
        mesh=mesh,
        in_specs=placed,
        out_specs=(
            P(None, ("tilt", "tile"), None),
            P("tilt", None, "tile"),
            P(None, "tilt", None, "tile"),
        ),
        check_vma=False,
    )
```

```python
import functools
import math

import jax
import jax.numpy as jnp
import ml_dtypes
import numpy as np
from jax import lax
from jax.experimental import pallas as pl
from jax.experimental.pallas import tpu as pltpu
from jax.sharding import PartitionSpec as P

LANES = 128
SUBLANES = 8
VMEM_BYTES = 60 * 1024 * 1024
SPLIT = jnp.bfloat16
ANY = pl.BlockSpec(memory_space=pl.ANY)
HBM = pl.BlockSpec(memory_space=pltpu.HBM)
SMEM = pl.BlockSpec(memory_space=pltpu.SMEM)
VMEM = pl.BlockSpec(memory_space=pltpu.VMEM)


def passed_along(block, axis, distance):
    devices = range(lax.axis_size(axis))
    route = [(i - distance, i) for i in devices if i - distance in devices]
    return lax.ppermute(block, axis, route)


def halves(table):
    high = table.astype(ml_dtypes.bfloat16)
    low = (table - high.astype(np.float64)).astype(ml_dtypes.bfloat16)
    return high, low


def dft_tables(length):
    half = length // 2
    index = np.arange(length)
    angle = (index[:, None] * index[None, :] % length) * (-2.0 * math.pi / length)
    wave = (np.cos(angle) + 1j * np.sin(angle)) / math.sqrt(length)
    tables = []
    for parity in (0, 1):
        part = wave[parity::2, :half]
        pair = np.block([[part.real, -part.imag], [part.imag, part.real]])
        tables += [*halves(pair), *halves(pair.T)]
    order = np.concatenate([index[0::2], index[1::2]])
    spread = np.zeros((length, length))
    spread[order, index] = 1.0
    return np.stack(tables), spread.astype(ml_dtypes.bfloat16)


def split(x):
    high = x.astype(SPLIT)
    return high, (x - high.astype(jnp.float32)).astype(SPLIT)


def dot(a, b):
    return jnp.dot(a, b, preferred_element_type=jnp.float32)


def dot3(ah, al, bh, bl):
    return dot(ah, bh) + dot(ah, bl) + dot(al, bh)


def lanes_of(shape):
    return lax.broadcasted_iota(jnp.int32, shape, len(shape) - 1)


def rows_of(shape):
    return lax.broadcasted_iota(jnp.int32, shape, len(shape) - 2)


def rolled(x, row, lane):
    size = x.shape[0]
    tiles = x.shape[1] // LANES
    cut = []
    for tile in range(tiles):
        part = x[:, tile * LANES : (tile + 1) * LANES].reshape(-1, SUBLANES, LANES)
        turned = pltpu.roll(part, row, axis=1)
        before = jnp.concatenate([turned[-1:], turned[:-1]], axis=0)
        part = jnp.where(rows_of(part.shape) < row, before, turned).reshape(size, LANES)
        cut.append(pltpu.roll(part, lane, axis=1))
    keep = lanes_of(cut[0].shape) >= lane
    return [jnp.where(keep, cut[tile], cut[tile - 1]) for tile in range(tiles)]


def probe_kernel(
    used_ref, positions_ref, shift_ref,
    *refs, base, beyond,
):
    if beyond:
        (tile_re, tile_im, edge_re, edge_im, begun, routed_left, probe_re, probe_im, intensity,
         tables, spread, grad_ref, early_ref, late_ref, routed_ref, *scratch) = refs
    else:
        (tile_re, tile_im, probe_re, probe_im, intensity, tables, spread,
         grad_ref, begun_ref, routed_ref, *scratch) = refs
    ext, acc, measured, turned, uh, ul, vh, vl, residual, routed, sems, slot_sems = scratch
    height = ext.shape[2]
    tiles = ext.shape[1]
    size = probe_re.shape[0]
    half = size // 2
    used = used_ref[0, 0]
    copies, late = [], []
    for part, tile in enumerate((tile_re, tile_im)):
        for column in range(tiles):
            if beyond and column == tiles - 1:
                source = (edge_re, edge_im)[part]
            else:
                source = tile.at[:, pl.ds(base + column * LANES, LANES)]
            sem = sems.at[0, part * tiles + column]
            copies.append(pltpu.make_async_copy(source, ext.at[part, column], sem))
            if beyond and column < tiles - 1:
                sem = sems.at[1, part * tiles + column]
                late.append(pltpu.make_async_copy(begun.at[part, column], acc.at[part, column], sem))
    if beyond:
        late.append(
            pltpu.make_async_copy(routed_left, routed.at[:, pl.ds(0, LANES)], sems.at[1, tiles - 1])
        )
    for copy in copies + late:
        copy.start()

    def fetch(slot):
        return [
            pltpu.make_async_copy(
                intensity.at[slot, :, pl.ds(tile * LANES, LANES)],
                measured.at[slot, tile],
                slot_sems.at[slot, tile],
            )
            for tile in range(2)
        ]

    def mine(slot):
        past = positions_ref[slot, 1] + size > base + tiles * LANES
        return past if not beyond else positions_ref[slot, 1] + size > base + (tiles - 1) * LANES

    def live(slot):
        return mine(slot) if beyond else jnp.logical_not(mine(slot))

    slots = measured.shape[0]
    for slot in range(slots):
        @pl.when(jnp.logical_and(slot < used, live(slot)))
        def _():
            for copy in fetch(slot):
                copy.start()

    first_fresh = tiles - 1 if beyond else 0

    @pl.loop(0, height // size)
    def _(chunk):
        rows = pl.ds(chunk * size, size)
        for part in range(2):
            for column in range(first_fresh, tiles):
                acc[part, column, rows, :] = jnp.zeros((size, LANES), jnp.float32)

    for copy in copies + late:
        copy.wait()

    le, let, lo, lot = 0, 2, 4, 6

    def table(which):
        return tables[which], tables[which + 1]

    def visit(slot):
        row = positions_ref[slot, 0]
        col = positions_ref[slot, 1] - base
        first = pl.multiple_of(row // SUBLANES * SUBLANES, SUBLANES)
        row_rest = row - first
        wrap = pl.multiple_of(jnp.minimum(first + size, height - SUBLANES), SUBLANES)
        column = col // LANES
        lane_rest = col - column * LANES
        wrap_column = jnp.minimum(column + 2, tiles - 1)
        body = pl.ds(first, size)
        tail = pl.ds(wrap, SUBLANES)
        low_rows = rows_of((SUBLANES, LANES)) < row_rest
        low_lanes = lanes_of((size, LANES)) < lane_rest

        for part, probe in enumerate((probe_re, probe_im)):
            for tile, piece in enumerate(rolled(probe[...], row_rest, lane_rest)):
                turned[part, tile] = piece

        def window(part, at):
            block = ext[part, at, body, :]
            top = jnp.where(low_rows, ext[part, at, tail, :], block[:SUBLANES])
            return jnp.concatenate([top, block[SUBLANES:]], axis=0)

        psi = []
        for tile in range(2):
            if tile == 0:
                o_re, o_im = (
                    jnp.where(low_lanes, window(part, wrap_column), window(part, column))
                    for part in range(2)
                )
            else:
                o_re, o_im = (window(part, column + 1) for part in range(2))
            p_re, p_im = turned[0, tile], turned[1, tile]
            psi.append((p_re * o_re - p_im * o_im, p_re * o_im + p_im * o_re))
        for part in range(2):
            lanes = slice(part * LANES, (part + 1) * LANES)
            uh[:, lanes], ul[:, lanes] = split(psi[0][part] + psi[1][part])
            vh[:, lanes], vl[:, lanes] = split(psi[0][part] - psi[1][part])
        even = dot3(uh[...], ul[...], *table(let))
        odd = dot3(vh[...], vl[...], *table(lot))
        for part in range(2):
            rows = slice(part * half, (part + 1) * half)
            for tile, y in enumerate((even, odd)):
                lanes = slice(tile * LANES, (tile + 1) * LANES)
                y = y[:, part * LANES : (part + 1) * LANES]
                uh[rows, lanes], ul[rows, lanes] = split(y[:half] + y[half:])
                vh[rows, lanes], vl[rows, lanes] = split(y[:half] - y[half:])
        for copy in fetch(slot):
            copy.wait()
        for parity, (h, l, which) in enumerate(((uh, ul, le), (vh, vl, lo))):
            th, tl = table(which)
            far = dot(th, h[...]) + dot(tl, h[...]) + dot(th, l[...])
            f_re, f_im = far[:half], far[half:]
            m = [measured[slot, tile, pl.ds(parity, half, stride=2), :] for tile in range(2)]
            mh, ml = split(jnp.concatenate(m, axis=1))
            excess = f_re * f_re + f_im * f_im - (dot(mh, spread[...]) + dot(ml, spread[...]))
            h[:half, :], l[:half, :] = split(excess * f_re)
            h[half:, :], l[half:, :] = split(excess * f_im)
        th, tl = table(let)
        even = dot(th, uh[...]) + dot(tl, uh[...]) + dot(th, ul[...])
        th, tl = table(lot)
        odd = dot(th, vh[...]) + dot(tl, vh[...]) + dot(th, vl[...])
        for part in range(2):
            rows = slice(part * half, (part + 1) * half)
            lanes = slice(part * LANES, (part + 1) * LANES)
            for sign in range(2):
                out = slice(sign * half, (sign + 1) * half)
                t = even[rows] + odd[rows] if sign == 0 else even[rows] - odd[rows]
                uh[out, lanes], ul[out, lanes] = split(t[:, :LANES])
                vh[out, lanes], vl[out, lanes] = split(t[:, LANES:])
        even = dot3(uh[...], ul[...], *table(le))
        odd = dot3(vh[...], vl[...], *table(lo))
        for tile in range(2):
            chi = even + odd if tile == 0 else even - odd
            c_re, c_im = chi[:, :LANES], chi[:, LANES:]
            p_re, p_im = turned[0, tile], turned[1, tile]
            for part, g in enumerate((p_re * c_re + p_im * c_im, p_re * c_im - p_im * c_re)):
                if tile == 0:
                    places = (
                        (column, jnp.where(low_lanes, 0.0, g)),
                        (wrap_column, jnp.where(low_lanes, g, 0.0)),
                    )
                else:
                    places = ((column + 1, g),)
                for at, value in places:
                    top = value[:SUBLANES]
                    kept = jnp.where(low_rows, 0.0, top)
                    acc[part, at, body, :] += jnp.concatenate([kept, value[SUBLANES:]], axis=0)
                    acc[part, at, tail, :] += jnp.where(low_rows, top, 0.0)

    @pl.loop(0, used)
    def _(slot):
        @pl.when(live(slot))
        def _():
            visit(slot)

    outs = []
    if beyond:
        for part in range(2):
            for column in range(tiles - 1):
                target = grad_ref.at[part, :, pl.ds(column * LANES, LANES)]
                outs.append((acc.at[part, column], target))
            rows = early_ref.shape[1]
            outs.append((acc.at[part, tiles - 1, pl.ds(0, rows)], early_ref.at[part]))
            outs.append((acc.at[part, tiles - 1, pl.ds(rows, height - rows)], late_ref.at[part]))
        routing = range(tiles)
    else:
        for part in range(2):
            outs.append((acc.at[part, 0], grad_ref.at[part]))
            for column in range(1, tiles):
                outs.append((acc.at[part, column], begun_ref.at[part, column - 1]))
        routing = range(1)
    outs = [pltpu.make_async_copy(*pair, sems.at[0, n]) for n, pair in enumerate(outs)]
    for copy in outs:
        copy.start()

    @pl.loop(0, height // size)
    def _(chunk):
        rows = pl.ds(chunk * size, size)
        for column in routing:
            value = ext[0, column, rows, :] * acc[1, column, rows, :] - (
                ext[1, column, rows, :] * acc[0, column, rows, :]
            )
            residual[column, rows, :] = value
            residual[column, pl.ds(height + chunk * size, size), :] = value

    shift = shift_ref[0]

    ahead = 1 if beyond else 0
    for chunk in range(height // size):
        rows = pl.ds(chunk * size, size)
        for column in routing:
            lanes = slice((column + ahead) * LANES, (column + ahead + 1) * LANES)
            routed[rows, lanes] = residual[column, pl.ds(height - shift + chunk * size, size), :]
        copy = pltpu.make_async_copy(routed.at[rows], routed_ref.at[rows], slot_sems.at[chunk, 0])
        copy.start()
        outs.append(copy)
    for copy in outs:
        copy.wait()


def probe_phase(used, positions, shift, tile, edge, begun, probe, intensity):
    height, width = tile[0].shape
    size = probe[0].shape[0]
    slots = intensity.shape[0]
    columns = width // LANES
    beyond = edge is not None
    tables, spread = dft_tables(size)
    plane = pltpu.VMEM((size, size), SPLIT)
    planes = pltpu.VMEM((2, columns, height, LANES), jnp.float32)
    routing = columns if beyond else 1

    def out(*shape):
        return jax.ShapeDtypeStruct(shape, jnp.float32)

    if beyond:
        operands = (*tile, *edge, *begun)
        early = height * 5 // 8 // SUBLANES * SUBLANES
        spills = (out(2, early, LANES), out(2, height - early, LANES))
        outs = (out(2, height, width - LANES), *spills, out(height, width + LANES))
        base = LANES
    else:
        operands = tile
        outs = (out(2, height, LANES), out(2, columns - 1, height, LANES), out(height, LANES))
        base = 0
    return pl.pallas_call(
        functools.partial(probe_kernel, base=base, beyond=beyond),
        out_shape=outs,
        in_specs=[SMEM, SMEM, SMEM, *[ANY] * len(operands), VMEM, VMEM, ANY, VMEM, VMEM],
        out_specs=(HBM,) * len(outs),
        scratch_shapes=[
            planes, planes,
            pltpu.VMEM((slots, 2, size, LANES), jnp.float32),
            pltpu.VMEM((2, 2, size, LANES), jnp.float32),
            plane, plane, plane, plane,
            pltpu.VMEM((routing, 2 * height, LANES), jnp.float32),
            pltpu.VMEM((height, outs[-1].shape[1]), jnp.float32),
            pltpu.SemaphoreType.DMA((2, 2 * columns + 2)),
            pltpu.SemaphoreType.DMA((max(slots, height // size), 2)),
        ],
        compiler_params=pltpu.CompilerParams(
            vmem_limit_bytes=VMEM_BYTES * 3 // 4 if beyond else VMEM_BYTES
        ),
        cost_estimate=pl.CostEstimate(
            flops=26 * slots * size**3, bytes_accessed=16 * height * width, transcendentals=0
        ),
        name="probes_beyond" if beyond else "probes_within",
    )(used, positions, shift, *operands, *probe, intensity, jnp.asarray(tables), jnp.asarray(spread))


def shift_tables(slope, depth):
    numer = jnp.arange(depth, dtype=jnp.int32)[None, :] * slope[:, None]
    whole = jnp.floor_divide(numer, depth)
    return whole, (numer - whole * depth).astype(jnp.float32) / depth


class Turned:
    def __init__(self, band, columns, margin):
        self.band = band
        self.segments = LANES // band
        self.length = columns // self.segments
        self.blocks = self.length // LANES
        self.margin = margin
        self.rows = self.length + 2 * margin

    def scratch(self, count):
        return pltpu.VMEM((count, self.rows, LANES), jnp.float32)

    def store(self, ref, lead, at, value):
        rows = value.shape[0]
        ref[lead, pl.ds(self.margin + at, rows), :] = value
        if at < self.margin:
            ref[lead, pl.ds(self.margin + self.length + at, rows), :] = pltpu.roll(
                value, LANES - self.band, axis=1
            )
        if at >= self.length - self.margin:
            ref[lead, pl.ds(at - self.length + self.margin, rows), :] = pltpu.roll(
                value, self.band, axis=1
            )

    def project(self, whole, frac, ref, tilt, at, rows):
        depth = ref.shape[0]

        def add_level(level, total):
            start = self.margin + at - whole[tilt, level]
            far = frac[tilt, level]
            return (
                total
                + (1.0 - far) * ref[level, pl.ds(start, rows), :]
                + far * ref[level, pl.ds(start - 1, rows), :]
            )

        zero = jnp.zeros((rows, LANES), jnp.float32)
        return lax.fori_loop(0, depth, add_level, zero, unroll=4)


def old_kernel(turned, whole, frac, volume, old, cells):
    depth = volume.shape[0]

    @pl.loop(0, depth)
    def _(level):
        for block in range(turned.blocks):
            cut = []
            for segment in range(turned.segments):
                start = segment * turned.length + block * LANES
                cut.append(volume[level, :, start : start + LANES])
            turned.store(cells, level, block * LANES, jnp.concatenate(cut, axis=0).T)

    @pl.loop(0, whole.shape[0])
    def _(tilt):
        for block in range(turned.blocks):
            at = block * LANES
            old[tilt, at : at + LANES, :] = turned.project(whole, frac, cells, tilt, at, LANES)


def step_kernel(
    turned, whole, frac, pieces, old, parts, update, near, cells, before, after, sems
):
    old_copy = pltpu.make_async_copy(old, before, sems.at[0])
    old_copy.start()
    depth = cells.shape[0]
    tilts = near.shape[0]
    tiles = pieces.shape[0] // tilts
    own = pieces.shape[2] // LANES - 1
    band = turned.band

    def place(block, segment):
        return divmod(segment * turned.blocks + block, own)

    @pl.loop(0, tilts)
    def _(tilt):
        for block in range(turned.blocks):
            cut = []
            for segment in range(turned.segments):
                tile, column = place(block, segment)
                source = tilt * tiles + tile
                value = pieces[source, :, column * LANES : (column + 1) * LANES]
                if column == 0 and tile > 0:
                    value = value + pieces[source - 1, :, own * LANES :]
                cut.append(value)
            turned.store(near, tilt, block * LANES, jnp.concatenate(cut, axis=0).T)

    rows = LANES // 2

    @pl.loop(0, depth)
    def _(level):
        for at in range(0, turned.length, rows):
            total = None
            for tilt in range(tilts):
                start = turned.margin + at + whole[tilt, level]
                far = frac[tilt, level] / tilts
                term = (1.0 / tilts - far) * near[tilt, pl.ds(start, rows), :] + (
                    far * near[tilt, pl.ds(start + 1, rows), :]
                )
                total = term if total is None else total + term
            turned.store(cells, level, at, total)

    main = cells.at[:, pl.ds(turned.margin, turned.length), :]
    update_copy = pltpu.make_async_copy(main, update, sems.at[1])
    update_copy.start()
    old_copy.wait()

    def send(tilt):
        block = pl.ds(tilt * tiles, tiles)
        return pltpu.make_async_copy(after.at[block], parts.at[block], sems.at[2 + tilt])

    @pl.loop(0, tilts)
    def _(tilt):
        for block in range(turned.blocks):
            at = block * LANES
            total = turned.project(whole, frac, cells, tilt, at, LANES)
            total = (total + before[tilt, at : at + LANES, :]).T
            for segment in range(turned.segments):
                tile, column = place(block, segment)
                after[tilt * tiles + tile, :, column * LANES : (column + 1) * LANES] = total[
                    segment * band : (segment + 1) * band
                ]

        send(tilt).start()

    for tilt in range(tilts):
        send(tilt).wait()
    update_copy.wait()


def fresh_kernel(turned, volume, update, fresh):
    for block in range(turned.blocks):
        value = update[0, block * LANES : (block + 1) * LANES, :].T
        for segment in range(turned.segments):
            start = segment * turned.length + block * LANES
            lanes = slice(start, start + LANES)
            rows = slice(segment * turned.band, (segment + 1) * turned.band)
            fresh[0, :, lanes] = volume[0, :, lanes] + value[rows]


def kernel_options(flops, size, share=1):
    return dict(
        compiler_params=pltpu.CompilerParams(vmem_limit_bytes=int(VMEM_BYTES * share)),
        cost_estimate=pl.CostEstimate(flops=flops, bytes_accessed=size, transcendentals=0),
    )


def old_projection(turned, whole, frac, volume):
    tilts = whole.shape[0]
    return pl.pallas_call(
        functools.partial(old_kernel, turned),
        out_shape=jax.ShapeDtypeStruct((tilts, turned.length, LANES), jnp.float32),
        in_specs=[SMEM, SMEM, VMEM],
        out_specs=VMEM,
        scratch_shapes=[turned.scratch(volume.shape[0])],
        name="old_projection",
        **kernel_options(8 * tilts * volume.size, 4 * volume.size),
    )(whole, frac, volume)


def volume_step(turned, whole, frac, pieces, old):
    tilts, depth = whole.shape
    width = pieces.shape[2] - LANES
    return pl.pallas_call(
        functools.partial(step_kernel, turned),
        out_shape=(
            jax.ShapeDtypeStruct((*pieces.shape[:2], width), jnp.float32),
            jax.ShapeDtypeStruct((depth, turned.length, LANES), jnp.float32),
        ),
        in_specs=[SMEM, SMEM, VMEM, HBM],
        out_specs=(HBM, HBM),
        scratch_shapes=[
            turned.scratch(tilts), turned.scratch(depth),
            pltpu.VMEM(old.shape, jnp.float32),
            pltpu.VMEM((*pieces.shape[:2], width), jnp.float32),
            pltpu.SemaphoreType.DMA((2 + tilts,)),
        ],
        name="volume_step",
        **kernel_options(16 * depth * old.size, 4 * depth * turned.length * LANES, 9 / 10),
    )(whole, frac, pieces, old)


def fresh_volume(turned, volume, update):
    depth, band, columns = volume.shape
    cells = pl.BlockSpec((1, band, columns), lambda i: (i, 0, 0))
    flat = pl.BlockSpec((1, turned.length, LANES), lambda i: (i, 0, 0))
    return pl.pallas_call(
        functools.partial(fresh_kernel, turned),
        grid=(depth,),
        out_shape=jax.ShapeDtypeStruct(volume.shape, jnp.float32),
        in_specs=[cells, flat],
        out_specs=cells,
        name="fresh_volume",
        **kernel_options(volume.size, 12 * volume.size),
    )(volume, update)


def local(
    obj_re, obj_im, probe_re, probe_im, intensity, positions, counts, row_shift, slope, volume
):
    tile = (obj_re[0], obj_im[0])
    height, width = tile[0].shape
    depth, band, columns = volume.shape
    axes = ("tilt", "tile")
    devices = lax.axis_size("tilt") * lax.axis_size("tile")
    turned = Turned(band, columns, width)
    whole, frac = shift_tables(slope, depth)
    probe = (probe_re, probe_im)

    edge = [passed_along(part[:, :LANES], "tile", -1) for part in tile]
    within = (counts, positions[0], row_shift)
    grad_left, *begun = probe_phase(*within, tile, None, None, probe, intensity[0])
    grad_right, early, late, routed = probe_phase(*within, tile, edge, begun, probe, intensity[0])
    routed = routed.reshape(devices, band, width + LANES)
    pieces = lax.all_to_all(routed, axes, split_axis=0, concat_axis=0, tiled=True)
    old = old_projection(turned, whole, frac, volume)
    pieces, early = lax.optimization_barrier((pieces, early))
    early = passed_along(early, "tile", 1)
    parts, update = volume_step(turned, whole, frac, pieces, old)
    parts, early, late = lax.optimization_barrier((parts, early, late))
    late = passed_along(late, "tile", 1)
    returned = lax.all_to_all(parts, axes, split_axis=0, concat_axis=0, tiled=True)
    fresh = fresh_volume(turned, volume, update)
    spill = jnp.concatenate([early, late], axis=1)
    grad = jnp.concatenate([grad_left + spill, grad_right], axis=2)[:, None]
    reprojection = jnp.roll(returned.reshape(height, width), -row_shift[0], axis=0)[None]
    return (fresh, reprojection, grad)


def solution(mesh):
    placed = (
        P("tilt", None, "tile"),
        P("tilt", None, "tile"),
        P(),
        P(),
        P("tilt", "tile", None, None),
        P("tilt", "tile", None),
        P("tilt", "tile"),
        P("tilt"),
        P(),
        P(None, ("tilt", "tile"), None),
    )
    return jax.shard_map(
        local,
        mesh=mesh,
        in_specs=placed,
        out_specs=(
            P(None, ("tilt", "tile"), None),
            P("tilt", None, "tile"),
            P(None, "tilt", None, "tile"),
        ),
        check_vma=False,
    )
```

```python
import functools
import math

import jax
import jax.numpy as jnp
import ml_dtypes
import numpy as np
from jax import lax
from jax.experimental import pallas as pl
from jax.experimental.pallas import tpu as pltpu
from jax.sharding import PartitionSpec as P

LANES = 128
SUBLANES = 8
VMEM_BYTES = 60 * 1024 * 1024
SPLIT = jnp.bfloat16
ANY = pl.BlockSpec(memory_space=pl.ANY)
HBM = pl.BlockSpec(memory_space=pltpu.HBM)
SMEM = pl.BlockSpec(memory_space=pltpu.SMEM)
VMEM = pl.BlockSpec(memory_space=pltpu.VMEM)


def passed_along(block, axis, distance):
    devices = range(lax.axis_size(axis))
    route = [(i - distance, i) for i in devices if i - distance in devices]
    return lax.ppermute(block, axis, route)


def halves(table):
    high = table.astype(ml_dtypes.bfloat16)
    low = (table - high.astype(np.float64)).astype(ml_dtypes.bfloat16)
    return high, low


def dft_tables(length):
    half = length // 2
    index = np.arange(length)
    angle = (index[:, None] * index[None, :] % length) * (-2.0 * math.pi / length)
    wave = (np.cos(angle) + 1j * np.sin(angle)) / math.sqrt(length)
    tables = []
    for parity in (0, 1):
        part = wave[parity::2, :half]
        pair = np.block([[part.real, -part.imag], [part.imag, part.real]])
        tables += [*halves(pair), *halves(pair.T)]
    order = np.concatenate([index[0::2], index[1::2]])
    spread = np.zeros((length, length))
    spread[order, index] = 1.0
    return np.stack(tables), spread.astype(ml_dtypes.bfloat16)


def split(x):
    high = x.astype(SPLIT)
    return high, (x - high.astype(jnp.float32)).astype(SPLIT)


def dot(a, b):
    return jnp.dot(a, b, preferred_element_type=jnp.float32)


def dot3(ah, al, bh, bl):
    return dot(ah, bh) + dot(ah, bl) + dot(al, bh)


def lanes_of(shape):
    return lax.broadcasted_iota(jnp.int32, shape, len(shape) - 1)


def rows_of(shape):
    return lax.broadcasted_iota(jnp.int32, shape, len(shape) - 2)


def rolled(x, row, lane):
    size = x.shape[0]
    tiles = x.shape[1] // LANES
    cut = []
    for tile in range(tiles):
        part = x[:, tile * LANES : (tile + 1) * LANES].reshape(-1, SUBLANES, LANES)
        turned = pltpu.roll(part, row, axis=1)
        before = jnp.concatenate([turned[-1:], turned[:-1]], axis=0)
        part = jnp.where(rows_of(part.shape) < row, before, turned).reshape(size, LANES)
        cut.append(pltpu.roll(part, lane, axis=1))
    keep = lanes_of(cut[0].shape) >= lane
    return [jnp.where(keep, cut[tile], cut[tile - 1]) for tile in range(tiles)]


def probe_kernel(
    used_ref, positions_ref, shift_ref,
    *refs, base, beyond,
):
    if beyond:
        (tile_re, tile_im, edge, begun, probe_re, probe_im, intensity, tables_from, spread_from,
         grad_ref, early_ref, late_ref, routed_ref, *scratch) = refs
    else:
        (tile_re, tile_im, probe_re, probe_im, intensity, tables_from, spread_from,
         grad_ref, begun_ref, routed_ref, *scratch) = refs
    (ext, acc, measured, probes, tables, spread, turned, uh, ul, vh, vl, residual, routed,
     prior, sems, slot_sems) = scratch
    height = ext.shape[2]
    tiles = ext.shape[1]
    size = probes.shape[1]
    half = size // 2
    used = used_ref[0, 0]
    copies = [
        pltpu.make_async_copy(probe_re, probes.at[0], sems.at[0, 2 * tiles]),
        pltpu.make_async_copy(probe_im, probes.at[1], sems.at[0, 2 * tiles + 1]),
        pltpu.make_async_copy(tables_from, tables, sems.at[1, 0]),
        pltpu.make_async_copy(spread_from, spread, sems.at[1, 1]),
    ]
    for part, tile in enumerate((tile_re, tile_im)):
        for column in range(tiles):
            if beyond and column == tiles - 1:
                source = edge.at[part]
            else:
                source = tile.at[:, pl.ds(base + column * LANES, LANES)]
            sem = sems.at[0, part * tiles + column]
            copies.append(pltpu.make_async_copy(source, ext.at[part, column], sem))
    for copy in copies:
        copy.start()

    def fetch(slot):
        return [
            pltpu.make_async_copy(
                intensity.at[slot, :, pl.ds(tile * LANES, LANES)],
                measured.at[slot, tile],
                slot_sems.at[slot, tile],
            )
            for tile in range(2)
        ]

    def mine(slot):
        past = positions_ref[slot, 1] + size > base + tiles * LANES
        return past if not beyond else positions_ref[slot, 1] + size > base + (tiles - 1) * LANES

    def live(slot):
        return mine(slot) if beyond else jnp.logical_not(mine(slot))

    slots = measured.shape[0]
    for slot in range(slots):
        @pl.when(jnp.logical_and(slot < used, live(slot)))
        def _():
            for copy in fetch(slot):
                copy.start()

    @pl.loop(0, height // size)
    def _(chunk):
        rows = pl.ds(chunk * size, size)
        for part in range(2):
            for column in range(tiles):
                acc[part, column, rows, :] = jnp.zeros((size, LANES), jnp.float32)

    for copy in copies:
        copy.wait()
    if beyond:
        earlier = pltpu.make_async_copy(begun, prior, sems.at[1, 2])
        earlier.start()

    le, let, lo, lot = 0, 2, 4, 6

    def table(which):
        return tables[which], tables[which + 1]

    def visit(slot):
        row = positions_ref[slot, 0]
        col = positions_ref[slot, 1] - base
        first = pl.multiple_of(row // SUBLANES * SUBLANES, SUBLANES)
        row_rest = row - first
        wrap = pl.multiple_of(jnp.minimum(first + size, height - SUBLANES), SUBLANES)
        column = col // LANES
        lane_rest = col - column * LANES
        wrap_column = jnp.minimum(column + 2, tiles - 1)
        body = pl.ds(first, size)
        tail = pl.ds(wrap, SUBLANES)
        low_rows = rows_of((SUBLANES, LANES)) < row_rest
        low_lanes = lanes_of((size, LANES)) < lane_rest

        for part in range(2):
            for tile, piece in enumerate(rolled(probes[part], row_rest, lane_rest)):
                turned[part, tile] = piece

        def window(part, at):
            block = ext[part, at, body, :]
            top = jnp.where(low_rows, ext[part, at, tail, :], block[:SUBLANES])
            return jnp.concatenate([top, block[SUBLANES:]], axis=0)

        psi = []
        for tile in range(2):
            if tile == 0:
                o_re, o_im = (
                    jnp.where(low_lanes, window(part, wrap_column), window(part, column))
                    for part in range(2)
                )
            else:
                o_re, o_im = (window(part, column + 1) for part in range(2))
            p_re, p_im = turned[0, tile], turned[1, tile]
            psi.append((p_re * o_re - p_im * o_im, p_re * o_im + p_im * o_re))
        for part in range(2):
            lanes = slice(part * LANES, (part + 1) * LANES)
            uh[:, lanes], ul[:, lanes] = split(psi[0][part] + psi[1][part])
            vh[:, lanes], vl[:, lanes] = split(psi[0][part] - psi[1][part])
        even = dot3(uh[...], ul[...], *table(let))
        odd = dot3(vh[...], vl[...], *table(lot))
        for part in range(2):
            rows = slice(part * half, (part + 1) * half)
            for tile, y in enumerate((even, odd)):
                lanes = slice(tile * LANES, (tile + 1) * LANES)
                y = y[:, part * LANES : (part + 1) * LANES]
                uh[rows, lanes], ul[rows, lanes] = split(y[:half] + y[half:])
                vh[rows, lanes], vl[rows, lanes] = split(y[:half] - y[half:])
        for copy in fetch(slot):
            copy.wait()
        for parity, (h, l, which) in enumerate(((uh, ul, le), (vh, vl, lo))):
            th, tl = table(which)
            far = dot(th, h[...]) + dot(tl, h[...]) + dot(th, l[...])
            f_re, f_im = far[:half], far[half:]
            m = [measured[slot, tile, pl.ds(parity, half, stride=2), :] for tile in range(2)]
            mh, ml = split(jnp.concatenate(m, axis=1))
            excess = f_re * f_re + f_im * f_im - (dot(mh, spread[...]) + dot(ml, spread[...]))
            h[:half, :], l[:half, :] = split(excess * f_re)
            h[half:, :], l[half:, :] = split(excess * f_im)
        th, tl = table(let)
        even = dot(th, uh[...]) + dot(tl, uh[...]) + dot(th, ul[...])
        th, tl = table(lot)
        odd = dot(th, vh[...]) + dot(tl, vh[...]) + dot(th, vl[...])
        for part in range(2):
            rows = slice(part * half, (part + 1) * half)
            lanes = slice(part * LANES, (part + 1) * LANES)
            for sign in range(2):
                out = slice(sign * half, (sign + 1) * half)
                t = even[rows] + odd[rows] if sign == 0 else even[rows] - odd[rows]
                uh[out, lanes], ul[out, lanes] = split(t[:, :LANES])
                vh[out, lanes], vl[out, lanes] = split(t[:, LANES:])
        even = dot3(uh[...], ul[...], *table(le))
        odd = dot3(vh[...], vl[...], *table(lo))
        for tile in range(2):
            chi = even + odd if tile == 0 else even - odd
            c_re, c_im = chi[:, :LANES], chi[:, LANES:]
            p_re, p_im = turned[0, tile], turned[1, tile]
            for part, g in enumerate((p_re * c_re + p_im * c_im, p_re * c_im - p_im * c_re)):
                if tile == 0:
                    places = (
                        (column, jnp.where(low_lanes, 0.0, g)),
                        (wrap_column, jnp.where(low_lanes, g, 0.0)),
                    )
                else:
                    places = ((column + 1, g),)
                for at, value in places:
                    top = value[:SUBLANES]
                    kept = jnp.where(low_rows, 0.0, top)
                    acc[part, at, body, :] += jnp.concatenate([kept, value[SUBLANES:]], axis=0)
                    acc[part, at, tail, :] += jnp.where(low_rows, top, 0.0)

    @pl.loop(0, used)
    def _(slot):
        @pl.when(live(slot))
        def _():
            visit(slot)

    if beyond:
        earlier.wait()
    routing = tiles if beyond else 1

    @pl.loop(0, height // size)
    def _(chunk):
        rows = pl.ds(chunk * size, size)
        for column in range(routing):
            g_re, g_im = acc[0, column, rows, :], acc[1, column, rows, :]
            if beyond and column < tiles - 1:
                g_re = g_re + prior[0, column, rows, :]
                g_im = g_im + prior[1, column, rows, :]
                acc[0, column, rows, :] = g_re
                acc[1, column, rows, :] = g_im
            value = ext[0, column, rows, :] * g_im - ext[1, column, rows, :] * g_re
            residual[column, rows, :] = value
            residual[column, pl.ds(height + chunk * size, size), :] = value

    shift = shift_ref[0]
    outs = []
    for chunk in range(height // size):
        rows = pl.ds(chunk * size, size)
        for column in range(routing):
            lanes = slice(column * LANES, (column + 1) * LANES)
            routed[rows, lanes] = residual[column, pl.ds(height - shift + chunk * size, size), :]
        outs.append((routed.at[rows], routed_ref.at[rows]))
    for part in range(2):
        if beyond:
            rows = early_ref.shape[1]
            for column in range(tiles - 1):
                target = grad_ref.at[part, :, pl.ds(column * LANES, LANES)]
                outs.append((acc.at[part, column], target))
            outs.append((acc.at[part, tiles - 1, pl.ds(0, rows)], early_ref.at[part]))
            outs.append((acc.at[part, tiles - 1, pl.ds(rows, height - rows)], late_ref.at[part]))
        else:
            outs.append((acc.at[part, 0], grad_ref.at[part]))
            for column in range(1, tiles):
                outs.append((acc.at[part, column], begun_ref.at[part, column - 1]))
    outs = [pltpu.make_async_copy(*pair, sems.at[2, n]) for n, pair in enumerate(outs)]
    for copy in outs:
        copy.start()
    for copy in outs:
        copy.wait()


def margin_kernel(tile_re, tile_im, out, sems):
    copies = [
        pltpu.make_async_copy(tile.at[:, pl.ds(0, LANES)], out.at[part], sems.at[part])
        for part, tile in enumerate((tile_re, tile_im))
    ]
    for copy in copies:
        copy.start()
    for copy in copies:
        copy.wait()


def margins(tile_re, tile_im):
    return pl.pallas_call(
        margin_kernel,
        out_shape=jax.ShapeDtypeStruct((2, tile_re.shape[0], LANES), jnp.float32),
        in_specs=[HBM, HBM],
        out_specs=HBM,
        scratch_shapes=[pltpu.SemaphoreType.DMA((2,))],
        compiler_params=pltpu.CompilerParams(vmem_limit_bytes=VMEM_BYTES),
        name="margins",
    )(tile_re, tile_im)


def probe_phase(used, positions, shift, tile, edge, begun, probe, intensity):
    height, width = tile[0].shape
    size = probe[0].shape[0]
    slots = intensity.shape[0]
    columns = width // LANES
    beyond = edge is not None
    tables, spread = dft_tables(size)
    plane = pltpu.VMEM((size, size), SPLIT)
    planes = pltpu.VMEM((2, columns, height, LANES), jnp.float32)
    routing = columns if beyond else 1

    def out(*shape):
        return jax.ShapeDtypeStruct(shape, jnp.float32)

    if beyond:
        operands = (*tile, edge, begun)
        early = height * 5 // 8 // SUBLANES * SUBLANES
        spills = (out(2, early, LANES), out(2, height - early, LANES))
        outs = (out(2, height, width - LANES), *spills, out(height, width))
        base = LANES
    else:
        operands = tile
        outs = (out(2, height, LANES), out(2, columns - 1, height, LANES), out(height, LANES))
        base = 0
    return pl.pallas_call(
        functools.partial(probe_kernel, base=base, beyond=beyond),
        out_shape=outs,
        in_specs=[SMEM, SMEM, SMEM, *[HBM] * (len(operands) + 5)],
        out_specs=(HBM,) * len(outs),
        scratch_shapes=[
            planes, planes,
            pltpu.VMEM((slots, 2, size, LANES), jnp.float32),
            pltpu.VMEM((2, size, size), jnp.float32),
            pltpu.VMEM(tables.shape, SPLIT),
            plane,
            pltpu.VMEM((2, 2, size, LANES), jnp.float32),
            plane, plane, plane, plane,
            pltpu.VMEM((routing, 2 * height, LANES), jnp.float32),
            pltpu.VMEM((height, outs[-1].shape[1]), jnp.float32),
            pltpu.VMEM((2, columns - 1, height, LANES), jnp.float32),
            pltpu.SemaphoreType.DMA((3, 2 * columns + 2 + height // size)),
            pltpu.SemaphoreType.DMA((slots, 2)),
        ],
        compiler_params=pltpu.CompilerParams(vmem_limit_bytes=VMEM_BYTES),
        cost_estimate=pl.CostEstimate(
            flops=26 * slots * size**3, bytes_accessed=16 * height * width, transcendentals=0
        ),
        name="probes_beyond" if beyond else "probes_within",
    )(used, positions, shift, *operands, *probe, intensity, jnp.asarray(tables), jnp.asarray(spread))


def shift_tables(slope, depth):
    numer = jnp.arange(depth, dtype=jnp.int32)[None, :] * slope[:, None]
    whole = jnp.floor_divide(numer, depth)
    return whole, (numer - whole * depth).astype(jnp.float32) / depth


class Turned:
    def __init__(self, band, columns, margin):
        self.band = band
        self.segments = LANES // band
        self.length = columns // self.segments
        self.blocks = self.length // LANES
        self.margin = margin
        self.rows = self.length + 2 * margin

    def scratch(self, count):
        return pltpu.VMEM((count, self.rows, LANES), jnp.float32)

    def store(self, ref, lead, at, value):
        rows = value.shape[0]
        ref[lead, pl.ds(self.margin + at, rows), :] = value
        if at < self.margin:
            ref[lead, pl.ds(self.margin + self.length + at, rows), :] = pltpu.roll(
                value, LANES - self.band, axis=1
            )
        if at >= self.length - self.margin:
            ref[lead, pl.ds(at - self.length + self.margin, rows), :] = pltpu.roll(
                value, self.band, axis=1
            )

    def project(self, whole, frac, ref, tilt, at, rows):
        depth = ref.shape[0]

        def add_level(level, total):
            start = self.margin + at - whole[tilt, level]
            far = frac[tilt, level]
            return (
                total
                + (1.0 - far) * ref[level, pl.ds(start, rows), :]
                + far * ref[level, pl.ds(start - 1, rows), :]
            )

        zero = jnp.zeros((rows, LANES), jnp.float32)
        return lax.fori_loop(0, depth, add_level, zero, unroll=4)


def old_kernel(turned, whole, frac, volume, old, cells):
    depth = volume.shape[0]

    @pl.loop(0, depth)
    def _(level):
        for block in range(turned.blocks):
            cut = []
            for segment in range(turned.segments):
                start = segment * turned.length + block * LANES
                cut.append(volume[level, :, start : start + LANES])
            turned.store(cells, level, block * LANES, jnp.concatenate(cut, axis=0).T)

    @pl.loop(0, whole.shape[0])
    def _(tilt):
        for block in range(turned.blocks):
            at = block * LANES
            old[tilt, at : at + LANES, :] = turned.project(whole, frac, cells, tilt, at, LANES)


def step_kernel(
    turned, whole, frac, left, right, old, parts, update, near, cells, before, after, sems
):
    old_copy = pltpu.make_async_copy(old, before, sems.at[0])
    old_copy.start()
    depth = cells.shape[0]
    tilts = near.shape[0]
    tiles = right.shape[0] // tilts
    own = right.shape[2] // LANES
    band = turned.band

    def place(block, segment):
        return divmod(segment * turned.blocks + block, own)

    @pl.loop(0, tilts)
    def _(tilt):
        for block in range(turned.blocks):
            cut = []
            for segment in range(turned.segments):
                tile, column = place(block, segment)
                source = tilt * tiles + tile
                if column > 0:
                    value = right[source, :, (column - 1) * LANES : column * LANES]
                elif tile > 0:
                    value = left[source] + right[source - 1, :, (own - 1) * LANES :]
                else:
                    value = left[source]
                cut.append(value)
            turned.store(near, tilt, block * LANES, jnp.concatenate(cut, axis=0).T)

    rows = LANES // 2

    @pl.loop(0, depth)
    def _(level):
        for at in range(0, turned.length, rows):
            total = None
            for tilt in range(tilts):
                start = turned.margin + at + whole[tilt, level]
                far = frac[tilt, level] / tilts
                term = (1.0 / tilts - far) * near[tilt, pl.ds(start, rows), :] + (
                    far * near[tilt, pl.ds(start + 1, rows), :]
                )
                total = term if total is None else total + term
            turned.store(cells, level, at, total)

    main = cells.at[:, pl.ds(turned.margin, turned.length), :]
    update_copy = pltpu.make_async_copy(main, update, sems.at[1])
    update_copy.start()
    old_copy.wait()

    def send(tilt):
        block = pl.ds(tilt * tiles, tiles)
        return pltpu.make_async_copy(after.at[block], parts.at[block], sems.at[2 + tilt])

    @pl.loop(0, tilts)
    def _(tilt):
        for block in range(turned.blocks):
            at = block * LANES
            total = turned.project(whole, frac, cells, tilt, at, LANES)
            total = (total + before[tilt, at : at + LANES, :]).T
            for segment in range(turned.segments):
                tile, column = place(block, segment)
                after[tilt * tiles + tile, :, column * LANES : (column + 1) * LANES] = total[
                    segment * band : (segment + 1) * band
                ]

        send(tilt).start()

    for tilt in range(tilts):
        send(tilt).wait()
    update_copy.wait()


def fresh_kernel(turned, volume, update, fresh):
    for block in range(turned.blocks):
        value = update[0, block * LANES : (block + 1) * LANES, :].T
        for segment in range(turned.segments):
            start = segment * turned.length + block * LANES
            lanes = slice(start, start + LANES)
            rows = slice(segment * turned.band, (segment + 1) * turned.band)
            fresh[0, :, lanes] = volume[0, :, lanes] + value[rows]


def kernel_options(flops, size, share=1):
    return dict(
        compiler_params=pltpu.CompilerParams(vmem_limit_bytes=int(VMEM_BYTES * share)),
        cost_estimate=pl.CostEstimate(flops=flops, bytes_accessed=size, transcendentals=0),
    )


def old_projection(turned, whole, frac, volume):
    tilts = whole.shape[0]
    return pl.pallas_call(
        functools.partial(old_kernel, turned),
        out_shape=jax.ShapeDtypeStruct((tilts, turned.length, LANES), jnp.float32),
        in_specs=[SMEM, SMEM, VMEM],
        out_specs=VMEM,
        scratch_shapes=[turned.scratch(volume.shape[0])],
        name="old_projection",
        **kernel_options(8 * tilts * volume.size, 4 * volume.size),
    )(whole, frac, volume)


def volume_step(turned, whole, frac, left, right, old):
    tilts, depth = whole.shape
    return pl.pallas_call(
        functools.partial(step_kernel, turned),
        out_shape=(
            jax.ShapeDtypeStruct(right.shape, jnp.float32),
            jax.ShapeDtypeStruct((depth, turned.length, LANES), jnp.float32),
        ),
        in_specs=[SMEM, SMEM, VMEM, VMEM, HBM],
        out_specs=(HBM, HBM),
        scratch_shapes=[
            turned.scratch(tilts), turned.scratch(depth),
            pltpu.VMEM(old.shape, jnp.float32),
            pltpu.VMEM(right.shape, jnp.float32),
            pltpu.SemaphoreType.DMA((2 + tilts,)),
        ],
        name="volume_step",
        **kernel_options(16 * depth * old.size, 4 * depth * turned.length * LANES, 9 / 10),
    )(whole, frac, left, right, old)


def fresh_volume(turned, volume, update):
    depth, band, columns = volume.shape
    cells = pl.BlockSpec((1, band, columns), lambda i: (i, 0, 0))
    flat = pl.BlockSpec((1, turned.length, LANES), lambda i: (i, 0, 0))
    return pl.pallas_call(
        functools.partial(fresh_kernel, turned),
        grid=(depth,),
        out_shape=jax.ShapeDtypeStruct(volume.shape, jnp.float32),
        in_specs=[cells, flat],
        out_specs=cells,
        name="fresh_volume",
        **kernel_options(volume.size, 12 * volume.size),
    )(volume, update)


def local(
    obj_re, obj_im, probe_re, probe_im, intensity, positions, counts, row_shift, slope, volume
):
    tile = (obj_re[0], obj_im[0])
    height, width = tile[0].shape
    depth, band, columns = volume.shape
    axes = ("tilt", "tile")
    devices = lax.axis_size("tilt") * lax.axis_size("tile")
    turned = Turned(band, columns, width)
    whole, frac = shift_tables(slope, depth)
    probe = (probe_re, probe_im)

    within = (counts, positions[0], row_shift)

    def exchanged(blocks):
        return lax.all_to_all(blocks, axes, split_axis=0, concat_axis=0, tiled=True)

    edge = passed_along(margins(*tile), "tile", -1)
    grad_left, begun, left = probe_phase(*within, tile, None, None, probe, intensity[0])
    left, edge = lax.optimization_barrier((left, edge))
    left = exchanged(left.reshape(devices, band, LANES))
    grad_right, early, late, right = probe_phase(*within, tile, edge, begun, probe, intensity[0])
    right, whole = lax.optimization_barrier((right, whole))
    right = exchanged(right.reshape(devices, band, width))
    old = old_projection(turned, whole, frac, volume)
    right, early, old = lax.optimization_barrier((right, early, old))
    early = passed_along(early, "tile", 1)
    parts, update = volume_step(turned, whole, frac, left, right, old)
    parts, early, late = lax.optimization_barrier((parts, early, late))
    late = passed_along(late, "tile", 1)
    returned = exchanged(parts)
    fresh = fresh_volume(turned, volume, update)
    spill = jnp.concatenate([early, late], axis=1)
    grad = jnp.concatenate([grad_left + spill, grad_right], axis=2)[:, None]
    reprojection = jnp.roll(returned.reshape(height, width), -row_shift[0], axis=0)[None]
    return (fresh, reprojection, grad)


def solution(mesh):
    placed = (
        P("tilt", None, "tile"),
        P("tilt", None, "tile"),
        P(),
        P(),
        P("tilt", "tile", None, None),
        P("tilt", "tile", None),
        P("tilt", "tile"),
        P("tilt"),
        P(),
        P(None, ("tilt", "tile"), None),
    )
    return jax.shard_map(
        local,
        mesh=mesh,
        in_specs=placed,
        out_specs=(
            P(None, ("tilt", "tile"), None),
            P("tilt", None, "tile"),
            P(None, "tilt", None, "tile"),
        ),
        check_vma=False,
    )
```

```python
import functools
import math

import jax
import jax.numpy as jnp
import ml_dtypes
import numpy as np
from jax import lax
from jax.experimental import pallas as pl
from jax.experimental.pallas import tpu as pltpu
from jax.sharding import PartitionSpec as P

LANES = 128
SUBLANES = 8
VMEM_BYTES = 60 * 1024 * 1024
PROBE_SCRATCH = 15
SPLIT = jnp.bfloat16
ANY = pl.BlockSpec(memory_space=pl.ANY)
HBM = pl.BlockSpec(memory_space=pltpu.HBM)
SMEM = pl.BlockSpec(memory_space=pltpu.SMEM)
VMEM = pl.BlockSpec(memory_space=pltpu.VMEM)


def passed_along(block, axis, distance):
    devices = range(lax.axis_size(axis))
    route = [(i - distance, i) for i in devices if i - distance in devices]
    return lax.ppermute(block, axis, route)


def passed_by(block, axis, first, step):
    count = lax.axis_size(axis)
    route = [(i, i + step) for i in range(first, count, 2) if 0 <= i + step < count]
    return lax.ppermute(block, axis, route)


def halves(table):
    high = table.astype(ml_dtypes.bfloat16)
    low = (table - high.astype(np.float64)).astype(ml_dtypes.bfloat16)
    return high, low


def dft_tables(length):
    half = length // 2
    index = np.arange(length)
    angle = (index[:, None] * index[None, :] % length) * (-2.0 * math.pi / length)
    wave = (np.cos(angle) + 1j * np.sin(angle)) / math.sqrt(length)
    tables = []
    for parity in (0, 1):
        part = wave[parity::2, :half]
        pair = np.block([[part.real, -part.imag], [part.imag, part.real]])
        tables += [*halves(pair), *halves(pair.T)]
    order = np.concatenate([index[0::2], index[1::2]])
    spread = np.zeros((length, length))
    spread[order, index] = 1.0
    return np.stack(tables), spread.astype(ml_dtypes.bfloat16)


def split(x):
    high = x.astype(SPLIT)
    return high, (x - high.astype(jnp.float32)).astype(SPLIT)


def dot(a, b):
    return jnp.dot(a, b, preferred_element_type=jnp.float32)


def dot3(ah, al, bh, bl):
    return dot(ah, bh) + dot(ah, bl) + dot(al, bh)


def lanes_of(shape):
    return lax.broadcasted_iota(jnp.int32, shape, len(shape) - 1)


def rows_of(shape):
    return lax.broadcasted_iota(jnp.int32, shape, len(shape) - 2)


def rolled(x, row, lane):
    size = x.shape[0]
    tiles = x.shape[1] // LANES
    cut = []
    for tile in range(tiles):
        part = x[:, tile * LANES : (tile + 1) * LANES].reshape(-1, SUBLANES, LANES)
        turned = pltpu.roll(part, row, axis=1)
        before = jnp.concatenate([turned[-1:], turned[:-1]], axis=0)
        part = jnp.where(rows_of(part.shape) < row, before, turned).reshape(size, LANES)
        cut.append(pltpu.roll(part, lane, axis=1))
    keep = lanes_of(cut[0].shape) >= lane
    return [jnp.where(keep, cut[tile], cut[tile - 1]) for tile in range(tiles)]


def probe_kernel(
    used_ref, positions_ref, shift_ref,
    *refs, base, beyond,
):
    if beyond:
        (tile_re, tile_im, edge, begun, probe_re, probe_im, intensity, tables_from, spread_from,
         grad_ref, *spill_refs, routed_ref) = refs[: len(refs) - PROBE_SCRATCH]
    else:
        (tile_re, tile_im, probe_re, probe_im, intensity, tables_from, spread_from,
         grad_ref, begun_ref, routed_ref) = refs[: len(refs) - PROBE_SCRATCH]
    (ext, acc, measured, probes, tables, spread, turned, planes, residual, routed,
     prior, listed, sems, slot_sems, out_sems) = refs[len(refs) - PROBE_SCRATCH :]
    height = ext.shape[2]
    tiles = ext.shape[1]
    size = probes.shape[1]
    half = size // 2
    used = used_ref[0, 0]
    copies = [
        pltpu.make_async_copy(probe_re, probes.at[0], sems.at[0, 2 * tiles]),
        pltpu.make_async_copy(probe_im, probes.at[1], sems.at[0, 2 * tiles + 1]),
        pltpu.make_async_copy(tables_from, tables, sems.at[1, 0]),
        pltpu.make_async_copy(spread_from, spread, sems.at[1, 1]),
    ]
    for part, tile in enumerate((tile_re, tile_im)):
        for column in range(tiles):
            if beyond and column == tiles - 1:
                source = edge.at[part]
            else:
                source = tile.at[:, pl.ds(base + column * LANES, LANES)]
            sem = sems.at[0, part * tiles + column]
            copies.append(pltpu.make_async_copy(source, ext.at[part, column], sem))
    for copy in copies:
        copy.start()

    def fetch(slot):
        return [
            pltpu.make_async_copy(
                intensity.at[slot, :, pl.ds(tile * LANES, LANES)],
                measured.at[slot, tile],
                slot_sems.at[slot, tile],
            )
            for tile in range(2)
        ]

    def mine(slot):
        past = positions_ref[slot, 1] + size > base + tiles * LANES
        return past if not beyond else positions_ref[slot, 1] + size > base + (tiles - 1) * LANES

    def live(slot):
        return mine(slot) if beyond else jnp.logical_not(mine(slot))

    slots = measured.shape[0]
    for slot in range(slots):
        @pl.when(jnp.logical_and(slot < used, live(slot)))
        def _():
            for copy in fetch(slot):
                copy.start()

    @pl.loop(0, height // size)
    def _(chunk):
        rows = pl.ds(chunk * size, size)
        for part in range(2):
            for column in range(tiles):
                acc[part, column, rows, :] = jnp.zeros((size, LANES), jnp.float32)

    for copy in copies:
        copy.wait()
    if beyond:
        earlier = pltpu.make_async_copy(begun, prior, sems.at[1, 2])
        earlier.start()

    le, let, lo, lot = 0, 2, 4, 6

    def table(which):
        return tables[which], tables[which + 1]

    def visit(slot, turned, uh, ul, vh, vl):
        row = positions_ref[slot, 0]
        col = positions_ref[slot, 1] - base
        first = pl.multiple_of(row // SUBLANES * SUBLANES, SUBLANES)
        row_rest = row - first
        wrap = pl.multiple_of(jnp.minimum(first + size, height - SUBLANES), SUBLANES)
        column = col // LANES
        lane_rest = col - column * LANES
        wrap_column = jnp.minimum(column + 2, tiles - 1)
        body = pl.ds(first, size)
        tail = pl.ds(wrap, SUBLANES)
        low_rows = rows_of((SUBLANES, LANES)) < row_rest
        low_lanes = lanes_of((size, LANES)) < lane_rest

        for part in range(2):
            for tile, piece in enumerate(rolled(probes[part], row_rest, lane_rest)):
                turned[part, tile] = piece

        def window(part, at):
            block = ext[part, at, body, :]
            top = jnp.where(low_rows, ext[part, at, tail, :], block[:SUBLANES])
            return jnp.concatenate([top, block[SUBLANES:]], axis=0)

        psi = []
        for tile in range(2):
            if tile == 0:
                o_re, o_im = (
                    jnp.where(low_lanes, window(part, wrap_column), window(part, column))
                    for part in range(2)
                )
            else:
                o_re, o_im = (window(part, column + 1) for part in range(2))
            p_re, p_im = turned[0, tile], turned[1, tile]
            psi.append((p_re * o_re - p_im * o_im, p_re * o_im + p_im * o_re))
        for part in range(2):
            lanes = slice(part * LANES, (part + 1) * LANES)
            uh[:, lanes], ul[:, lanes] = split(psi[0][part] + psi[1][part])
            vh[:, lanes], vl[:, lanes] = split(psi[0][part] - psi[1][part])
        yield
        even = dot3(uh[...], ul[...], *table(let))
        odd = dot3(vh[...], vl[...], *table(lot))
        for part in range(2):
            rows = slice(part * half, (part + 1) * half)
            for tile, y in enumerate((even, odd)):
                lanes = slice(tile * LANES, (tile + 1) * LANES)
                y = y[:, part * LANES : (part + 1) * LANES]
                uh[rows, lanes], ul[rows, lanes] = split(y[:half] + y[half:])
                vh[rows, lanes], vl[rows, lanes] = split(y[:half] - y[half:])
        yield
        for copy in fetch(slot):
            copy.wait()
        for parity, (h, l, which) in enumerate(((uh, ul, le), (vh, vl, lo))):
            th, tl = table(which)
            far = dot(th, h[...]) + dot(tl, h[...]) + dot(th, l[...])
            f_re, f_im = far[:half], far[half:]
            m = [measured[slot, tile, pl.ds(parity, half, stride=2), :] for tile in range(2)]
            mh, ml = split(jnp.concatenate(m, axis=1))
            excess = f_re * f_re + f_im * f_im - (dot(mh, spread[...]) + dot(ml, spread[...]))
            h[:half, :], l[:half, :] = split(excess * f_re)
            h[half:, :], l[half:, :] = split(excess * f_im)
        yield
        th, tl = table(let)
        even = dot(th, uh[...]) + dot(tl, uh[...]) + dot(th, ul[...])
        th, tl = table(lot)
        odd = dot(th, vh[...]) + dot(tl, vh[...]) + dot(th, vl[...])
        for part in range(2):
            rows = slice(part * half, (part + 1) * half)
            lanes = slice(part * LANES, (part + 1) * LANES)
            for sign in range(2):
                out = slice(sign * half, (sign + 1) * half)
                t = even[rows] + odd[rows] if sign == 0 else even[rows] - odd[rows]
                uh[out, lanes], ul[out, lanes] = split(t[:, :LANES])
                vh[out, lanes], vl[out, lanes] = split(t[:, LANES:])
        yield
        even = dot3(uh[...], ul[...], *table(le))
        odd = dot3(vh[...], vl[...], *table(lo))
        for tile in range(2):
            chi = even + odd if tile == 0 else even - odd
            c_re, c_im = chi[:, :LANES], chi[:, LANES:]
            p_re, p_im = turned[0, tile], turned[1, tile]
            for part, g in enumerate((p_re * c_re + p_im * c_im, p_re * c_im - p_im * c_re)):
                if tile == 0:
                    places = (
                        (column, jnp.where(low_lanes, 0.0, g)),
                        (wrap_column, jnp.where(low_lanes, g, 0.0)),
                    )
                else:
                    places = ((column + 1, g),)
                for at, value in places:
                    top = value[:SUBLANES]
                    kept = jnp.where(low_rows, 0.0, top)
                    acc[part, at, body, :] += jnp.concatenate([kept, value[SUBLANES:]], axis=0)
                    acc[part, at, tail, :] += jnp.where(low_rows, top, 0.0)
        yield

    def buffers(which):
        return (turned.at[which], *(planes.at[which, n] for n in range(4)))

    def together(*slots):
        for _ in zip(*(visit(slot, *buffers(which)) for which, slot in enumerate(slots))):
            pass

    def enlist(slot, count):
        @pl.when(live(slot))
        def _():
            listed[count] = slot

        return count + live(slot).astype(jnp.int32)

    count = lax.fori_loop(0, used, enlist, 0)

    @pl.loop(0, count // 2)
    def _(pair):
        together(listed[2 * pair], listed[2 * pair + 1])

    @pl.when(count % 2 == 1)
    def _():
        together(listed[count - 1])

    sent = []

    def send(source, target):
        sent.append(pltpu.make_async_copy(source, target, out_sems.at[len(sent)]))
        sent[-1].start()

    last = tiles - 1
    for part in range(2):
        if beyond:
            first_row = 0
            for spill_ref in spill_refs:
                rows = pl.ds(first_row, spill_ref.shape[1])
                send(acc.at[part, last, rows], spill_ref.at[part])
                first_row += spill_ref.shape[1]
        else:
            send(acc.at[part, 0], grad_ref.at[part])
            for column in range(1, tiles):
                send(acc.at[part, column], begun_ref.at[part, column - 1])
    if beyond:
        earlier.wait()
    routing = tiles if beyond else 1

    for chunk in range(height // size):
        rows = pl.ds(chunk * size, size)
        for column in range(routing):
            g_re, g_im = acc[0, column, rows, :], acc[1, column, rows, :]
            if beyond and column < last:
                g_re = g_re + prior[0, column, rows, :]
                g_im = g_im + prior[1, column, rows, :]
                lanes = pl.ds(column * LANES, LANES)
                for part, g in enumerate((g_re, g_im)):
                    acc[part, column, rows, :] = g
                    send(acc.at[part, column, rows], grad_ref.at[part, rows, lanes])
            value = ext[0, column, rows, :] * g_im - ext[1, column, rows, :] * g_re
            residual[column, rows, :] = value
            residual[column, pl.ds(height + chunk * size, size), :] = value

    shift = shift_ref[0]
    for chunk in range(height // size):
        rows = pl.ds(chunk * size, size)
        for column in range(routing):
            lanes = slice(column * LANES, (column + 1) * LANES)
            routed[rows, lanes] = residual[column, pl.ds(height - shift + chunk * size, size), :]
        send(routed.at[rows], routed_ref.at[rows])
    for copy in sent:
        copy.wait()


def margin_kernel(tile_re, tile_im, out, sems):
    copies = [
        pltpu.make_async_copy(tile.at[:, pl.ds(0, LANES)], out.at[part], sems.at[part])
        for part, tile in enumerate((tile_re, tile_im))
    ]
    for copy in copies:
        copy.start()
    for copy in copies:
        copy.wait()


def margins(tile_re, tile_im):
    shape = (2, tile_re.shape[0], LANES)
    return pl.pallas_call(
        margin_kernel,
        out_shape=jax.ShapeDtypeStruct(shape, jnp.float32),
        in_specs=[HBM, HBM],
        out_specs=VMEM,
        scratch_shapes=[pltpu.SemaphoreType.DMA((2,))],
        compiler_params=pltpu.CompilerParams(vmem_limit_bytes=VMEM_BYTES // 4),
        name="margins",
    )(tile_re, tile_im)


def probe_phase(used, positions, shift, tile, edge, begun, probe, intensity):
    height, width = tile[0].shape
    size = probe[0].shape[0]
    slots = intensity.shape[0]
    columns = width // LANES
    beyond = edge is not None
    tables, spread = dft_tables(size)
    plane = pltpu.VMEM((size, size), SPLIT)
    planes = pltpu.VMEM((2, columns, height, LANES), jnp.float32)
    routing = columns if beyond else 1

    def out(*shape):
        return jax.ShapeDtypeStruct(shape, jnp.float32)

    if beyond:
        operands = (*tile, edge, begun)
        early = height * 9 // 16 // SUBLANES * SUBLANES
        late = (height - early) // 2 // SUBLANES * SUBLANES
        spills = [out(2, rows, LANES) for rows in (early, late, height - early - late)]
        outs = (out(2, height, width - LANES), *spills, out(height, width))
        base = LANES
    else:
        operands = tile
        outs = (out(2, height, LANES), out(2, columns - 1, height, LANES), out(height, LANES))
        base = 0
    return pl.pallas_call(
        functools.partial(probe_kernel, base=base, beyond=beyond),
        out_shape=outs,
        in_specs=[SMEM, SMEM, SMEM, *[HBM if x is not edge else ANY for x in operands], *[HBM] * 5],
        out_specs=(HBM,) * len(outs),
        scratch_shapes=[
            planes, planes,
            pltpu.VMEM((slots, 2, size, LANES), jnp.float32),
            pltpu.VMEM((2, size, size), jnp.float32),
            pltpu.VMEM(tables.shape, SPLIT),
            plane,
            pltpu.VMEM((2, 2, 2, size, LANES), jnp.float32),
            pltpu.VMEM((2, 4, size, size), SPLIT),
            pltpu.VMEM((routing, 2 * height, LANES), jnp.float32),
            pltpu.VMEM((height, outs[-1].shape[1]), jnp.float32),
            pltpu.VMEM((2, columns - 1, height, LANES), jnp.float32),
            pltpu.SMEM((slots,), jnp.int32),
            pltpu.SemaphoreType.DMA((2, 2 * columns + 2)),
            pltpu.SemaphoreType.DMA((slots, 2)),
            pltpu.SemaphoreType.DMA((3 * columns + (2 * columns + 1) * (height // size),)),
        ],
        compiler_params=pltpu.CompilerParams(vmem_limit_bytes=VMEM_BYTES),
        cost_estimate=pl.CostEstimate(
            flops=26 * slots * size**3, bytes_accessed=16 * height * width, transcendentals=0
        ),
        name="probes_beyond" if beyond else "probes_within",
    )(used, positions, shift, *operands, *probe, intensity, jnp.asarray(tables), jnp.asarray(spread))


def shift_tables(slope, depth):
    numer = jnp.arange(depth, dtype=jnp.int32)[None, :] * slope[:, None]
    whole = jnp.floor_divide(numer, depth)
    return whole, (numer - whole * depth).astype(jnp.float32) / depth


class Turned:
    def __init__(self, band, columns, margin):
        self.band = band
        self.segments = LANES // band
        self.length = columns // self.segments
        self.blocks = self.length // LANES
        self.margin = margin
        self.rows = self.length + 2 * margin

    def scratch(self, count):
        return pltpu.VMEM((count, self.rows, LANES), jnp.float32)

    def store(self, ref, lead, at, value):
        rows = value.shape[0]
        ref[lead, pl.ds(self.margin + at, rows), :] = value
        if at < self.margin:
            ref[lead, pl.ds(self.margin + self.length + at, rows), :] = pltpu.roll(
                value, LANES - self.band, axis=1
            )
        if at >= self.length - self.margin:
            ref[lead, pl.ds(at - self.length + self.margin, rows), :] = pltpu.roll(
                value, self.band, axis=1
            )

    def project(self, whole, frac, ref, tilt, at, rows):
        depth = ref.shape[0]

        def add_level(level, totals):
            plain, weighted = totals
            start = self.margin + at - whole[tilt, level] - SUBLANES
            x = ref[level, pl.ds(start, rows + SUBLANES), :]
            return plain + x[SUBLANES:], weighted + frac[tilt, level] * x

        zero = jnp.zeros((rows + SUBLANES, LANES), jnp.float32)
        plain, weighted = lax.fori_loop(
            0, depth, add_level, (zero[SUBLANES:], zero), unroll=8
        )
        return plain - weighted[SUBLANES:] + weighted[SUBLANES - 1 : SUBLANES - 1 + rows]


def old_kernel(turned, whole, frac, volume, old, cells):
    depth = volume.shape[0]

    @pl.loop(0, depth)
    def _(level):
        for block in range(turned.blocks):
            cut = []
            for segment in range(turned.segments):
                start = segment * turned.length + block * LANES
                cut.append(volume[level, :, start : start + LANES])
            turned.store(cells, level, block * LANES, jnp.concatenate(cut, axis=0).T)

    @pl.loop(0, whole.shape[0])
    def _(tilt):
        for block in range(turned.blocks):
            at = block * LANES
            old[tilt, at : at + LANES, :] = turned.project(whole, frac, cells, tilt, at, LANES)


def step_kernel(
    turned, whole, frac, left_from, right_from, old, parts, update,
    near, cells, left, right, before, after, sems, level_sems,
):
    old_copy = pltpu.make_async_copy(old, before, sems.at[0, 0])
    depth = cells.shape[0]
    tilts = near.shape[0]
    tiles = right_from.shape[0] // tilts
    own = right_from.shape[2] // LANES
    band = turned.band

    def fetch(tilt):
        block = pl.ds(tilt * tiles, tiles)
        return [
            pltpu.make_async_copy(source.at[block], target.at[block], sems.at[2 + n, tilt])
            for n, (source, target) in enumerate(((left_from, left), (right_from, right)))
        ]

    for tilt in range(tilts):
        for copy in fetch(tilt):
            copy.start()
    old_copy.start()

    def place(block, segment):
        return divmod(segment * turned.blocks + block, own)

    @pl.loop(0, tilts)
    def _(tilt):
        for copy in fetch(tilt):
            copy.wait()
        for block in range(turned.blocks):
            cut = []
            for segment in range(turned.segments):
                tile, column = place(block, segment)
                source = tilt * tiles + tile
                if column > 0:
                    value = right[source, :, (column - 1) * LANES : column * LANES]
                elif tile > 0:
                    value = left[source] + right[source - 1, :, (own - 1) * LANES :]
                else:
                    value = left[source]
                cut.append(value)
            value = jnp.concatenate(cut, axis=0).T * (1.0 / tilts)
            turned.store(near, tilt, block * LANES, value)

    rows = LANES // 2

    def keep(level):
        main = cells.at[level, pl.ds(turned.margin, turned.length), :]
        return pltpu.make_async_copy(main, update.at[level], level_sems.at[level])

    @pl.loop(0, depth)
    def _(level):
        for at in range(0, turned.length, rows):
            plain = weighted = None
            for tilt in range(tilts):
                start = turned.margin + at + whole[tilt, level]
                x = near[tilt, pl.ds(start, rows + SUBLANES), :]
                y = frac[tilt, level] * x
                plain = x[:rows] if plain is None else plain + x[:rows]
                weighted = y if weighted is None else weighted + y
            value = plain - weighted[:rows] + weighted[1 : 1 + rows]
            turned.store(cells, level, at, value)
        keep(level).start()

    old_copy.wait()

    def send(tilt):
        block = pl.ds(tilt * tiles, tiles)
        return pltpu.make_async_copy(after.at[block], parts.at[block], sems.at[1, tilt])

    @pl.loop(0, tilts)
    def _(tilt):
        for block in range(turned.blocks):
            at = block * LANES
            before[tilt, at : at + LANES, :] += turned.project(whole, frac, cells, tilt, at, LANES)
        for block in range(turned.blocks):
            total = before[tilt, block * LANES : (block + 1) * LANES, :].T
            for segment in range(turned.segments):
                tile, column = place(block, segment)
                after[tilt * tiles + tile, :, column * LANES : (column + 1) * LANES] = total[
                    segment * band : (segment + 1) * band
                ]

        send(tilt).start()

    for tilt in range(tilts):
        send(tilt).wait()
    for level in range(depth):
        keep(level).wait()


def fresh_kernel(turned, volume, update, fresh):
    for level in range(volume.shape[0]):
        for block in range(turned.blocks):
            value = update[level, block * LANES : (block + 1) * LANES, :].T
            for segment in range(turned.segments):
                start = segment * turned.length + block * LANES
                lanes = slice(start, start + LANES)
                rows = slice(segment * turned.band, (segment + 1) * turned.band)
                fresh[level, :, lanes] = volume[level, :, lanes] + value[rows]


def kernel_options(flops, size, share=1):
    return dict(
        compiler_params=pltpu.CompilerParams(vmem_limit_bytes=int(VMEM_BYTES * share)),
        cost_estimate=pl.CostEstimate(flops=flops, bytes_accessed=size, transcendentals=0),
    )


def old_projection(turned, whole, frac, volume):
    tilts = whole.shape[0]
    return pl.pallas_call(
        functools.partial(old_kernel, turned),
        out_shape=jax.ShapeDtypeStruct((tilts, turned.length, LANES), jnp.float32),
        in_specs=[SMEM, SMEM, VMEM],
        out_specs=VMEM,
        scratch_shapes=[turned.scratch(volume.shape[0])],
        name="old_projection",
        **kernel_options(8 * tilts * volume.size, 4 * volume.size),
    )(whole, frac, volume)


def volume_step(turned, whole, frac, left, right, old):
    tilts, depth = whole.shape
    return pl.pallas_call(
        functools.partial(step_kernel, turned),
        out_shape=(
            jax.ShapeDtypeStruct(right.shape, jnp.float32),
            jax.ShapeDtypeStruct((depth, turned.length, LANES), jnp.float32),
        ),
        in_specs=[SMEM, SMEM, ANY, ANY, HBM],
        out_specs=(HBM, HBM),
        scratch_shapes=[
            turned.scratch(tilts), turned.scratch(depth),
            pltpu.VMEM(left.shape, jnp.float32),
            pltpu.VMEM(right.shape, jnp.float32),
            pltpu.VMEM(old.shape, jnp.float32),
            pltpu.VMEM(right.shape, jnp.float32),
            pltpu.SemaphoreType.DMA((4, tilts)),
            pltpu.SemaphoreType.DMA((depth,)),
        ],
        name="volume_step",
        **kernel_options(16 * depth * old.size, 4 * depth * turned.length * LANES, 9 / 10),
    )(whole, frac, left, right, old)


def fresh_volume(turned, volume, update):
    depth, band, columns = volume.shape
    levels = math.gcd(depth, 4)
    cells = pl.BlockSpec((levels, band, columns), lambda i: (i, 0, 0))
    flat = pl.BlockSpec((levels, turned.length, LANES), lambda i: (i, 0, 0))
    return pl.pallas_call(
        functools.partial(fresh_kernel, turned),
        grid=(depth // levels,),
        out_shape=jax.ShapeDtypeStruct(volume.shape, jnp.float32),
        in_specs=[cells, flat],
        out_specs=cells,
        name="fresh_volume",
        **kernel_options(volume.size, 12 * volume.size),
    )(volume, update)


def local(
    obj_re, obj_im, probe_re, probe_im, intensity, positions, counts, row_shift, slope, volume
):
    tile = (obj_re[0], obj_im[0])
    height, width = tile[0].shape
    depth, band, columns = volume.shape
    axes = ("tilt", "tile")
    devices = lax.axis_size("tilt") * lax.axis_size("tile")
    turned = Turned(band, columns, width)
    whole, frac = shift_tables(slope, depth)
    probe = (probe_re, probe_im)

    within = (counts, positions[0], row_shift)

    def exchanged(blocks):
        return lax.all_to_all(blocks, axes, split_axis=0, concat_axis=0, tiled=True)

    edge = passed_along(margins(*tile), "tile", -1)
    grad_left, begun, left = probe_phase(*within, tile, None, None, probe, intensity[0])
    left, whole, frac = lax.optimization_barrier((left, whole, frac))
    left = exchanged(left.reshape(devices, band, LANES))
    grad_right, early, late, relayed, right = probe_phase(*within, tile, edge, begun, probe, intensity[0])
    right, left, whole = lax.optimization_barrier((right, left, whole))
    right = exchanged(right.reshape(devices, band, width))
    old = old_projection(turned, whole, frac, volume)
    right, early, old = lax.optimization_barrier((right, early, old))
    early = passed_along(early, "tile", 1)
    parts, update = volume_step(turned, whole, frac, left, right, old)
    parts, early, late, relayed = lax.optimization_barrier((parts, early, late, relayed))
    late = passed_along(late, "tile", 1)
    straight = passed_by(relayed, "tile", 0, 1)
    relayed = passed_by(relayed, "tile", 1, -1)
    returned = exchanged(parts)
    fresh = fresh_volume(turned, volume, update)
    relayed, fresh = lax.optimization_barrier((relayed, fresh))
    relayed = straight + passed_by(relayed, "tile", 0, 2)
    spill = jnp.concatenate([early, late, relayed], axis=1)
    grad = jnp.concatenate([grad_left + spill, grad_right], axis=2)[:, None]
    reprojection = jnp.roll(returned.reshape(height, width), -row_shift[0], axis=0)[None]
    return (fresh, reprojection, grad)


def solution(mesh):
    placed = (
        P("tilt", None, "tile"),
        P("tilt", None, "tile"),
        P(),
        P(),
        P("tilt", "tile", None, None),
        P("tilt", "tile", None),
        P("tilt", "tile"),
        P("tilt"),
        P(),
        P(None, ("tilt", "tile"), None),
    )
    return jax.shard_map(
        local,
        mesh=mesh,
        in_specs=placed,
        out_specs=(
            P(None, ("tilt", "tile"), None),
            P("tilt", None, "tile"),
            P(None, "tilt", None, "tile"),
        ),
        check_vma=False,
    )
```

```python
import functools
import math

import jax
import jax.numpy as jnp
import ml_dtypes
import numpy as np
from jax import lax
from jax.experimental import pallas as pl
from jax.experimental.pallas import tpu as pltpu
from jax.sharding import PartitionSpec as P

LANES = 128
SUBLANES = 8
VMEM_BYTES = 60 * 1024 * 1024
PROBE_SCRATCH = 15
SPLIT = jnp.bfloat16
ANY = pl.BlockSpec(memory_space=pl.ANY)
HBM = pl.BlockSpec(memory_space=pltpu.HBM)
SMEM = pl.BlockSpec(memory_space=pltpu.SMEM)
VMEM = pl.BlockSpec(memory_space=pltpu.VMEM)


def passed_along(block, axis, distance):
    devices = range(lax.axis_size(axis))
    route = [(i - distance, i) for i in devices if i - distance in devices]
    return lax.ppermute(block, axis, route)


def passed_by(block, axis, first, step):
    count = lax.axis_size(axis)
    route = [(i, i + step) for i in range(first, count, 2) if 0 <= i + step < count]
    return lax.ppermute(block, axis, route)


def halves(table):
    high = table.astype(ml_dtypes.bfloat16)
    low = (table - high.astype(np.float64)).astype(ml_dtypes.bfloat16)
    return high, low


def dft_tables(length):
    half = length // 2
    index = np.arange(length)
    angle = (index[:, None] * index[None, :] % length) * (-2.0 * math.pi / length)
    wave = (np.cos(angle) + 1j * np.sin(angle)) / math.sqrt(length)
    tables = []
    for parity in (0, 1):
        part = wave[parity::2, :half]
        pair = np.block([[part.real, -part.imag], [part.imag, part.real]])
        tables += [*halves(pair), *halves(pair.T)]
    order = np.concatenate([index[0::2], index[1::2]])
    spread = np.zeros((length, length))
    spread[order, index] = 1.0
    return np.stack(tables), spread.astype(ml_dtypes.bfloat16)


def split(x):
    high = x.astype(SPLIT)
    return high, (x - high.astype(jnp.float32)).astype(SPLIT)


def dot(a, b):
    return jnp.dot(a, b, preferred_element_type=jnp.float32)


def dot3(ah, al, bh, bl):
    return dot(ah, bh) + dot(ah, bl) + dot(al, bh)


def lanes_of(shape):
    return lax.broadcasted_iota(jnp.int32, shape, len(shape) - 1)


def rows_of(shape):
    return lax.broadcasted_iota(jnp.int32, shape, len(shape) - 2)


def rolled(x, row, lane):
    size = x.shape[0]
    tiles = x.shape[1] // LANES
    cut = []
    for tile in range(tiles):
        part = x[:, tile * LANES : (tile + 1) * LANES].reshape(-1, SUBLANES, LANES)
        turned = pltpu.roll(part, row, axis=1)
        before = jnp.concatenate([turned[-1:], turned[:-1]], axis=0)
        part = jnp.where(rows_of(part.shape) < row, before, turned).reshape(size, LANES)
        cut.append(pltpu.roll(part, lane, axis=1))
    keep = lanes_of(cut[0].shape) >= lane
    return [jnp.where(keep, cut[tile], cut[tile - 1]) for tile in range(tiles)]


def probe_kernel(
    used_ref, positions_ref, shift_ref,
    *refs, base, beyond,
):
    if beyond:
        (tile_re, tile_im, edge, begun, probe_re, probe_im, intensity, tables_from, spread_from,
         grad_ref, *spill_refs, routed_ref) = refs[: len(refs) - PROBE_SCRATCH]
    else:
        (tile_re, tile_im, probe_re, probe_im, intensity, tables_from, spread_from,
         grad_ref, begun_ref, routed_ref) = refs[: len(refs) - PROBE_SCRATCH]
    (ext, acc, measured, probes, tables, spread, turned, planes, residual, routed,
     prior, listed, sems, slot_sems, out_sems) = refs[len(refs) - PROBE_SCRATCH :]
    height = ext.shape[2]
    tiles = ext.shape[1]
    size = probes.shape[1]
    half = size // 2
    used = used_ref[0, 0]
    copies = [
        pltpu.make_async_copy(probe_re, probes.at[0], sems.at[0, 2 * tiles]),
        pltpu.make_async_copy(probe_im, probes.at[1], sems.at[0, 2 * tiles + 1]),
        pltpu.make_async_copy(tables_from, tables, sems.at[1, 0]),
        pltpu.make_async_copy(spread_from, spread, sems.at[1, 1]),
    ]
    for part, tile in enumerate((tile_re, tile_im)):
        for column in range(tiles):
            if beyond and column == tiles - 1:
                source = edge.at[part]
            else:
                source = tile.at[:, pl.ds(base + column * LANES, LANES)]
            sem = sems.at[0, part * tiles + column]
            copies.append(pltpu.make_async_copy(source, ext.at[part, column], sem))
    for copy in copies:
        copy.start()

    def fetch(slot):
        return [
            pltpu.make_async_copy(
                intensity.at[slot, :, pl.ds(tile * LANES, LANES)],
                measured.at[slot, tile],
                slot_sems.at[slot, tile],
            )
            for tile in range(2)
        ]

    def mine(slot):
        past = positions_ref[slot, 1] + size > base + tiles * LANES
        return past if not beyond else positions_ref[slot, 1] + size > base + (tiles - 1) * LANES

    def live(slot):
        return mine(slot) if beyond else jnp.logical_not(mine(slot))

    slots = measured.shape[0]
    for slot in range(slots):
        @pl.when(jnp.logical_and(slot < used, live(slot)))
        def _():
            for copy in fetch(slot):
                copy.start()

    @pl.loop(0, height // size)
    def _(chunk):
        rows = pl.ds(chunk * size, size)
        for part in range(2):
            for column in range(tiles):
                acc[part, column, rows, :] = jnp.zeros((size, LANES), jnp.float32)

    for copy in copies:
        copy.wait()
    if beyond:
        earlier = pltpu.make_async_copy(begun, prior, sems.at[1, 2])
        earlier.start()

    le, let, lo, lot = 0, 2, 4, 6

    def table(which):
        return tables[which], tables[which + 1]

    def visit(slot, turned, uh, ul, vh, vl):
        row = positions_ref[slot, 0]
        col = positions_ref[slot, 1] - base
        first = pl.multiple_of(row // SUBLANES * SUBLANES, SUBLANES)
        row_rest = row - first
        wrap = pl.multiple_of(jnp.minimum(first + size, height - SUBLANES), SUBLANES)
        column = col // LANES
        lane_rest = col - column * LANES
        wrap_column = jnp.minimum(column + 2, tiles - 1)
        body = pl.ds(first, size)
        tail = pl.ds(wrap, SUBLANES)
        low_rows = rows_of((SUBLANES, LANES)) < row_rest
        low_lanes = lanes_of((size, LANES)) < lane_rest

        for part in range(2):
            for tile, piece in enumerate(rolled(probes[part], row_rest, lane_rest)):
                turned[part, tile] = piece

        def window(part, at):
            block = ext[part, at, body, :]
            top = jnp.where(low_rows, ext[part, at, tail, :], block[:SUBLANES])
            return jnp.concatenate([top, block[SUBLANES:]], axis=0)

        psi = []
        for tile in range(2):
            if tile == 0:
                o_re, o_im = (
                    jnp.where(low_lanes, window(part, wrap_column), window(part, column))
                    for part in range(2)
                )
            else:
                o_re, o_im = (window(part, column + 1) for part in range(2))
            p_re, p_im = turned[0, tile], turned[1, tile]
            psi.append((p_re * o_re - p_im * o_im, p_re * o_im + p_im * o_re))
        for part in range(2):
            lanes = slice(part * LANES, (part + 1) * LANES)
            uh[:, lanes], ul[:, lanes] = split(psi[0][part] + psi[1][part])
            vh[:, lanes], vl[:, lanes] = split(psi[0][part] - psi[1][part])
        yield
        even = dot3(uh[...], ul[...], *table(let))
        odd = dot3(vh[...], vl[...], *table(lot))
        for part in range(2):
            rows = slice(part * half, (part + 1) * half)
            for tile, y in enumerate((even, odd)):
                lanes = slice(tile * LANES, (tile + 1) * LANES)
                y = y[:, part * LANES : (part + 1) * LANES]
                uh[rows, lanes], ul[rows, lanes] = split(y[:half] + y[half:])
                vh[rows, lanes], vl[rows, lanes] = split(y[:half] - y[half:])
        yield
        for copy in fetch(slot):
            copy.wait()
        for parity, (h, l, which) in enumerate(((uh, ul, le), (vh, vl, lo))):
            th, tl = table(which)
            far = dot(th, h[...]) + dot(tl, h[...]) + dot(th, l[...])
            f_re, f_im = far[:half], far[half:]
            m = [measured[slot, tile, pl.ds(parity, half, stride=2), :] for tile in range(2)]
            mh, ml = split(jnp.concatenate(m, axis=1))
            excess = f_re * f_re + f_im * f_im - (dot(mh, spread[...]) + dot(ml, spread[...]))
            h[:half, :], l[:half, :] = split(excess * f_re)
            h[half:, :], l[half:, :] = split(excess * f_im)
        yield
        th, tl = table(let)
        even = dot(th, uh[...]) + dot(tl, uh[...]) + dot(th, ul[...])
        th, tl = table(lot)
        odd = dot(th, vh[...]) + dot(tl, vh[...]) + dot(th, vl[...])
        for part in range(2):
            rows = slice(part * half, (part + 1) * half)
            lanes = slice(part * LANES, (part + 1) * LANES)
            for sign in range(2):
                out = slice(sign * half, (sign + 1) * half)
                t = even[rows] + odd[rows] if sign == 0 else even[rows] - odd[rows]
                uh[out, lanes], ul[out, lanes] = split(t[:, :LANES])
                vh[out, lanes], vl[out, lanes] = split(t[:, LANES:])
        yield
        even = dot3(uh[...], ul[...], *table(le))
        odd = dot3(vh[...], vl[...], *table(lo))
        for tile in range(2):
            chi = even + odd if tile == 0 else even - odd
            c_re, c_im = chi[:, :LANES], chi[:, LANES:]
            p_re, p_im = turned[0, tile], turned[1, tile]
            for part, g in enumerate((p_re * c_re + p_im * c_im, p_re * c_im - p_im * c_re)):
                if tile == 0:
                    places = (
                        (column, jnp.where(low_lanes, 0.0, g)),
                        (wrap_column, jnp.where(low_lanes, g, 0.0)),
                    )
                else:
                    places = ((column + 1, g),)
                for at, value in places:
                    top = value[:SUBLANES]
                    kept = jnp.where(low_rows, 0.0, top)
                    acc[part, at, body, :] += jnp.concatenate([kept, value[SUBLANES:]], axis=0)
                    acc[part, at, tail, :] += jnp.where(low_rows, top, 0.0)
        yield

    def buffers(which):
        return (turned.at[which], *(planes.at[which, n] for n in range(4)))

    def together(*slots):
        for _ in zip(*(visit(slot, *buffers(which)) for which, slot in enumerate(slots))):
            pass

    def enlist(slot, count):
        @pl.when(live(slot))
        def _():
            listed[count] = slot

        return count + live(slot).astype(jnp.int32)

    count = lax.fori_loop(0, used, enlist, 0)

    @pl.loop(0, count // 2)
    def _(pair):
        together(listed[2 * pair], listed[2 * pair + 1])

    @pl.when(count % 2 == 1)
    def _():
        together(listed[count - 1])

    sent = []

    def send(source, target):
        sent.append(pltpu.make_async_copy(source, target, out_sems.at[len(sent)]))
        sent[-1].start()

    last = tiles - 1
    for part in range(2):
        if beyond:
            first_row = 0
            for spill_ref in spill_refs:
                rows = pl.ds(first_row, spill_ref.shape[1])
                send(acc.at[part, last, rows], spill_ref.at[part])
                first_row += spill_ref.shape[1]
        else:
            send(acc.at[part, 0], grad_ref.at[part])
            for column in range(1, tiles):
                send(acc.at[part, column], begun_ref.at[part, column - 1])
    if beyond:
        earlier.wait()
    routing = tiles if beyond else 1

    for chunk in range(height // size):
        rows = pl.ds(chunk * size, size)
        for column in range(routing):
            g_re, g_im = acc[0, column, rows, :], acc[1, column, rows, :]
            if beyond and column < last:
                g_re = g_re + prior[0, column, rows, :]
                g_im = g_im + prior[1, column, rows, :]
                lanes = pl.ds(column * LANES, LANES)
                for part, g in enumerate((g_re, g_im)):
                    acc[part, column, rows, :] = g
                    send(acc.at[part, column, rows], grad_ref.at[part, rows, lanes])
            value = ext[0, column, rows, :] * g_im - ext[1, column, rows, :] * g_re
            residual[column, rows, :] = value
            residual[column, pl.ds(height + chunk * size, size), :] = value

    shift = shift_ref[0]
    for chunk in range(height // size):
        rows = pl.ds(chunk * size, size)
        for column in range(routing):
            lanes = slice(column * LANES, (column + 1) * LANES)
            routed[rows, lanes] = residual[column, pl.ds(height - shift + chunk * size, size), :]
        send(routed.at[rows], routed_ref.at[rows])
    for copy in sent:
        copy.wait()


def margin_kernel(tile_re, tile_im, out, held, sems):
    height = tile_re.shape[0]
    first, second = [], []
    for n, tile in enumerate((tile_re, tile_im)):
        for part in range(2):
            rows = pl.ds(part * height // 2, height // 2)
            source = tile.at[rows, pl.ds(0, LANES)]
            sem = sems.at[2 * n + part]
            first.append(pltpu.make_async_copy(source, held.at[n, rows], sem))
            second.append(pltpu.make_async_copy(held.at[n, rows], out.at[n, rows], sem))
    for copy in first:
        copy.start()
    for before, after in zip(first, second):
        before.wait()
        after.start()
    for copy in second:
        copy.wait()


def margins(tile_re, tile_im):
    shape = (2, tile_re.shape[0], LANES)
    return pl.pallas_call(
        margin_kernel,
        out_shape=jax.ShapeDtypeStruct(shape, jnp.float32),
        in_specs=[HBM, HBM],
        out_specs=HBM,
        scratch_shapes=[pltpu.VMEM(shape, jnp.float32), pltpu.SemaphoreType.DMA((4,))],
        compiler_params=pltpu.CompilerParams(vmem_limit_bytes=VMEM_BYTES),
        name="margins",
    )(tile_re, tile_im)


def probe_phase(used, positions, shift, tile, edge, begun, probe, intensity):
    height, width = tile[0].shape
    size = probe[0].shape[0]
    slots = intensity.shape[0]
    columns = width // LANES
    beyond = edge is not None
    tables, spread = dft_tables(size)
    plane = pltpu.VMEM((size, size), SPLIT)
    planes = pltpu.VMEM((2, columns, height, LANES), jnp.float32)
    routing = columns if beyond else 1

    def out(*shape):
        return jax.ShapeDtypeStruct(shape, jnp.float32)

    if beyond:
        operands = (*tile, edge, begun)
        early = height * 9 // 16 // SUBLANES * SUBLANES
        late = (height - early) // 2 // SUBLANES * SUBLANES
        spills = [out(2, rows, LANES) for rows in (early, late, height - early - late)]
        outs = (out(2, height, width - LANES), *spills, out(height, width))
        base = LANES
    else:
        operands = tile
        outs = (out(2, height, LANES), out(2, columns - 1, height, LANES), out(height, LANES))
        base = 0
    return pl.pallas_call(
        functools.partial(probe_kernel, base=base, beyond=beyond),
        out_shape=outs,
        in_specs=[SMEM, SMEM, SMEM, *[HBM if x is not edge else ANY for x in operands], *[HBM] * 5],
        out_specs=(HBM,) * len(outs),
        scratch_shapes=[
            planes, planes,
            pltpu.VMEM((slots, 2, size, LANES), jnp.float32),
            pltpu.VMEM((2, size, size), jnp.float32),
            pltpu.VMEM(tables.shape, SPLIT),
            plane,
            pltpu.VMEM((2, 2, 2, size, LANES), jnp.float32),
            pltpu.VMEM((2, 4, size, size), SPLIT),
            pltpu.VMEM((routing, 2 * height, LANES), jnp.float32),
            pltpu.VMEM((height, outs[-1].shape[1]), jnp.float32),
            pltpu.VMEM((2, columns - 1, height, LANES), jnp.float32),
            pltpu.SMEM((slots,), jnp.int32),
            pltpu.SemaphoreType.DMA((2, 2 * columns + 2)),
            pltpu.SemaphoreType.DMA((slots, 2)),
            pltpu.SemaphoreType.DMA((3 * columns + (2 * columns + 1) * (height // size),)),
        ],
        compiler_params=pltpu.CompilerParams(vmem_limit_bytes=VMEM_BYTES),
        cost_estimate=pl.CostEstimate(
            flops=26 * slots * size**3, bytes_accessed=16 * height * width, transcendentals=0
        ),
        name="probes_beyond" if beyond else "probes_within",
    )(used, positions, shift, *operands, *probe, intensity, jnp.asarray(tables), jnp.asarray(spread))


def shift_tables(slope, depth):
    numer = jnp.arange(depth, dtype=jnp.int32)[None, :] * slope[:, None]
    whole = jnp.floor_divide(numer, depth)
    return whole, (numer - whole * depth).astype(jnp.float32) / depth


class Turned:
    def __init__(self, band, columns, margin):
        self.band = band
        self.segments = LANES // band
        self.length = columns // self.segments
        self.blocks = self.length // LANES
        self.margin = margin
        self.rows = self.length + 2 * margin

    def scratch(self, count):
        return pltpu.VMEM((count, self.rows, LANES), jnp.float32)

    def store(self, ref, lead, at, value):
        rows = value.shape[0]
        ref[lead, pl.ds(self.margin + at, rows), :] = value
        if at < self.margin:
            ref[lead, pl.ds(self.margin + self.length + at, rows), :] = pltpu.roll(
                value, LANES - self.band, axis=1
            )
        if at >= self.length - self.margin:
            ref[lead, pl.ds(at - self.length + self.margin, rows), :] = pltpu.roll(
                value, self.band, axis=1
            )

    def project(self, whole, frac, ref, tilt, at, rows):
        depth = ref.shape[0]

        def add_level(level, totals):
            plain, weighted = totals
            start = self.margin + at - whole[tilt, level] - SUBLANES
            x = ref[level, pl.ds(start, rows + SUBLANES), :]
            return plain + x[SUBLANES:], weighted + frac[tilt, level] * x

        zero = jnp.zeros((rows + SUBLANES, LANES), jnp.float32)
        plain, weighted = lax.fori_loop(
            0, depth, add_level, (zero[SUBLANES:], zero), unroll=8
        )
        return plain - weighted[SUBLANES:] + weighted[SUBLANES - 1 : SUBLANES - 1 + rows]


def old_kernel(turned, whole, frac, volume, old, cells):
    depth = volume.shape[0]

    @pl.loop(0, depth)
    def _(level):
        for block in range(turned.blocks):
            cut = []
            for segment in range(turned.segments):
                start = segment * turned.length + block * LANES
                cut.append(volume[level, :, start : start + LANES])
            turned.store(cells, level, block * LANES, jnp.concatenate(cut, axis=0).T)

    @pl.loop(0, whole.shape[0])
    def _(tilt):
        for block in range(turned.blocks):
            at = block * LANES
            old[tilt, at : at + LANES, :] = turned.project(whole, frac, cells, tilt, at, LANES)


def step_kernel(
    turned, whole, frac, left_from, right_from, old, parts, update,
    near, cells, left, right, before, after, sems, level_sems,
):
    old_copy = pltpu.make_async_copy(old, before, sems.at[0, 0])
    depth = cells.shape[0]
    tilts = near.shape[0]
    tiles = right_from.shape[0] // tilts
    own = right_from.shape[2] // LANES
    band = turned.band

    def fetch(tilt):
        block = pl.ds(tilt * tiles, tiles)
        return [
            pltpu.make_async_copy(source.at[block], target.at[block], sems.at[2 + n, tilt])
            for n, (source, target) in enumerate(((left_from, left), (right_from, right)))
        ]

    for tilt in range(tilts):
        for copy in fetch(tilt):
            copy.start()
    old_copy.start()

    def place(block, segment):
        return divmod(segment * turned.blocks + block, own)

    @pl.loop(0, tilts)
    def _(tilt):
        for copy in fetch(tilt):
            copy.wait()
        for block in range(turned.blocks):
            cut = []
            for segment in range(turned.segments):
                tile, column = place(block, segment)
                source = tilt * tiles + tile
                if column > 0:
                    value = right[source, :, (column - 1) * LANES : column * LANES]
                elif tile > 0:
                    value = left[source] + right[source - 1, :, (own - 1) * LANES :]
                else:
                    value = left[source]
                cut.append(value)
            value = jnp.concatenate(cut, axis=0).T * (1.0 / tilts)
            turned.store(near, tilt, block * LANES, value)

    rows = LANES // 2

    def keep(level):
        main = cells.at[level, pl.ds(turned.margin, turned.length), :]
        return pltpu.make_async_copy(main, update.at[level], level_sems.at[level])

    @pl.loop(0, depth)
    def _(level):
        for at in range(0, turned.length, rows):
            plain = weighted = None
            for tilt in range(tilts):
                start = turned.margin + at + whole[tilt, level]
                x = near[tilt, pl.ds(start, rows + SUBLANES), :]
                y = frac[tilt, level] * x
                plain = x[:rows] if plain is None else plain + x[:rows]
                weighted = y if weighted is None else weighted + y
            value = plain - weighted[:rows] + weighted[1 : 1 + rows]
            turned.store(cells, level, at, value)
        keep(level).start()

    old_copy.wait()

    def send(tilt):
        block = pl.ds(tilt * tiles, tiles)
        return pltpu.make_async_copy(after.at[block], parts.at[block], sems.at[1, tilt])

    @pl.loop(0, tilts)
    def _(tilt):
        for block in range(turned.blocks):
            at = block * LANES
            before[tilt, at : at + LANES, :] += turned.project(whole, frac, cells, tilt, at, LANES)
        for block in range(turned.blocks):
            total = before[tilt, block * LANES : (block + 1) * LANES, :].T
            for segment in range(turned.segments):
                tile, column = place(block, segment)
                after[tilt * tiles + tile, :, column * LANES : (column + 1) * LANES] = total[
                    segment * band : (segment + 1) * band
                ]

        send(tilt).start()

    for tilt in range(tilts):
        send(tilt).wait()
    for level in range(depth):
        keep(level).wait()


def fresh_kernel(turned, volume, update, fresh):
    for level in range(volume.shape[0]):
        for block in range(turned.blocks):
            value = update[level, block * LANES : (block + 1) * LANES, :].T
            for segment in range(turned.segments):
                start = segment * turned.length + block * LANES
                lanes = slice(start, start + LANES)
                rows = slice(segment * turned.band, (segment + 1) * turned.band)
                fresh[level, :, lanes] = volume[level, :, lanes] + value[rows]


def kernel_options(flops, size, share=1):
    return dict(
        compiler_params=pltpu.CompilerParams(vmem_limit_bytes=int(VMEM_BYTES * share)),
        cost_estimate=pl.CostEstimate(flops=flops, bytes_accessed=size, transcendentals=0),
    )


def old_projection(turned, whole, frac, volume):
    tilts = whole.shape[0]
    return pl.pallas_call(
        functools.partial(old_kernel, turned),
        out_shape=jax.ShapeDtypeStruct((tilts, turned.length, LANES), jnp.float32),
        in_specs=[SMEM, SMEM, VMEM],
        out_specs=VMEM,
        scratch_shapes=[turned.scratch(volume.shape[0])],
        name="old_projection",
        **kernel_options(8 * tilts * volume.size, 4 * volume.size),
    )(whole, frac, volume)


def volume_step(turned, whole, frac, left, right, old):
    tilts, depth = whole.shape
    return pl.pallas_call(
        functools.partial(step_kernel, turned),
        out_shape=(
            jax.ShapeDtypeStruct(right.shape, jnp.float32),
            jax.ShapeDtypeStruct((depth, turned.length, LANES), jnp.float32),
        ),
        in_specs=[SMEM, SMEM, ANY, ANY, HBM],
        out_specs=(HBM, HBM),
        scratch_shapes=[
            turned.scratch(tilts), turned.scratch(depth),
            pltpu.VMEM(left.shape, jnp.float32),
            pltpu.VMEM(right.shape, jnp.float32),
            pltpu.VMEM(old.shape, jnp.float32),
            pltpu.VMEM(right.shape, jnp.float32),
            pltpu.SemaphoreType.DMA((4, tilts)),
            pltpu.SemaphoreType.DMA((depth,)),
        ],
        name="volume_step",
        **kernel_options(16 * depth * old.size, 4 * depth * turned.length * LANES, 9 / 10),
    )(whole, frac, left, right, old)


def fresh_volume(turned, volume, update):
    depth, band, columns = volume.shape
    levels = math.gcd(depth, 4)
    cells = pl.BlockSpec((levels, band, columns), lambda i: (i, 0, 0))
    flat = pl.BlockSpec((levels, turned.length, LANES), lambda i: (i, 0, 0))
    return pl.pallas_call(
        functools.partial(fresh_kernel, turned),
        grid=(depth // levels,),
        out_shape=jax.ShapeDtypeStruct(volume.shape, jnp.float32),
        in_specs=[cells, flat],
        out_specs=cells,
        name="fresh_volume",
        **kernel_options(volume.size, 12 * volume.size),
    )(volume, update)


def local(
    obj_re, obj_im, probe_re, probe_im, intensity, positions, counts, row_shift, slope, volume
):
    tile = (obj_re[0], obj_im[0])
    height, width = tile[0].shape
    depth, band, columns = volume.shape
    axes = ("tilt", "tile")
    devices = lax.axis_size("tilt") * lax.axis_size("tile")
    turned = Turned(band, columns, width)
    whole, frac = shift_tables(slope, depth)
    probe = (probe_re, probe_im)

    within = (counts, positions[0], row_shift)

    def exchanged(blocks):
        return lax.all_to_all(blocks, axes, split_axis=0, concat_axis=0, tiled=True)

    edge = passed_along(margins(*tile), "tile", -1)
    grad_left, begun, left = probe_phase(*within, tile, None, None, probe, intensity[0])
    left, whole, frac = lax.optimization_barrier((left, whole, frac))
    left = exchanged(left.reshape(devices, band, LANES))
    grad_right, early, late, relayed, right = probe_phase(*within, tile, edge, begun, probe, intensity[0])
    right, left, whole = lax.optimization_barrier((right, left, whole))
    right = exchanged(right.reshape(devices, band, width))
    old = old_projection(turned, whole, frac, volume)
    right, early, old = lax.optimization_barrier((right, early, old))
    early = passed_along(early, "tile", 1)
    parts, update = volume_step(turned, whole, frac, left, right, old)
    parts, early, late, relayed = lax.optimization_barrier((parts, early, late, relayed))
    late = passed_along(late, "tile", 1)
    straight = passed_by(relayed, "tile", 0, 1)
    relayed = passed_by(relayed, "tile", 1, -1)
    returned = exchanged(parts)
    fresh = fresh_volume(turned, volume, update)
    rows = early.shape[1]
    early = jnp.pad(early, ((0, 0), (0, height - rows), (0, 0)))
    grad = jnp.concatenate([grad_left + early, grad_right], axis=2)[:, None]
    relayed, fresh, grad = lax.optimization_barrier((relayed, fresh, grad))
    relayed = straight + passed_by(relayed, "tile", 0, 2)
    late = jnp.concatenate([late, relayed], axis=1)
    grad = grad.at[:, 0, rows:, :LANES].add(late)
    reprojection = jnp.roll(returned.reshape(height, width), -row_shift[0], axis=0)[None]
    return (fresh, reprojection, grad)


def solution(mesh):
    placed = (
        P("tilt", None, "tile"),
        P("tilt", None, "tile"),
        P(),
        P(),
        P("tilt", "tile", None, None),
        P("tilt", "tile", None),
        P("tilt", "tile"),
        P("tilt"),
        P(),
        P(None, ("tilt", "tile"), None),
    )
    return jax.shard_map(
        local,
        mesh=mesh,
        in_specs=placed,
        out_specs=(
            P(None, ("tilt", "tile"), None),
            P("tilt", None, "tile"),
            P(None, "tilt", None, "tile"),
        ),
        check_vma=False,
    )
```

```python
import functools
import math

import jax
import jax.numpy as jnp
import ml_dtypes
import numpy as np
from jax import lax
from jax.experimental import pallas as pl
from jax.experimental.pallas import tpu as pltpu
from jax.sharding import PartitionSpec as P

LANES = 128
SUBLANES = 8
VMEM_BYTES = 60 * 1024 * 1024
PROBE_SCRATCH = 15
SPLIT = jnp.bfloat16
ANY = pl.BlockSpec(memory_space=pl.ANY)
HBM = pl.BlockSpec(memory_space=pltpu.HBM)
SMEM = pl.BlockSpec(memory_space=pltpu.SMEM)
VMEM = pl.BlockSpec(memory_space=pltpu.VMEM)


def passed_along(block, axis, distance):
    devices = range(lax.axis_size(axis))
    route = [(i - distance, i) for i in devices if i - distance in devices]
    return lax.ppermute(block, axis, route)


def passed_by(block, axis, first, step):
    count = lax.axis_size(axis)
    route = [(i, i + step) for i in range(first, count, 2) if 0 <= i + step < count]
    return lax.ppermute(block, axis, route)


def halves(table):
    high = table.astype(ml_dtypes.bfloat16)
    low = (table - high.astype(np.float64)).astype(ml_dtypes.bfloat16)
    return high, low


def dft_tables(length):
    half = length // 2
    index = np.arange(length)
    angle = (index[:, None] * index[None, :] % length) * (-2.0 * math.pi / length)
    wave = (np.cos(angle) + 1j * np.sin(angle)) / math.sqrt(length)
    tables = []
    for parity in (0, 1):
        part = wave[parity::2, :half]
        pair = np.block([[part.real, -part.imag], [part.imag, part.real]])
        tables += [*halves(pair), *halves(pair.T)]
    order = np.concatenate([index[0::2], index[1::2]])
    spread = np.zeros((length, length))
    spread[order, index] = 1.0
    return np.stack(tables), spread.astype(ml_dtypes.bfloat16)


def split(x):
    high = x.astype(SPLIT)
    return high, (x - high.astype(jnp.float32)).astype(SPLIT)


def dot(a, b):
    return jnp.dot(a, b, preferred_element_type=jnp.float32)


def dot3(ah, al, bh, bl):
    return dot(ah, bh) + dot(ah, bl) + dot(al, bh)


def lanes_of(shape):
    return lax.broadcasted_iota(jnp.int32, shape, len(shape) - 1)


def rows_of(shape):
    return lax.broadcasted_iota(jnp.int32, shape, len(shape) - 2)


def rolled(x, row, lane):
    size = x.shape[0]
    tiles = x.shape[1] // LANES
    cut = []
    for tile in range(tiles):
        part = x[:, tile * LANES : (tile + 1) * LANES].reshape(-1, SUBLANES, LANES)
        turned = pltpu.roll(part, row, axis=1)
        before = jnp.concatenate([turned[-1:], turned[:-1]], axis=0)
        part = jnp.where(rows_of(part.shape) < row, before, turned).reshape(size, LANES)
        cut.append(pltpu.roll(part, lane, axis=1))
    keep = lanes_of(cut[0].shape) >= lane
    return [jnp.where(keep, cut[tile], cut[tile - 1]) for tile in range(tiles)]


def probe_kernel(
    used_ref, positions_ref, shift_ref,
    *refs, base, beyond,
):
    if beyond:
        (tile_re, tile_im, edge, begun, probe_re, probe_im, intensity, tables_from, spread_from,
         grad_ref, *spill_refs, routed_ref) = refs[: len(refs) - PROBE_SCRATCH]
    else:
        (tile_re, tile_im, probe_re, probe_im, intensity, tables_from, spread_from,
         grad_ref, begun_ref, routed_ref) = refs[: len(refs) - PROBE_SCRATCH]
    (ext, acc, measured, probes, tables, spread, turned, planes, residual, routed,
     prior, listed, sems, slot_sems, out_sems) = refs[len(refs) - PROBE_SCRATCH :]
    height = ext.shape[2]
    tiles = ext.shape[1]
    size = probes.shape[1]
    half = size // 2
    used = used_ref[0, 0]
    copies = [
        pltpu.make_async_copy(probe_re, probes.at[0], sems.at[0, 2 * tiles]),
        pltpu.make_async_copy(probe_im, probes.at[1], sems.at[0, 2 * tiles + 1]),
        pltpu.make_async_copy(tables_from, tables, sems.at[1, 0]),
        pltpu.make_async_copy(spread_from, spread, sems.at[1, 1]),
    ]
    for part, tile in enumerate((tile_re, tile_im)):
        for column in range(tiles):
            if beyond and column == tiles - 1:
                source = edge.at[part]
            else:
                source = tile.at[:, pl.ds(base + column * LANES, LANES)]
            sem = sems.at[0, part * tiles + column]
            copies.append(pltpu.make_async_copy(source, ext.at[part, column], sem))
    for copy in copies:
        copy.start()

    def fetch(slot):
        return [
            pltpu.make_async_copy(
                intensity.at[slot, :, pl.ds(tile * LANES, LANES)],
                measured.at[slot, tile],
                slot_sems.at[slot, tile],
            )
            for tile in range(2)
        ]

    def mine(slot):
        past = positions_ref[slot, 1] + size > base + tiles * LANES
        return past if not beyond else positions_ref[slot, 1] + size > base + (tiles - 1) * LANES

    def live(slot):
        return mine(slot) if beyond else jnp.logical_not(mine(slot))

    slots = measured.shape[0]
    for slot in range(slots):
        @pl.when(jnp.logical_and(slot < used, live(slot)))
        def _():
            for copy in fetch(slot):
                copy.start()

    @pl.loop(0, height // size)
    def _(chunk):
        rows = pl.ds(chunk * size, size)
        for part in range(2):
            for column in range(tiles):
                acc[part, column, rows, :] = jnp.zeros((size, LANES), jnp.float32)

    for copy in copies:
        copy.wait()
    if beyond:
        earlier = pltpu.make_async_copy(begun, prior, sems.at[1, 2])
        earlier.start()

    le, let, lo, lot = 0, 2, 4, 6

    def table(which):
        return tables[which], tables[which + 1]

    def visit(slot, turned, uh, ul, vh, vl):
        row = positions_ref[slot, 0]
        col = positions_ref[slot, 1] - base
        first = pl.multiple_of(row // SUBLANES * SUBLANES, SUBLANES)
        row_rest = row - first
        wrap = pl.multiple_of(jnp.minimum(first + size, height - SUBLANES), SUBLANES)
        column = col // LANES
        lane_rest = col - column * LANES
        wrap_column = jnp.minimum(column + 2, tiles - 1)
        body = pl.ds(first, size)
        tail = pl.ds(wrap, SUBLANES)
        low_rows = rows_of((SUBLANES, LANES)) < row_rest
        low_lanes = lanes_of((size, LANES)) < lane_rest

        for part in range(2):
            for tile, piece in enumerate(rolled(probes[part], row_rest, lane_rest)):
                turned[part, tile] = piece

        def window(part, at):
            block = ext[part, at, body, :]
            top = jnp.where(low_rows, ext[part, at, tail, :], block[:SUBLANES])
            return jnp.concatenate([top, block[SUBLANES:]], axis=0)

        psi = []
        for tile in range(2):
            if tile == 0:
                o_re, o_im = (
                    jnp.where(low_lanes, window(part, wrap_column), window(part, column))
                    for part in range(2)
                )
            else:
                o_re, o_im = (window(part, column + 1) for part in range(2))
            p_re, p_im = turned[0, tile], turned[1, tile]
            psi.append((p_re * o_re - p_im * o_im, p_re * o_im + p_im * o_re))
        for part in range(2):
            lanes = slice(part * LANES, (part + 1) * LANES)
            uh[:, lanes], ul[:, lanes] = split(psi[0][part] + psi[1][part])
            vh[:, lanes], vl[:, lanes] = split(psi[0][part] - psi[1][part])
        yield
        even = dot3(uh[...], ul[...], *table(let))
        odd = dot3(vh[...], vl[...], *table(lot))
        for part in range(2):
            rows = slice(part * half, (part + 1) * half)
            for tile, y in enumerate((even, odd)):
                lanes = slice(tile * LANES, (tile + 1) * LANES)
                y = y[:, part * LANES : (part + 1) * LANES]
                uh[rows, lanes], ul[rows, lanes] = split(y[:half] + y[half:])
                vh[rows, lanes], vl[rows, lanes] = split(y[:half] - y[half:])
        yield
        for copy in fetch(slot):
            copy.wait()
        for parity, (h, l, which) in enumerate(((uh, ul, le), (vh, vl, lo))):
            th, tl = table(which)
            far = dot(th, h[...]) + dot(tl, h[...]) + dot(th, l[...])
            f_re, f_im = far[:half], far[half:]
            m = [measured[slot, tile, pl.ds(parity, half, stride=2), :] for tile in range(2)]
            mh, ml = split(jnp.concatenate(m, axis=1))
            excess = f_re * f_re + f_im * f_im - (dot(mh, spread[...]) + dot(ml, spread[...]))
            h[:half, :], l[:half, :] = split(excess * f_re)
            h[half:, :], l[half:, :] = split(excess * f_im)
        yield
        th, tl = table(let)
        even = dot(th, uh[...]) + dot(tl, uh[...]) + dot(th, ul[...])
        th, tl = table(lot)
        odd = dot(th, vh[...]) + dot(tl, vh[...]) + dot(th, vl[...])
        for part in range(2):
            rows = slice(part * half, (part + 1) * half)
            lanes = slice(part * LANES, (part + 1) * LANES)
            for sign in range(2):
                out = slice(sign * half, (sign + 1) * half)
                t = even[rows] + odd[rows] if sign == 0 else even[rows] - odd[rows]
                uh[out, lanes], ul[out, lanes] = split(t[:, :LANES])
                vh[out, lanes], vl[out, lanes] = split(t[:, LANES:])
        yield
        even = dot3(uh[...], ul[...], *table(le))
        odd = dot3(vh[...], vl[...], *table(lo))
        for tile in range(2):
            chi = even + odd if tile == 0 else even - odd
            c_re, c_im = chi[:, :LANES], chi[:, LANES:]
            p_re, p_im = turned[0, tile], turned[1, tile]
            for part, g in enumerate((p_re * c_re + p_im * c_im, p_re * c_im - p_im * c_re)):
                if tile == 0:
                    places = (
                        (column, jnp.where(low_lanes, 0.0, g)),
                        (wrap_column, jnp.where(low_lanes, g, 0.0)),
                    )
                else:
                    places = ((column + 1, g),)
                for at, value in places:
                    top = value[:SUBLANES]
                    kept = jnp.where(low_rows, 0.0, top)
                    acc[part, at, body, :] += jnp.concatenate([kept, value[SUBLANES:]], axis=0)
                    acc[part, at, tail, :] += jnp.where(low_rows, top, 0.0)
        yield

    def buffers(which):
        return (turned.at[which], *(planes.at[which, n] for n in range(4)))

    def together(*slots):
        for _ in zip(*(visit(slot, *buffers(which)) for which, slot in enumerate(slots))):
            pass

    def enlist(slot, count):
        @pl.when(live(slot))
        def _():
            listed[count] = slot

        return count + live(slot).astype(jnp.int32)

    count = lax.fori_loop(0, used, enlist, 0)

    @pl.loop(0, count // 2)
    def _(pair):
        together(listed[2 * pair], listed[2 * pair + 1])

    @pl.when(count % 2 == 1)
    def _():
        together(listed[count - 1])

    sent = []

    def send(source, target):
        sent.append(pltpu.make_async_copy(source, target, out_sems.at[len(sent)]))
        sent[-1].start()

    last = tiles - 1
    for part in range(2):
        if beyond:
            first_row = 0
            for spill_ref in spill_refs:
                rows = pl.ds(first_row, spill_ref.shape[1])
                send(acc.at[part, last, rows], spill_ref.at[part])
                first_row += spill_ref.shape[1]
        else:
            send(acc.at[part, 0], grad_ref.at[part])
            for column in range(1, tiles):
                send(acc.at[part, column], begun_ref.at[part, column - 1])
    if beyond:
        earlier.wait()
    routing = tiles if beyond else 1

    for chunk in range(height // size):
        rows = pl.ds(chunk * size, size)
        for column in range(routing):
            g_re, g_im = acc[0, column, rows, :], acc[1, column, rows, :]
            if beyond and column < last:
                g_re = g_re + prior[0, column, rows, :]
                g_im = g_im + prior[1, column, rows, :]
                lanes = pl.ds(column * LANES, LANES)
                for part, g in enumerate((g_re, g_im)):
                    acc[part, column, rows, :] = g
                    send(acc.at[part, column, rows], grad_ref.at[part, rows, lanes])
            value = ext[0, column, rows, :] * g_im - ext[1, column, rows, :] * g_re
            residual[column, rows, :] = value
            residual[column, pl.ds(height + chunk * size, size), :] = value

    shift = shift_ref[0]
    for chunk in range(height // size):
        rows = pl.ds(chunk * size, size)
        for column in range(routing):
            lanes = slice(column * LANES, (column + 1) * LANES)
            routed[rows, lanes] = residual[column, pl.ds(height - shift + chunk * size, size), :]
        send(routed.at[rows], routed_ref.at[rows])
    for copy in sent:
        copy.wait()


def margin_kernel(tile_re, tile_im, out, held, sems):
    height = tile_re.shape[0]
    first, second = [], []
    for n, tile in enumerate((tile_re, tile_im)):
        for part in range(2):
            rows = pl.ds(part * height // 2, height // 2)
            source = tile.at[rows, pl.ds(0, LANES)]
            sem = sems.at[2 * n + part]
            first.append(pltpu.make_async_copy(source, held.at[n, rows], sem))
            second.append(pltpu.make_async_copy(held.at[n, rows], out.at[n, rows], sem))
    for copy in first:
        copy.start()
    for before, after in zip(first, second):
        before.wait()
        after.start()
    for copy in second:
        copy.wait()


def margins(tile_re, tile_im):
    shape = (2, tile_re.shape[0], LANES)
    return pl.pallas_call(
        margin_kernel,
        out_shape=jax.ShapeDtypeStruct(shape, jnp.float32),
        in_specs=[HBM, HBM],
        out_specs=HBM,
        scratch_shapes=[pltpu.VMEM(shape, jnp.float32), pltpu.SemaphoreType.DMA((4,))],
        compiler_params=pltpu.CompilerParams(vmem_limit_bytes=VMEM_BYTES),
        name="margins",
    )(tile_re, tile_im)


def probe_phase(used, positions, shift, tile, edge, begun, probe, intensity):
    height, width = tile[0].shape
    size = probe[0].shape[0]
    slots = intensity.shape[0]
    columns = width // LANES
    beyond = edge is not None
    tables, spread = dft_tables(size)
    plane = pltpu.VMEM((size, size), SPLIT)
    planes = pltpu.VMEM((2, columns, height, LANES), jnp.float32)
    routing = columns if beyond else 1

    def out(*shape):
        return jax.ShapeDtypeStruct(shape, jnp.float32)

    if beyond:
        operands = (*tile, edge, begun)
        early = height * 9 // 16 // SUBLANES * SUBLANES
        late = (height - early) // 2 // SUBLANES * SUBLANES
        spills = [out(2, rows, LANES) for rows in (early, late, height - early - late)]
        outs = (out(2, height, width - LANES), *spills, out(height, width))
        base = LANES
    else:
        operands = tile
        outs = (out(2, height, LANES), out(2, columns - 1, height, LANES), out(height, LANES))
        base = 0
    return pl.pallas_call(
        functools.partial(probe_kernel, base=base, beyond=beyond),
        out_shape=outs,
        in_specs=[SMEM, SMEM, SMEM, *[HBM if x is not edge else ANY for x in operands], *[HBM] * 5],
        out_specs=(HBM,) * len(outs),
        scratch_shapes=[
            planes, planes,
            pltpu.VMEM((slots, 2, size, LANES), jnp.float32),
            pltpu.VMEM((2, size, size), jnp.float32),
            pltpu.VMEM(tables.shape, SPLIT),
            plane,
            pltpu.VMEM((2, 2, 2, size, LANES), jnp.float32),
            pltpu.VMEM((2, 4, size, size), SPLIT),
            pltpu.VMEM((routing, 2 * height, LANES), jnp.float32),
            pltpu.VMEM((height, outs[-1].shape[1]), jnp.float32),
            pltpu.VMEM((2, columns - 1, height, LANES), jnp.float32),
            pltpu.SMEM((slots,), jnp.int32),
            pltpu.SemaphoreType.DMA((2, 2 * columns + 2)),
            pltpu.SemaphoreType.DMA((slots, 2)),
            pltpu.SemaphoreType.DMA((3 * columns + (2 * columns + 1) * (height // size),)),
        ],
        compiler_params=pltpu.CompilerParams(vmem_limit_bytes=VMEM_BYTES * 21 // 20),
        cost_estimate=pl.CostEstimate(
            flops=26 * slots * size**3, bytes_accessed=16 * height * width, transcendentals=0
        ),
        name="probes_beyond" if beyond else "probes_within",
    )(used, positions, shift, *operands, *probe, intensity, jnp.asarray(tables), jnp.asarray(spread))


def shift_tables(slope, depth):
    numer = jnp.arange(depth, dtype=jnp.int32)[None, :] * slope[:, None]
    whole = jnp.floor_divide(numer, depth)
    return whole, (numer - whole * depth).astype(jnp.float32) / depth


class Turned:
    def __init__(self, band, columns, margin):
        self.band = band
        self.segments = LANES // band
        self.length = columns // self.segments
        self.blocks = self.length // LANES
        self.margin = margin
        self.rows = self.length + 2 * margin

    def scratch(self, count):
        return pltpu.VMEM((count, self.rows, LANES), jnp.float32)

    def store(self, ref, lead, at, value):
        rows = value.shape[0]
        ref[lead, pl.ds(self.margin + at, rows), :] = value
        if at < self.margin:
            ref[lead, pl.ds(self.margin + self.length + at, rows), :] = pltpu.roll(
                value, LANES - self.band, axis=1
            )
        if at >= self.length - self.margin:
            ref[lead, pl.ds(at - self.length + self.margin, rows), :] = pltpu.roll(
                value, self.band, axis=1
            )

    def project(self, whole, frac, ref, tilt, at, rows):
        depth = ref.shape[0]

        def add_level(level, totals):
            plain, weighted = totals
            start = self.margin + at - whole[tilt, level] - SUBLANES
            x = ref[level, pl.ds(start, rows + SUBLANES), :]
            return plain + x[SUBLANES:], weighted + frac[tilt, level] * x

        zero = jnp.zeros((rows + SUBLANES, LANES), jnp.float32)
        plain, weighted = lax.fori_loop(
            0, depth, add_level, (zero[SUBLANES:], zero), unroll=8
        )
        return plain - weighted[SUBLANES:] + weighted[SUBLANES - 1 : SUBLANES - 1 + rows]


def old_kernel(turned, whole, frac, volume, old, cells):
    depth = volume.shape[0]

    @pl.loop(0, depth)
    def _(level):
        for block in range(turned.blocks):
            cut = []
            for segment in range(turned.segments):
                start = segment * turned.length + block * LANES
                cut.append(volume[level, :, start : start + LANES])
            turned.store(cells, level, block * LANES, jnp.concatenate(cut, axis=0).T)

    @pl.loop(0, whole.shape[0])
    def _(tilt):
        for block in range(turned.blocks):
            at = block * LANES
            old[tilt, at : at + LANES, :] = turned.project(whole, frac, cells, tilt, at, LANES)


def step_kernel(
    turned, whole, frac, left_from, right_from, old, parts, update,
    near, cells, left, right, before, after, sems, level_sems,
):
    old_copy = pltpu.make_async_copy(old, before, sems.at[0, 0])
    depth = cells.shape[0]
    tilts = near.shape[0]
    tiles = right_from.shape[0] // tilts
    own = right_from.shape[2] // LANES
    band = turned.band

    def fetch(tilt):
        block = pl.ds(tilt * tiles, tiles)
        return [
            pltpu.make_async_copy(source.at[block], target.at[block], sems.at[2 + n, tilt])
            for n, (source, target) in enumerate(((left_from, left), (right_from, right)))
        ]

    for tilt in range(tilts):
        for copy in fetch(tilt):
            copy.start()
    old_copy.start()

    def place(block, segment):
        return divmod(segment * turned.blocks + block, own)

    @pl.loop(0, tilts)
    def _(tilt):
        for copy in fetch(tilt):
            copy.wait()
        for block in range(turned.blocks):
            cut = []
            for segment in range(turned.segments):
                tile, column = place(block, segment)
                source = tilt * tiles + tile
                if column > 0:
                    value = right[source, :, (column - 1) * LANES : column * LANES]
                elif tile > 0:
                    value = left[source] + right[source - 1, :, (own - 1) * LANES :]
                else:
                    value = left[source]
                cut.append(value)
            value = jnp.concatenate(cut, axis=0).T * (1.0 / tilts)
            turned.store(near, tilt, block * LANES, value)

    rows = LANES // 2

    def keep(level):
        main = cells.at[level, pl.ds(turned.margin, turned.length), :]
        return pltpu.make_async_copy(main, update.at[level], level_sems.at[level])

    @pl.loop(0, depth)
    def _(level):
        for at in range(0, turned.length, rows):
            plain = weighted = None
            for tilt in range(tilts):
                start = turned.margin + at + whole[tilt, level]
                x = near[tilt, pl.ds(start, rows + SUBLANES), :]
                y = frac[tilt, level] * x
                plain = x[:rows] if plain is None else plain + x[:rows]
                weighted = y if weighted is None else weighted + y
            value = plain - weighted[:rows] + weighted[1 : 1 + rows]
            turned.store(cells, level, at, value)
        keep(level).start()

    old_copy.wait()

    def send(tilt):
        block = pl.ds(tilt * tiles, tiles)
        return pltpu.make_async_copy(after.at[block], parts.at[block], sems.at[1, tilt])

    @pl.loop(0, tilts)
    def _(tilt):
        for block in range(turned.blocks):
            at = block * LANES
            before[tilt, at : at + LANES, :] += turned.project(whole, frac, cells, tilt, at, LANES)
        for block in range(turned.blocks):
            total = before[tilt, block * LANES : (block + 1) * LANES, :].T
            for segment in range(turned.segments):
                tile, column = place(block, segment)
                after[tilt * tiles + tile, :, column * LANES : (column + 1) * LANES] = total[
                    segment * band : (segment + 1) * band
                ]

        send(tilt).start()

    for tilt in range(tilts):
        send(tilt).wait()
    for level in range(depth):
        keep(level).wait()


def fresh_kernel(turned, volume, update, fresh):
    for level in range(volume.shape[0]):
        for block in range(turned.blocks):
            value = update[level, block * LANES : (block + 1) * LANES, :].T
            for segment in range(turned.segments):
                start = segment * turned.length + block * LANES
                lanes = slice(start, start + LANES)
                rows = slice(segment * turned.band, (segment + 1) * turned.band)
                fresh[level, :, lanes] = volume[level, :, lanes] + value[rows]


def kernel_options(flops, size, share=1):
    return dict(
        compiler_params=pltpu.CompilerParams(vmem_limit_bytes=int(VMEM_BYTES * share)),
        cost_estimate=pl.CostEstimate(flops=flops, bytes_accessed=size, transcendentals=0),
    )


def old_projection(turned, whole, frac, volume):
    tilts = whole.shape[0]
    return pl.pallas_call(
        functools.partial(old_kernel, turned),
        out_shape=jax.ShapeDtypeStruct((tilts, turned.length, LANES), jnp.float32),
        in_specs=[SMEM, SMEM, VMEM],
        out_specs=VMEM,
        scratch_shapes=[turned.scratch(volume.shape[0])],
        name="old_projection",
        **kernel_options(8 * tilts * volume.size, 4 * volume.size),
    )(whole, frac, volume)


def volume_step(turned, whole, frac, left, right, old):
    tilts, depth = whole.shape
    return pl.pallas_call(
        functools.partial(step_kernel, turned),
        out_shape=(
            jax.ShapeDtypeStruct(right.shape, jnp.float32),
            jax.ShapeDtypeStruct((depth, turned.length, LANES), jnp.float32),
        ),
        in_specs=[SMEM, SMEM, ANY, ANY, HBM],
        out_specs=(HBM, HBM),
        scratch_shapes=[
            turned.scratch(tilts), turned.scratch(depth),
            pltpu.VMEM(left.shape, jnp.float32),
            pltpu.VMEM(right.shape, jnp.float32),
            pltpu.VMEM(old.shape, jnp.float32),
            pltpu.VMEM(right.shape, jnp.float32),
            pltpu.SemaphoreType.DMA((4, tilts)),
            pltpu.SemaphoreType.DMA((depth,)),
        ],
        name="volume_step",
        **kernel_options(16 * depth * old.size, 4 * depth * turned.length * LANES, 9 / 10),
    )(whole, frac, left, right, old)


def fresh_volume(turned, volume, update):
    depth, band, columns = volume.shape
    levels = math.gcd(depth, 4)
    cells = pl.BlockSpec((levels, band, columns), lambda i: (i, 0, 0))
    flat = pl.BlockSpec((levels, turned.length, LANES), lambda i: (i, 0, 0))
    return pl.pallas_call(
        functools.partial(fresh_kernel, turned),
        grid=(depth // levels,),
        out_shape=jax.ShapeDtypeStruct(volume.shape, jnp.float32),
        in_specs=[cells, flat],
        out_specs=cells,
        name="fresh_volume",
        **kernel_options(volume.size, 12 * volume.size),
    )(volume, update)


def local(
    obj_re, obj_im, probe_re, probe_im, intensity, positions, counts, row_shift, slope, volume
):
    tile = (obj_re[0], obj_im[0])
    height, width = tile[0].shape
    depth, band, columns = volume.shape
    axes = ("tilt", "tile")
    devices = lax.axis_size("tilt") * lax.axis_size("tile")
    turned = Turned(band, columns, width)
    whole, frac = shift_tables(slope, depth)
    probe = (probe_re, probe_im)

    within = (counts, positions[0], row_shift)

    def exchanged(blocks):
        return lax.all_to_all(blocks, axes, split_axis=0, concat_axis=0, tiled=True)

    edge = passed_along(margins(*tile), "tile", -1)
    grad_left, begun, left = probe_phase(*within, tile, None, None, probe, intensity[0])
    left, whole, frac = lax.optimization_barrier((left, whole, frac))
    left = exchanged(left.reshape(devices, band, LANES))
    grad_right, early, late, relayed, right = probe_phase(*within, tile, edge, begun, probe, intensity[0])
    right, left, whole = lax.optimization_barrier((right, left, whole))
    right = exchanged(right.reshape(devices, band, width))
    old = old_projection(turned, whole, frac, volume)
    right, early, old = lax.optimization_barrier((right, early, old))
    early = passed_along(early, "tile", 1)
    parts, update = volume_step(turned, whole, frac, left, right, old)
    parts, early, late, relayed = lax.optimization_barrier((parts, early, late, relayed))
    late = passed_along(late, "tile", 1)
    straight = passed_by(relayed, "tile", 0, 1)
    relayed = passed_by(relayed, "tile", 1, -1)
    returned = exchanged(parts)
    fresh = fresh_volume(turned, volume, update)
    rows = early.shape[1]
    early = jnp.pad(early, ((0, 0), (0, height - rows), (0, 0)))
    grad = jnp.concatenate([grad_left + early, grad_right], axis=2)[:, None]
    relayed, fresh, grad = lax.optimization_barrier((relayed, fresh, grad))
    relayed = straight + passed_by(relayed, "tile", 0, 2)
    late = jnp.concatenate([late, relayed], axis=1)
    grad = grad.at[:, 0, rows:, :LANES].add(late)
    reprojection = jnp.roll(returned.reshape(height, width), -row_shift[0], axis=0)[None]
    return (fresh, reprojection, grad)


def solution(mesh):
    placed = (
        P("tilt", None, "tile"),
        P("tilt", None, "tile"),
        P(),
        P(),
        P("tilt", "tile", None, None),
        P("tilt", "tile", None),
        P("tilt", "tile"),
        P("tilt"),
        P(),
        P(None, ("tilt", "tile"), None),
    )
    return jax.shard_map(
        local,
        mesh=mesh,
        in_specs=placed,
        out_specs=(
            P(None, ("tilt", "tile"), None),
            P("tilt", None, "tile"),
            P(None, "tilt", None, "tile"),
        ),
        check_vma=False,
    )
```

```python
import functools
import math

import jax
import jax.numpy as jnp
import ml_dtypes
import numpy as np
from jax import lax
from jax.experimental import pallas as pl
from jax.experimental.pallas import tpu as pltpu
from jax.sharding import PartitionSpec as P

LANES = 128
SUBLANES = 8
VMEM_BYTES = 60 * 1024 * 1024
PROBE_SCRATCH = 15
SPLIT = jnp.bfloat16
ANY = pl.BlockSpec(memory_space=pl.ANY)
HBM = pl.BlockSpec(memory_space=pltpu.HBM)
SMEM = pl.BlockSpec(memory_space=pltpu.SMEM)
VMEM = pl.BlockSpec(memory_space=pltpu.VMEM)


def passed_along(block, axis, distance):
    devices = range(lax.axis_size(axis))
    route = [(i - distance, i) for i in devices if i - distance in devices]
    return lax.ppermute(block, axis, route)


def passed_by(block, axis, first, step):
    count = lax.axis_size(axis)
    route = [(i, i + step) for i in range(first, count, 2) if 0 <= i + step < count]
    return lax.ppermute(block, axis, route)


def halves(table):
    high = table.astype(ml_dtypes.bfloat16)
    low = (table - high.astype(np.float64)).astype(ml_dtypes.bfloat16)
    return high, low


def dft_tables(length):
    half = length // 2
    index = np.arange(length)
    angle = (index[:, None] * index[None, :] % length) * (-2.0 * math.pi / length)
    wave = (np.cos(angle) + 1j * np.sin(angle)) / math.sqrt(length)
    tables = []
    for parity in (0, 1):
        part = wave[parity::2, :half]
        pair = np.block([[part.real, -part.imag], [part.imag, part.real]])
        tables += [*halves(pair), *halves(pair.T)]
    order = np.concatenate([index[0::2], index[1::2]])
    spread = np.zeros((length, length))
    spread[order, index] = 1.0
    return np.stack(tables), spread.astype(ml_dtypes.bfloat16)


def split(x):
    high = x.astype(SPLIT)
    return high, (x - high.astype(jnp.float32)).astype(SPLIT)


def dot(a, b):
    return jnp.dot(a, b, preferred_element_type=jnp.float32)


def dot3(ah, al, bh, bl):
    return dot(ah, bh) + dot(ah, bl) + dot(al, bh)


def lanes_of(shape):
    return lax.broadcasted_iota(jnp.int32, shape, len(shape) - 1)


def rows_of(shape):
    return lax.broadcasted_iota(jnp.int32, shape, len(shape) - 2)


def rolled(x, row, lane):
    size = x.shape[0]
    tiles = x.shape[1] // LANES
    cut = []
    for tile in range(tiles):
        part = x[:, tile * LANES : (tile + 1) * LANES].reshape(-1, SUBLANES, LANES)
        turned = pltpu.roll(part, row, axis=1)
        before = jnp.concatenate([turned[-1:], turned[:-1]], axis=0)
        part = jnp.where(rows_of(part.shape) < row, before, turned).reshape(size, LANES)
        cut.append(pltpu.roll(part, lane, axis=1))
    keep = lanes_of(cut[0].shape) >= lane
    return [jnp.where(keep, cut[tile], cut[tile - 1]) for tile in range(tiles)]


def probe_kernel(
    used_ref, positions_ref, shift_ref,
    *refs, base, beyond,
):
    if beyond:
        (tile_re, tile_im, edge, begun, probe_re, probe_im, intensity, tables_from, spread_from,
         grad_ref, *spill_refs, routed_ref) = refs[: len(refs) - PROBE_SCRATCH]
    else:
        (tile_re, tile_im, probe_re, probe_im, intensity, tables_from, spread_from,
         grad_ref, begun_ref, routed_ref) = refs[: len(refs) - PROBE_SCRATCH]
    (ext, acc, measured, probes, tables, spread, turned, planes, residual, routed,
     prior, listed, sems, slot_sems, out_sems) = refs[len(refs) - PROBE_SCRATCH :]
    height = ext.shape[2]
    tiles = ext.shape[1]
    size = probes.shape[1]
    half = size // 2
    used = used_ref[0, 0]
    copies = [
        pltpu.make_async_copy(probe_re, probes.at[0], sems.at[0, 2 * tiles]),
        pltpu.make_async_copy(probe_im, probes.at[1], sems.at[0, 2 * tiles + 1]),
        pltpu.make_async_copy(tables_from, tables, sems.at[1, 0]),
        pltpu.make_async_copy(spread_from, spread, sems.at[1, 1]),
    ]
    for part, tile in enumerate((tile_re, tile_im)):
        for column in range(tiles):
            if beyond and column == tiles - 1:
                source = edge.at[part]
            else:
                source = tile.at[:, pl.ds(base + column * LANES, LANES)]
            sem = sems.at[0, part * tiles + column]
            copies.append(pltpu.make_async_copy(source, ext.at[part, column], sem))
    for copy in copies:
        copy.start()

    def fetch(slot):
        return [
            pltpu.make_async_copy(
                intensity.at[slot, :, pl.ds(tile * LANES, LANES)],
                measured.at[slot, tile],
                slot_sems.at[slot, tile],
            )
            for tile in range(2)
        ]

    def mine(slot):
        past = positions_ref[0, 1, slot] + size > base + tiles * LANES
        return past if not beyond else positions_ref[0, 1, slot] + size > base + (tiles - 1) * LANES

    def live(slot):
        return mine(slot) if beyond else jnp.logical_not(mine(slot))

    slots = measured.shape[0]
    for slot in range(slots):
        @pl.when(jnp.logical_and(slot < used, live(slot)))
        def _():
            for copy in fetch(slot):
                copy.start()

    @pl.loop(0, height // size)
    def _(chunk):
        rows = pl.ds(chunk * size, size)
        for part in range(2):
            for column in range(tiles):
                acc[part, column, rows, :] = jnp.zeros((size, LANES), jnp.float32)

    for copy in copies:
        copy.wait()
    if beyond:
        earlier = pltpu.make_async_copy(begun, prior, sems.at[1, 2])
        earlier.start()

    le, let, lo, lot = 0, 2, 4, 6

    def table(which):
        return tables[which], tables[which + 1]

    def visit(slot, turned, uh, ul, vh, vl):
        row = positions_ref[0, 0, slot]
        col = positions_ref[0, 1, slot] - base
        first = pl.multiple_of(row // SUBLANES * SUBLANES, SUBLANES)
        row_rest = row - first
        wrap = pl.multiple_of(jnp.minimum(first + size, height - SUBLANES), SUBLANES)
        column = col // LANES
        lane_rest = col - column * LANES
        wrap_column = jnp.minimum(column + 2, tiles - 1)
        body = pl.ds(first, size)
        tail = pl.ds(wrap, SUBLANES)
        low_rows = rows_of((SUBLANES, LANES)) < row_rest
        low_lanes = lanes_of((size, LANES)) < lane_rest

        for part in range(2):
            for tile, piece in enumerate(rolled(probes[part], row_rest, lane_rest)):
                turned[part, tile] = piece

        def window(part, at):
            block = ext[part, at, body, :]
            top = jnp.where(low_rows, ext[part, at, tail, :], block[:SUBLANES])
            return jnp.concatenate([top, block[SUBLANES:]], axis=0)

        psi = []
        for tile in range(2):
            if tile == 0:
                o_re, o_im = (
                    jnp.where(low_lanes, window(part, wrap_column), window(part, column))
                    for part in range(2)
                )
            else:
                o_re, o_im = (window(part, column + 1) for part in range(2))
            p_re, p_im = turned[0, tile], turned[1, tile]
            psi.append((p_re * o_re - p_im * o_im, p_re * o_im + p_im * o_re))
        for part in range(2):
            lanes = slice(part * LANES, (part + 1) * LANES)
            uh[:, lanes], ul[:, lanes] = split(psi[0][part] + psi[1][part])
            vh[:, lanes], vl[:, lanes] = split(psi[0][part] - psi[1][part])
        yield
        even = dot3(uh[...], ul[...], *table(let))
        odd = dot3(vh[...], vl[...], *table(lot))
        for part in range(2):
            rows = slice(part * half, (part + 1) * half)
            for tile, y in enumerate((even, odd)):
                lanes = slice(tile * LANES, (tile + 1) * LANES)
                y = y[:, part * LANES : (part + 1) * LANES]
                uh[rows, lanes], ul[rows, lanes] = split(y[:half] + y[half:])
                vh[rows, lanes], vl[rows, lanes] = split(y[:half] - y[half:])
        yield
        for copy in fetch(slot):
            copy.wait()
        for parity, (h, l, which) in enumerate(((uh, ul, le), (vh, vl, lo))):
            th, tl = table(which)
            far = dot(th, h[...]) + dot(tl, h[...]) + dot(th, l[...])
            f_re, f_im = far[:half], far[half:]
            m = [measured[slot, tile, pl.ds(parity, half, stride=2), :] for tile in range(2)]
            mh, ml = split(jnp.concatenate(m, axis=1))
            excess = f_re * f_re + f_im * f_im - (dot(mh, spread[...]) + dot(ml, spread[...]))
            h[:half, :], l[:half, :] = split(excess * f_re)
            h[half:, :], l[half:, :] = split(excess * f_im)
        yield
        th, tl = table(let)
        even = dot(th, uh[...]) + dot(tl, uh[...]) + dot(th, ul[...])
        th, tl = table(lot)
        odd = dot(th, vh[...]) + dot(tl, vh[...]) + dot(th, vl[...])
        for part in range(2):
            rows = slice(part * half, (part + 1) * half)
            lanes = slice(part * LANES, (part + 1) * LANES)
            for sign in range(2):
                out = slice(sign * half, (sign + 1) * half)
                t = even[rows] + odd[rows] if sign == 0 else even[rows] - odd[rows]
                uh[out, lanes], ul[out, lanes] = split(t[:, :LANES])
                vh[out, lanes], vl[out, lanes] = split(t[:, LANES:])
        yield
        even = dot3(uh[...], ul[...], *table(le))
        odd = dot3(vh[...], vl[...], *table(lo))
        for tile in range(2):
            chi = even + odd if tile == 0 else even - odd
            c_re, c_im = chi[:, :LANES], chi[:, LANES:]
            p_re, p_im = turned[0, tile], turned[1, tile]
            for part, g in enumerate((p_re * c_re + p_im * c_im, p_re * c_im - p_im * c_re)):
                if tile == 0:
                    places = (
                        (column, jnp.where(low_lanes, 0.0, g)),
                        (wrap_column, jnp.where(low_lanes, g, 0.0)),
                    )
                else:
                    places = ((column + 1, g),)
                for at, value in places:
                    top = value[:SUBLANES]
                    kept = jnp.where(low_rows, 0.0, top)
                    acc[part, at, body, :] += jnp.concatenate([kept, value[SUBLANES:]], axis=0)
                    acc[part, at, tail, :] += jnp.where(low_rows, top, 0.0)
        yield

    def buffers(which):
        return (turned.at[which], *(planes.at[which, n] for n in range(4)))

    def together(*slots):
        for _ in zip(*(visit(slot, *buffers(which)) for which, slot in enumerate(slots))):
            pass

    def enlist(slot, count):
        @pl.when(live(slot))
        def _():
            listed[count] = slot

        return count + live(slot).astype(jnp.int32)

    count = lax.fori_loop(0, used, enlist, 0)

    @pl.loop(0, count // 2)
    def _(pair):
        together(listed[2 * pair], listed[2 * pair + 1])

    @pl.when(count % 2 == 1)
    def _():
        together(listed[count - 1])

    sent = []

    def send(source, target):
        sent.append(pltpu.make_async_copy(source, target, out_sems.at[len(sent)]))
        sent[-1].start()

    last = tiles - 1
    for part in range(2):
        if beyond:
            first_row = 0
            for spill_ref in spill_refs:
                rows = pl.ds(first_row, spill_ref.shape[1])
                send(acc.at[part, last, rows], spill_ref.at[part])
                first_row += spill_ref.shape[1]
        else:
            send(acc.at[part, 0], grad_ref.at[part])
            for column in range(1, tiles):
                send(acc.at[part, column], begun_ref.at[part, column - 1])
    if beyond:
        earlier.wait()
    routing = tiles if beyond else 1

    for chunk in range(height // size):
        rows = pl.ds(chunk * size, size)
        for column in range(routing):
            g_re, g_im = acc[0, column, rows, :], acc[1, column, rows, :]
            if beyond and column < last:
                g_re = g_re + prior[0, column, rows, :]
                g_im = g_im + prior[1, column, rows, :]
                lanes = pl.ds(column * LANES, LANES)
                for part, g in enumerate((g_re, g_im)):
                    acc[part, column, rows, :] = g
                    send(acc.at[part, column, rows], grad_ref.at[part, rows, lanes])
            value = ext[0, column, rows, :] * g_im - ext[1, column, rows, :] * g_re
            residual[column, rows, :] = value
            residual[column, pl.ds(height + chunk * size, size), :] = value

    shift = shift_ref[0]
    for chunk in range(height // size):
        rows = pl.ds(chunk * size, size)
        for column in range(routing):
            lanes = slice(column * LANES, (column + 1) * LANES)
            routed[rows, lanes] = residual[column, pl.ds(height - shift + chunk * size, size), :]
        send(routed.at[rows], routed_ref.at[rows])
    for copy in sent:
        copy.wait()


def margin_kernel(tile_re, tile_im, out, held, sems):
    height = tile_re.shape[0]
    first, second = [], []
    for n, tile in enumerate((tile_re, tile_im)):
        for part in range(2):
            rows = pl.ds(part * height // 2, height // 2)
            source = tile.at[rows, pl.ds(0, LANES)]
            sem = sems.at[2 * n + part]
            first.append(pltpu.make_async_copy(source, held.at[n, rows], sem))
            second.append(pltpu.make_async_copy(held.at[n, rows], out.at[n, rows], sem))
    for copy in first:
        copy.start()
    for before, after in zip(first, second):
        before.wait()
        after.start()
    for copy in second:
        copy.wait()


def margins(tile_re, tile_im):
    shape = (2, tile_re.shape[0], LANES)
    return pl.pallas_call(
        margin_kernel,
        out_shape=jax.ShapeDtypeStruct(shape, jnp.float32),
        in_specs=[HBM, HBM],
        out_specs=HBM,
        scratch_shapes=[pltpu.VMEM(shape, jnp.float32), pltpu.SemaphoreType.DMA((4,))],
        compiler_params=pltpu.CompilerParams(vmem_limit_bytes=VMEM_BYTES),
        name="margins",
    )(tile_re, tile_im)


def probe_phase(used, positions, shift, tile, edge, begun, probe, intensity):
    height, width = tile[0].shape
    size = probe[0].shape[0]
    slots = intensity.shape[0]
    columns = width // LANES
    beyond = edge is not None
    tables, spread = dft_tables(size)
    plane = pltpu.VMEM((size, size), SPLIT)
    planes = pltpu.VMEM((2, columns, height, LANES), jnp.float32)
    routing = columns if beyond else 1

    def out(*shape):
        return jax.ShapeDtypeStruct(shape, jnp.float32)

    if beyond:
        operands = (*tile, edge, begun)
        early = height * 9 // 16 // SUBLANES * SUBLANES
        late = (height - early) // 2 // SUBLANES * SUBLANES
        spills = [out(2, rows, LANES) for rows in (early, late, height - early - late)]
        outs = (out(2, height, width - LANES), *spills, out(height, width))
        base = LANES
    else:
        operands = tile
        outs = (out(2, height, LANES), out(2, columns - 1, height, LANES), out(height, LANES))
        base = 0
    return pl.pallas_call(
        functools.partial(probe_kernel, base=base, beyond=beyond),
        out_shape=outs,
        in_specs=[SMEM, SMEM, SMEM, *[HBM if x is not edge else ANY for x in operands], *[HBM] * 5],
        out_specs=(HBM,) * len(outs),
        scratch_shapes=[
            planes, planes,
            pltpu.VMEM((slots, 2, size, LANES), jnp.float32),
            pltpu.VMEM((2, size, size), jnp.float32),
            pltpu.VMEM(tables.shape, SPLIT),
            plane,
            pltpu.VMEM((2, 2, 2, size, LANES), jnp.float32),
            pltpu.VMEM((2, 4, size, size), SPLIT),
            pltpu.VMEM((routing, 2 * height, LANES), jnp.float32),
            pltpu.VMEM((height, outs[-1].shape[1]), jnp.float32),
            pltpu.VMEM((2, columns - 1, height, LANES), jnp.float32),
            pltpu.SMEM((slots,), jnp.int32),
            pltpu.SemaphoreType.DMA((2, 2 * columns + 2)),
            pltpu.SemaphoreType.DMA((slots, 2)),
            pltpu.SemaphoreType.DMA((3 * columns + (2 * columns + 1) * (height // size),)),
        ],
        compiler_params=pltpu.CompilerParams(vmem_limit_bytes=VMEM_BYTES * 21 // 20),
        cost_estimate=pl.CostEstimate(
            flops=26 * slots * size**3, bytes_accessed=16 * height * width, transcendentals=0
        ),
        name="probes_beyond" if beyond else "probes_within",
    )(used, positions, shift, *operands, *probe, intensity, jnp.asarray(tables), jnp.asarray(spread))


def shift_tables(slope, depth):
    numer = jnp.arange(depth, dtype=jnp.int32)[None, :] * slope[:, None]
    whole = jnp.floor_divide(numer, depth)
    return whole, (numer - whole * depth).astype(jnp.float32) / depth


class Turned:
    def __init__(self, band, columns, margin):
        self.band = band
        self.segments = LANES // band
        self.length = columns // self.segments
        self.blocks = self.length // LANES
        self.margin = margin
        self.rows = self.length + 2 * margin

    def scratch(self, count):
        return pltpu.VMEM((count, self.rows, LANES), jnp.float32)

    def store(self, ref, lead, at, value):
        rows = value.shape[0]
        ref[lead, pl.ds(self.margin + at, rows), :] = value
        if at < self.margin:
            ref[lead, pl.ds(self.margin + self.length + at, rows), :] = pltpu.roll(
                value, LANES - self.band, axis=1
            )
        if at >= self.length - self.margin:
            ref[lead, pl.ds(at - self.length + self.margin, rows), :] = pltpu.roll(
                value, self.band, axis=1
            )

    def project(self, whole, frac, ref, tilt, at, rows):
        depth = ref.shape[0]

        def add_level(level, totals):
            plain, weighted = totals
            start = self.margin + at - whole[tilt, level] - SUBLANES
            x = ref[level, pl.ds(start, rows + SUBLANES), :]
            return plain + x[SUBLANES:], weighted + frac[tilt, level] * x

        zero = jnp.zeros((rows + SUBLANES, LANES), jnp.float32)
        plain, weighted = lax.fori_loop(
            0, depth, add_level, (zero[SUBLANES:], zero), unroll=16
        )
        return plain - weighted[SUBLANES:] + weighted[SUBLANES - 1 : SUBLANES - 1 + rows]


def old_kernel(turned, whole, frac, volume, old, cells):
    depth = volume.shape[0]

    @pl.loop(0, depth)
    def _(level):
        for block in range(turned.blocks):
            cut = []
            for segment in range(turned.segments):
                start = segment * turned.length + block * LANES
                cut.append(volume[level, :, start : start + LANES])
            turned.store(cells, level, block * LANES, jnp.concatenate(cut, axis=0).T)

    @pl.loop(0, whole.shape[0])
    def _(tilt):
        for block in range(turned.blocks):
            at = block * LANES
            old[tilt, at : at + LANES, :] = turned.project(whole, frac, cells, tilt, at, LANES)


def step_kernel(
    turned, whole, frac, left_from, right_from, old, parts, update,
    near, cells, left, right, before, after, sems, level_sems,
):
    old_copy = pltpu.make_async_copy(old, before, sems.at[0, 0])
    depth = cells.shape[0]
    tilts = near.shape[0]
    tiles = right_from.shape[0] // tilts
    own = right_from.shape[2] // LANES
    band = turned.band

    def fetch(tilt):
        block = pl.ds(tilt * tiles, tiles)
        return [
            pltpu.make_async_copy(source.at[block], target.at[block], sems.at[2 + n, tilt])
            for n, (source, target) in enumerate(((left_from, left), (right_from, right)))
        ]

    for tilt in range(tilts):
        for copy in fetch(tilt):
            copy.start()
    old_copy.start()

    def place(block, segment):
        return divmod(segment * turned.blocks + block, own)

    @pl.loop(0, tilts)
    def _(tilt):
        for copy in fetch(tilt):
            copy.wait()
        for block in range(turned.blocks):
            cut = []
            for segment in range(turned.segments):
                tile, column = place(block, segment)
                source = tilt * tiles + tile
                if column > 0:
                    value = right[source, :, (column - 1) * LANES : column * LANES]
                elif tile > 0:
                    value = left[source] + right[source - 1, :, (own - 1) * LANES :]
                else:
                    value = left[source]
                cut.append(value)
            value = jnp.concatenate(cut, axis=0).T * (1.0 / tilts)
            turned.store(near, tilt, block * LANES, value)

    rows = LANES // 2

    def keep(level):
        main = cells.at[level, pl.ds(turned.margin, turned.length), :]
        return pltpu.make_async_copy(main, update.at[level], level_sems.at[level])

    @pl.loop(0, depth, unroll=2)
    def _(level):
        for at in range(0, turned.length, rows):
            plain = weighted = None
            for tilt in range(tilts):
                start = turned.margin + at + whole[tilt, level]
                x = near[tilt, pl.ds(start, rows + SUBLANES), :]
                y = frac[tilt, level] * x
                plain = x[:rows] if plain is None else plain + x[:rows]
                weighted = y if weighted is None else weighted + y
            value = plain - weighted[:rows] + weighted[1 : 1 + rows]
            turned.store(cells, level, at, value)
        keep(level).start()

    old_copy.wait()

    def send(tilt):
        block = pl.ds(tilt * tiles, tiles)
        return pltpu.make_async_copy(after.at[block], parts.at[block], sems.at[1, tilt])

    @pl.loop(0, tilts)
    def _(tilt):
        for block in range(turned.blocks):
            at = block * LANES
            before[tilt, at : at + LANES, :] += turned.project(whole, frac, cells, tilt, at, LANES)
        for block in range(turned.blocks):
            total = before[tilt, block * LANES : (block + 1) * LANES, :].T
            for segment in range(turned.segments):
                tile, column = place(block, segment)
                after[tilt * tiles + tile, :, column * LANES : (column + 1) * LANES] = total[
                    segment * band : (segment + 1) * band
                ]

        send(tilt).start()

    for tilt in range(tilts):
        send(tilt).wait()
    for level in range(depth):
        keep(level).wait()


def fresh_kernel(turned, volume, update, fresh):
    for level in range(volume.shape[0]):
        for block in range(turned.blocks):
            value = update[level, block * LANES : (block + 1) * LANES, :].T
            for segment in range(turned.segments):
                start = segment * turned.length + block * LANES
                lanes = slice(start, start + LANES)
                rows = slice(segment * turned.band, (segment + 1) * turned.band)
                fresh[level, :, lanes] = volume[level, :, lanes] + value[rows]


def kernel_options(flops, size, share=1):
    return dict(
        compiler_params=pltpu.CompilerParams(vmem_limit_bytes=int(VMEM_BYTES * share)),
        cost_estimate=pl.CostEstimate(flops=flops, bytes_accessed=size, transcendentals=0),
    )


def old_projection(turned, whole, frac, volume):
    tilts = whole.shape[0]
    return pl.pallas_call(
        functools.partial(old_kernel, turned),
        out_shape=jax.ShapeDtypeStruct((tilts, turned.length, LANES), jnp.float32),
        in_specs=[SMEM, SMEM, VMEM],
        out_specs=VMEM,
        scratch_shapes=[turned.scratch(volume.shape[0])],
        name="old_projection",
        **kernel_options(8 * tilts * volume.size, 4 * volume.size),
    )(whole, frac, volume)


def volume_step(turned, whole, frac, left, right, old):
    tilts, depth = whole.shape
    return pl.pallas_call(
        functools.partial(step_kernel, turned),
        out_shape=(
            jax.ShapeDtypeStruct(right.shape, jnp.float32),
            jax.ShapeDtypeStruct((depth, turned.length, LANES), jnp.float32),
        ),
        in_specs=[SMEM, SMEM, ANY, ANY, HBM],
        out_specs=(HBM, HBM),
        scratch_shapes=[
            turned.scratch(tilts), turned.scratch(depth),
            pltpu.VMEM(left.shape, jnp.float32),
            pltpu.VMEM(right.shape, jnp.float32),
            pltpu.VMEM(old.shape, jnp.float32),
            pltpu.VMEM(right.shape, jnp.float32),
            pltpu.SemaphoreType.DMA((4, tilts)),
            pltpu.SemaphoreType.DMA((depth,)),
        ],
        name="volume_step",
        **kernel_options(16 * depth * old.size, 4 * depth * turned.length * LANES, 9 / 10),
    )(whole, frac, left, right, old)


def fresh_volume(turned, volume, update):
    depth, band, columns = volume.shape
    levels = math.gcd(depth, 4)
    cells = pl.BlockSpec((levels, band, columns), lambda i: (i, 0, 0))
    flat = pl.BlockSpec((levels, turned.length, LANES), lambda i: (i, 0, 0))
    return pl.pallas_call(
        functools.partial(fresh_kernel, turned),
        grid=(depth // levels,),
        out_shape=jax.ShapeDtypeStruct(volume.shape, jnp.float32),
        in_specs=[cells, flat],
        out_specs=cells,
        name="fresh_volume",
        **kernel_options(volume.size, 12 * volume.size),
    )(volume, update)


def local(
    obj_re, obj_im, probe_re, probe_im, intensity, positions, counts, row_shift, slope, volume
):
    tile = (obj_re[0], obj_im[0])
    height, width = tile[0].shape
    depth, band, columns = volume.shape
    axes = ("tilt", "tile")
    devices = lax.axis_size("tilt") * lax.axis_size("tile")
    turned = Turned(band, columns, width)
    probe = (probe_re, probe_im)

    within = (counts, jnp.swapaxes(positions, 1, 2), row_shift)

    def exchanged(blocks):
        return lax.all_to_all(blocks, axes, split_axis=0, concat_axis=0, tiled=True)

    edge = passed_along(margins(*tile), "tile", -1)
    grad_left, begun, left = probe_phase(*within, tile, None, None, probe, intensity[0])
    left = exchanged(left.reshape(devices, band, LANES))
    grad_right, early, late, relayed, right = probe_phase(*within, tile, edge, begun, probe, intensity[0])
    right, left, slope = lax.optimization_barrier((right, left, slope))
    whole, frac = shift_tables(slope, depth)
    right = exchanged(right.reshape(devices, band, width))
    old = old_projection(turned, whole, frac, volume)
    right, early, old = lax.optimization_barrier((right, early, old))
    early = passed_along(early, "tile", 1)
    parts, update = volume_step(turned, whole, frac, left, right, old)
    parts, early, late, relayed = lax.optimization_barrier((parts, early, late, relayed))
    late = passed_along(late, "tile", 1)
    straight = passed_by(relayed, "tile", 0, 1)
    relayed = passed_by(relayed, "tile", 1, -1)
    returned = exchanged(parts)
    fresh = fresh_volume(turned, volume, update)
    rows = early.shape[1]
    early = jnp.pad(early, ((0, 0), (0, height - rows), (0, 0)))
    grad = jnp.concatenate([grad_left + early, grad_right], axis=2)[:, None]
    relayed, fresh, grad = lax.optimization_barrier((relayed, fresh, grad))
    relayed = straight + passed_by(relayed, "tile", 0, 2)
    late = jnp.concatenate([late, relayed], axis=1)
    late = (late + grad_left[:, rows:])[:, None]
    grad = lax.dynamic_update_slice(grad, late, (0, 0, rows, 0))
    reprojection = jnp.roll(returned.reshape(height, width), -row_shift[0], axis=0)[None]
    return (fresh, reprojection, grad)


def solution(mesh):
    placed = (
        P("tilt", None, "tile"),
        P("tilt", None, "tile"),
        P(),
        P(),
        P("tilt", "tile", None, None),
        P("tilt", "tile", None),
        P("tilt", "tile"),
        P("tilt"),
        P(),
        P(None, ("tilt", "tile"), None),
    )
    return jax.shard_map(
        local,
        mesh=mesh,
        in_specs=placed,
        out_specs=(
            P(None, ("tilt", "tile"), None),
            P("tilt", None, "tile"),
            P(None, "tilt", None, "tile"),
        ),
        check_vma=False,
    )
```

```python
import functools
import math

import jax
import jax.numpy as jnp
import ml_dtypes
import numpy as np
from jax import lax
from jax.experimental import pallas as pl
from jax.experimental.pallas import tpu as pltpu
from jax.sharding import PartitionSpec as P

LANES = 128
SUBLANES = 8
VMEM_BYTES = 60 * 1024 * 1024
PROBE_SCRATCH = 15
SPLIT = jnp.bfloat16
ANY = pl.BlockSpec(memory_space=pl.ANY)
HBM = pl.BlockSpec(memory_space=pltpu.HBM)
SMEM = pl.BlockSpec(memory_space=pltpu.SMEM)
VMEM = pl.BlockSpec(memory_space=pltpu.VMEM)


def passed_along(block, axis, distance):
    devices = range(lax.axis_size(axis))
    route = [(i - distance, i) for i in devices if i - distance in devices]
    return lax.ppermute(block, axis, route)


def passed_by(block, axis, first, step):
    count = lax.axis_size(axis)
    route = [(i, i + step) for i in range(first, count, 2) if 0 <= i + step < count]
    return lax.ppermute(block, axis, route)


def halves(table):
    high = table.astype(ml_dtypes.bfloat16)
    low = (table - high.astype(np.float64)).astype(ml_dtypes.bfloat16)
    return high, low


def dft_tables(length):
    half = length // 2
    index = np.arange(length)
    angle = (index[:, None] * index[None, :] % length) * (-2.0 * math.pi / length)
    wave = (np.cos(angle) + 1j * np.sin(angle)) / math.sqrt(length)
    tables = []
    for parity in (0, 1):
        part = wave[parity::2, :half]
        pair = np.block([[part.real, -part.imag], [part.imag, part.real]])
        tables += [*halves(pair), *halves(pair.T)]
    order = np.concatenate([index[0::2], index[1::2]])
    spread = np.zeros((length, length))
    spread[order, index] = 1.0
    return np.stack(tables), spread.astype(ml_dtypes.bfloat16)


def split(x):
    high = x.astype(SPLIT)
    return high, (x - high.astype(jnp.float32)).astype(SPLIT)


def dot(a, b):
    return jnp.dot(a, b, preferred_element_type=jnp.float32)


def dot3(ah, al, bh, bl):
    return dot(ah, bh) + dot(ah, bl) + dot(al, bh)


def lanes_of(shape):
    return lax.broadcasted_iota(jnp.int32, shape, len(shape) - 1)


def rows_of(shape):
    return lax.broadcasted_iota(jnp.int32, shape, len(shape) - 2)


def rolled(x, row, lane):
    size = x.shape[0]
    tiles = x.shape[1] // LANES
    cut = []
    for tile in range(tiles):
        part = x[:, tile * LANES : (tile + 1) * LANES].reshape(-1, SUBLANES, LANES)
        turned = pltpu.roll(part, row, axis=1)
        before = jnp.concatenate([turned[-1:], turned[:-1]], axis=0)
        part = jnp.where(rows_of(part.shape) < row, before, turned).reshape(size, LANES)
        cut.append(pltpu.roll(part, lane, axis=1))
    keep = lanes_of(cut[0].shape) >= lane
    return [jnp.where(keep, cut[tile], cut[tile - 1]) for tile in range(tiles)]


def probe_kernel(
    used_ref, positions_ref, shift_ref,
    *refs, base, beyond,
):
    if beyond:
        (tile_re, tile_im, edge, begun, probe_re, probe_im, intensity, tables_from, spread_from,
         grad_ref, *spill_refs, routed_ref) = refs[: len(refs) - PROBE_SCRATCH]
    else:
        (tile_re, tile_im, probe_re, probe_im, intensity, tables_from, spread_from,
         grad_ref, begun_ref, routed_ref) = refs[: len(refs) - PROBE_SCRATCH]
    (ext, acc, measured, probes, tables, spread, turned, planes, residual, routed,
     prior, listed, sems, slot_sems, out_sems) = refs[len(refs) - PROBE_SCRATCH :]
    height = ext.shape[2]
    tiles = ext.shape[1]
    size = probes.shape[1]
    half = size // 2
    used = used_ref[0, 0]
    copies = [
        pltpu.make_async_copy(probe_re, probes.at[0], sems.at[0, 2 * tiles]),
        pltpu.make_async_copy(probe_im, probes.at[1], sems.at[0, 2 * tiles + 1]),
        pltpu.make_async_copy(tables_from, tables, sems.at[1, 0]),
        pltpu.make_async_copy(spread_from, spread, sems.at[1, 1]),
    ]
    for part, tile in enumerate((tile_re, tile_im)):
        for column in range(tiles):
            if beyond and column == tiles - 1:
                source = edge.at[part]
            else:
                source = tile.at[:, pl.ds(base + column * LANES, LANES)]
            sem = sems.at[0, part * tiles + column]
            copies.append(pltpu.make_async_copy(source, ext.at[part, column], sem))
    for copy in copies:
        copy.start()

    def fetch(slot):
        return [
            pltpu.make_async_copy(
                intensity.at[slot, :, pl.ds(tile * LANES, LANES)],
                measured.at[slot, tile],
                slot_sems.at[slot, tile],
            )
            for tile in range(2)
        ]

    def mine(slot):
        past = positions_ref[0, 1, slot] + size > base + tiles * LANES
        return past if not beyond else positions_ref[0, 1, slot] + size > base + (tiles - 1) * LANES

    def live(slot):
        return mine(slot) if beyond else jnp.logical_not(mine(slot))

    slots = measured.shape[0]
    for slot in range(slots):
        @pl.when(jnp.logical_and(slot < used, live(slot)))
        def _():
            for copy in fetch(slot):
                copy.start()

    @pl.loop(0, height // size)
    def _(chunk):
        rows = pl.ds(chunk * size, size)
        for part in range(2):
            for column in range(tiles):
                acc[part, column, rows, :] = jnp.zeros((size, LANES), jnp.float32)

    for copy in copies:
        copy.wait()
    if beyond:
        earlier = pltpu.make_async_copy(begun, prior, sems.at[1, 2])
        earlier.start()

    le, let, lo, lot = 0, 2, 4, 6

    def table(which):
        return tables[which], tables[which + 1]

    def visit(slot, turned, uh, ul, vh, vl):
        row = positions_ref[0, 0, slot]
        col = positions_ref[0, 1, slot] - base
        first = pl.multiple_of(row // SUBLANES * SUBLANES, SUBLANES)
        row_rest = row - first
        wrap = pl.multiple_of(jnp.minimum(first + size, height - SUBLANES), SUBLANES)
        column = col // LANES
        lane_rest = col - column * LANES
        wrap_column = jnp.minimum(column + 2, tiles - 1)
        body = pl.ds(first, size)
        tail = pl.ds(wrap, SUBLANES)
        low_rows = rows_of((SUBLANES, LANES)) < row_rest
        low_lanes = lanes_of((size, LANES)) < lane_rest

        for part in range(2):
            for tile, piece in enumerate(rolled(probes[part], row_rest, lane_rest)):
                turned[part, tile] = piece

        def window(part, at):
            block = ext[part, at, body, :]
            top = jnp.where(low_rows, ext[part, at, tail, :], block[:SUBLANES])
            return jnp.concatenate([top, block[SUBLANES:]], axis=0)

        psi = []
        for tile in range(2):
            if tile == 0:
                o_re, o_im = (
                    jnp.where(low_lanes, window(part, wrap_column), window(part, column))
                    for part in range(2)
                )
            else:
                o_re, o_im = (window(part, column + 1) for part in range(2))
            p_re, p_im = turned[0, tile], turned[1, tile]
            psi.append((p_re * o_re - p_im * o_im, p_re * o_im + p_im * o_re))
        for part in range(2):
            lanes = slice(part * LANES, (part + 1) * LANES)
            uh[:, lanes], ul[:, lanes] = split(psi[0][part] + psi[1][part])
            vh[:, lanes], vl[:, lanes] = split(psi[0][part] - psi[1][part])
        yield
        even = dot3(uh[...], ul[...], *table(let))
        odd = dot3(vh[...], vl[...], *table(lot))
        for part in range(2):
            rows = slice(part * half, (part + 1) * half)
            for tile, y in enumerate((even, odd)):
                lanes = slice(tile * LANES, (tile + 1) * LANES)
                y = y[:, part * LANES : (part + 1) * LANES]
                uh[rows, lanes], ul[rows, lanes] = split(y[:half] + y[half:])
                vh[rows, lanes], vl[rows, lanes] = split(y[:half] - y[half:])
        yield
        for copy in fetch(slot):
            copy.wait()
        for parity, (h, l, which) in enumerate(((uh, ul, le), (vh, vl, lo))):
            th, tl = table(which)
            far = dot(th, h[...]) + dot(tl, h[...]) + dot(th, l[...])
            f_re, f_im = far[:half], far[half:]
            m = [measured[slot, tile, pl.ds(parity, half, stride=2), :] for tile in range(2)]
            mh, ml = split(jnp.concatenate(m, axis=1))
            excess = f_re * f_re + f_im * f_im - (dot(mh, spread[...]) + dot(ml, spread[...]))
            h[:half, :], l[:half, :] = split(excess * f_re)
            h[half:, :], l[half:, :] = split(excess * f_im)
        yield
        th, tl = table(let)
        even = dot(th, uh[...]) + dot(tl, uh[...]) + dot(th, ul[...])
        th, tl = table(lot)
        odd = dot(th, vh[...]) + dot(tl, vh[...]) + dot(th, vl[...])
        for part in range(2):
            rows = slice(part * half, (part + 1) * half)
            lanes = slice(part * LANES, (part + 1) * LANES)
            for sign in range(2):
                out = slice(sign * half, (sign + 1) * half)
                t = even[rows] + odd[rows] if sign == 0 else even[rows] - odd[rows]
                uh[out, lanes], ul[out, lanes] = split(t[:, :LANES])
                vh[out, lanes], vl[out, lanes] = split(t[:, LANES:])
        yield
        even = dot3(uh[...], ul[...], *table(le))
        odd = dot3(vh[...], vl[...], *table(lo))
        for tile in range(2):
            chi = even + odd if tile == 0 else even - odd
            c_re, c_im = chi[:, :LANES], chi[:, LANES:]
            p_re, p_im = turned[0, tile], turned[1, tile]
            for part, g in enumerate((p_re * c_re + p_im * c_im, p_re * c_im - p_im * c_re)):
                if tile == 0:
                    places = (
                        (column, jnp.where(low_lanes, 0.0, g)),
                        (wrap_column, jnp.where(low_lanes, g, 0.0)),
                    )
                else:
                    places = ((column + 1, g),)
                for at, value in places:
                    top = value[:SUBLANES]
                    kept = jnp.where(low_rows, 0.0, top)
                    acc[part, at, body, :] += jnp.concatenate([kept, value[SUBLANES:]], axis=0)
                    acc[part, at, tail, :] += jnp.where(low_rows, top, 0.0)
        yield

    def buffers(which):
        return (turned.at[which], *(planes.at[which, n] for n in range(4)))

    def together(*slots):
        for _ in zip(*(visit(slot, *buffers(which)) for which, slot in enumerate(slots))):
            pass

    def enlist(slot, count):
        @pl.when(live(slot))
        def _():
            listed[count] = slot

        return count + live(slot).astype(jnp.int32)

    count = lax.fori_loop(0, used, enlist, 0)

    @pl.loop(0, count // 2)
    def _(pair):
        together(listed[2 * pair], listed[2 * pair + 1])

    @pl.when(count % 2 == 1)
    def _():
        together(listed[count - 1])

    sent = []

    def send(source, target):
        sent.append(pltpu.make_async_copy(source, target, out_sems.at[len(sent)]))
        sent[-1].start()

    last = tiles - 1
    for part in range(2):
        if beyond:
            first_row = 0
            for spill_ref in spill_refs:
                rows = pl.ds(first_row, spill_ref.shape[1])
                send(acc.at[part, last, rows], spill_ref.at[part])
                first_row += spill_ref.shape[1]
        else:
            send(acc.at[part, 0], grad_ref.at[part])
            for column in range(1, tiles):
                send(acc.at[part, column], begun_ref.at[part, column - 1])
    if beyond:
        earlier.wait()
    routing = tiles if beyond else 1

    for chunk in range(height // size):
        rows = pl.ds(chunk * size, size)
        for column in range(routing):
            g_re, g_im = acc[0, column, rows, :], acc[1, column, rows, :]
            if beyond and column < last:
                g_re = g_re + prior[0, column, rows, :]
                g_im = g_im + prior[1, column, rows, :]
                lanes = pl.ds(column * LANES, LANES)
                for part, g in enumerate((g_re, g_im)):
                    acc[part, column, rows, :] = g
                    send(acc.at[part, column, rows], grad_ref.at[part, rows, lanes])
            value = ext[0, column, rows, :] * g_im - ext[1, column, rows, :] * g_re
            residual[column, rows, :] = value
            residual[column, pl.ds(height + chunk * size, size), :] = value

    shift = shift_ref[0]
    for chunk in range(height // size):
        rows = pl.ds(chunk * size, size)
        for column in range(routing):
            lanes = slice(column * LANES, (column + 1) * LANES)
            routed[rows, lanes] = residual[column, pl.ds(height - shift + chunk * size, size), :]
        send(routed.at[rows], routed_ref.at[rows])
    for copy in sent:
        copy.wait()


def margin_kernel(tile_re, tile_im, out, held, sems):
    height = tile_re.shape[0]
    first, second = [], []
    for n, tile in enumerate((tile_re, tile_im)):
        for part in range(2):
            rows = pl.ds(part * height // 2, height // 2)
            source = tile.at[rows, pl.ds(0, LANES)]
            sem = sems.at[2 * n + part]
            first.append(pltpu.make_async_copy(source, held.at[n, rows], sem))
            second.append(pltpu.make_async_copy(held.at[n, rows], out.at[n, rows], sem))
    for copy in first:
        copy.start()
    for before, after in zip(first, second):
        before.wait()
        after.start()
    for copy in second:
        copy.wait()


def margins(tile_re, tile_im):
    shape = (2, tile_re.shape[0], LANES)
    return pl.pallas_call(
        margin_kernel,
        out_shape=jax.ShapeDtypeStruct(shape, jnp.float32),
        in_specs=[HBM, HBM],
        out_specs=HBM,
        scratch_shapes=[pltpu.VMEM(shape, jnp.float32), pltpu.SemaphoreType.DMA((4,))],
        compiler_params=pltpu.CompilerParams(vmem_limit_bytes=VMEM_BYTES),
        name="margins",
    )(tile_re, tile_im)


def probe_phase(used, positions, shift, tile, edge, begun, probe, intensity):
    height, width = tile[0].shape
    size = probe[0].shape[0]
    slots = intensity.shape[0]
    columns = width // LANES
    beyond = edge is not None
    tables, spread = dft_tables(size)
    plane = pltpu.VMEM((size, size), SPLIT)
    planes = pltpu.VMEM((2, columns, height, LANES), jnp.float32)
    routing = columns if beyond else 1

    def out(*shape):
        return jax.ShapeDtypeStruct(shape, jnp.float32)

    if beyond:
        operands = (*tile, edge, begun)
        early = height * 9 // 16 // SUBLANES * SUBLANES
        spills = [out(2, rows, LANES) for rows in (early, height - early)]
        outs = (out(2, height, width - LANES), *spills, out(height, width))
        base = LANES
    else:
        operands = tile
        outs = (out(2, height, LANES), out(2, columns - 1, height, LANES), out(height, LANES))
        base = 0
    return pl.pallas_call(
        functools.partial(probe_kernel, base=base, beyond=beyond),
        out_shape=outs,
        in_specs=[SMEM, SMEM, SMEM, *[HBM if x is not edge else ANY for x in operands], *[HBM] * 5],
        out_specs=(HBM,) * len(outs),
        scratch_shapes=[
            planes, planes,
            pltpu.VMEM((slots, 2, size, LANES), jnp.float32),
            pltpu.VMEM((2, size, size), jnp.float32),
            pltpu.VMEM(tables.shape, SPLIT),
            plane,
            pltpu.VMEM((2, 2, 2, size, LANES), jnp.float32),
            pltpu.VMEM((2, 4, size, size), SPLIT),
            pltpu.VMEM((routing, 2 * height, LANES), jnp.float32),
            pltpu.VMEM((height, outs[-1].shape[1]), jnp.float32),
            pltpu.VMEM((2, columns - 1, height, LANES), jnp.float32),
            pltpu.SMEM((slots,), jnp.int32),
            pltpu.SemaphoreType.DMA((2, 2 * columns + 2)),
            pltpu.SemaphoreType.DMA((slots, 2)),
            pltpu.SemaphoreType.DMA((3 * columns + (2 * columns + 1) * (height // size),)),
        ],
        compiler_params=pltpu.CompilerParams(vmem_limit_bytes=VMEM_BYTES * 21 // 20),
        cost_estimate=pl.CostEstimate(
            flops=26 * slots * size**3, bytes_accessed=16 * height * width, transcendentals=0
        ),
        name="probes_beyond" if beyond else "probes_within",
    )(used, positions, shift, *operands, *probe, intensity, jnp.asarray(tables), jnp.asarray(spread))


def shift_tables(slope, depth):
    numer = jnp.arange(depth, dtype=jnp.int32)[None, :] * slope[:, None]
    whole = jnp.floor_divide(numer, depth)
    return whole, (numer - whole * depth).astype(jnp.float32) / depth


class Turned:
    def __init__(self, band, columns, margin):
        self.band = band
        self.segments = LANES // band
        self.length = columns // self.segments
        self.blocks = self.length // LANES
        self.margin = margin
        self.rows = self.length + 2 * margin

    def scratch(self, count):
        return pltpu.VMEM((count, self.rows, LANES), jnp.float32)

    def store(self, ref, lead, at, value):
        rows = value.shape[0]
        ref[lead, pl.ds(self.margin + at, rows), :] = value
        if at < self.margin:
            ref[lead, pl.ds(self.margin + self.length + at, rows), :] = pltpu.roll(
                value, LANES - self.band, axis=1
            )
        if at >= self.length - self.margin:
            ref[lead, pl.ds(at - self.length + self.margin, rows), :] = pltpu.roll(
                value, self.band, axis=1
            )

    def project(self, whole, frac, ref, tilt, at, rows):
        depth = ref.shape[0]

        def add_level(level, totals):
            plain, weighted = totals
            start = self.margin + at - whole[tilt, level] - SUBLANES
            x = ref[level, pl.ds(start, rows + SUBLANES), :]
            return plain + x[SUBLANES:], weighted + frac[tilt, level] * x

        zero = jnp.zeros((rows + SUBLANES, LANES), jnp.float32)
        plain, weighted = lax.fori_loop(
            0, depth, add_level, (zero[SUBLANES:], zero), unroll=16
        )
        return plain - weighted[SUBLANES:] + weighted[SUBLANES - 1 : SUBLANES - 1 + rows]


def old_kernel(turned, whole, frac, volume, old, cells):
    depth = volume.shape[0]

    @pl.loop(0, depth)
    def _(level):
        for block in range(turned.blocks):
            cut = []
            for segment in range(turned.segments):
                start = segment * turned.length + block * LANES
                cut.append(volume[level, :, start : start + LANES])
            turned.store(cells, level, block * LANES, jnp.concatenate(cut, axis=0).T)

    @pl.loop(0, whole.shape[0])
    def _(tilt):
        for block in range(turned.blocks):
            at = block * LANES
            old[tilt, at : at + LANES, :] = turned.project(whole, frac, cells, tilt, at, LANES)


def step_kernel(
    turned, whole, frac, left, right, old, parts, update,
    near, cells, before, after, sems, level_sems,
):
    old_copy = pltpu.make_async_copy(old, before, sems.at[0, 0])
    depth = cells.shape[0]
    tilts = near.shape[0]
    tiles = right.shape[0] // tilts
    own = right.shape[2] // LANES
    band = turned.band

    old_copy.start()

    def place(block, segment):
        return divmod(segment * turned.blocks + block, own)

    @pl.loop(0, tilts)
    def _(tilt):
        for block in range(turned.blocks):
            cut = []
            for segment in range(turned.segments):
                tile, column = place(block, segment)
                source = tilt * tiles + tile
                if column > 0:
                    value = right[source, :, (column - 1) * LANES : column * LANES]
                elif tile > 0:
                    value = left[source] + right[source - 1, :, (own - 1) * LANES :]
                else:
                    value = left[source]
                cut.append(value)
            value = jnp.concatenate(cut, axis=0).T * (1.0 / tilts)
            turned.store(near, tilt, block * LANES, value)

    rows = LANES // 2

    def keep(level):
        main = cells.at[level, pl.ds(turned.margin, turned.length), :]
        return pltpu.make_async_copy(main, update.at[level], level_sems.at[level])

    @pl.loop(0, depth, unroll=2)
    def _(level):
        for at in range(0, turned.length, rows):
            plain = weighted = None
            for tilt in range(tilts):
                start = turned.margin + at + whole[tilt, level]
                x = near[tilt, pl.ds(start, rows + SUBLANES), :]
                y = frac[tilt, level] * x
                plain = x[:rows] if plain is None else plain + x[:rows]
                weighted = y if weighted is None else weighted + y
            value = plain - weighted[:rows] + weighted[1 : 1 + rows]
            turned.store(cells, level, at, value)
        keep(level).start()

    old_copy.wait()

    def send(tilt):
        block = pl.ds(tilt * tiles, tiles)
        return pltpu.make_async_copy(after.at[block], parts.at[block], sems.at[1, tilt])

    @pl.loop(0, tilts)
    def _(tilt):
        for block in range(turned.blocks):
            at = block * LANES
            before[tilt, at : at + LANES, :] += turned.project(whole, frac, cells, tilt, at, LANES)
        for block in range(turned.blocks):
            total = before[tilt, block * LANES : (block + 1) * LANES, :].T
            for segment in range(turned.segments):
                tile, column = place(block, segment)
                after[tilt * tiles + tile, :, column * LANES : (column + 1) * LANES] = total[
                    segment * band : (segment + 1) * band
                ]

        send(tilt).start()

    for tilt in range(tilts):
        send(tilt).wait()
    for level in range(depth):
        keep(level).wait()


def fresh_kernel(turned, volume, update, fresh):
    for level in range(volume.shape[0]):
        for block in range(turned.blocks):
            value = update[level, block * LANES : (block + 1) * LANES, :].T
            for segment in range(turned.segments):
                start = segment * turned.length + block * LANES
                lanes = slice(start, start + LANES)
                rows = slice(segment * turned.band, (segment + 1) * turned.band)
                fresh[level, :, lanes] = volume[level, :, lanes] + value[rows]


def kernel_options(flops, size, share=1):
    return dict(
        compiler_params=pltpu.CompilerParams(vmem_limit_bytes=int(VMEM_BYTES * share)),
        cost_estimate=pl.CostEstimate(flops=flops, bytes_accessed=size, transcendentals=0),
    )


def old_projection(turned, whole, frac, volume):
    tilts = whole.shape[0]
    return pl.pallas_call(
        functools.partial(old_kernel, turned),
        out_shape=jax.ShapeDtypeStruct((tilts, turned.length, LANES), jnp.float32),
        in_specs=[SMEM, SMEM, VMEM],
        out_specs=VMEM,
        scratch_shapes=[turned.scratch(volume.shape[0])],
        name="old_projection",
        **kernel_options(8 * tilts * volume.size, 4 * volume.size),
    )(whole, frac, volume)


def volume_step(turned, whole, frac, left, right, old):
    tilts, depth = whole.shape
    return pl.pallas_call(
        functools.partial(step_kernel, turned),
        out_shape=(
            jax.ShapeDtypeStruct(right.shape, jnp.float32),
            jax.ShapeDtypeStruct((depth, turned.length, LANES), jnp.float32),
        ),
        in_specs=[SMEM, SMEM, VMEM, VMEM, HBM],
        out_specs=(HBM, HBM),
        scratch_shapes=[
            turned.scratch(tilts), turned.scratch(depth),
            pltpu.VMEM(old.shape, jnp.float32),
            pltpu.VMEM(right.shape, jnp.float32),
            pltpu.SemaphoreType.DMA((2, tilts)),
            pltpu.SemaphoreType.DMA((depth,)),
        ],
        name="volume_step",
        **kernel_options(16 * depth * old.size, 4 * depth * turned.length * LANES, 1),
    )(whole, frac, left, right, old)


def fresh_volume(turned, volume, update):
    depth, band, columns = volume.shape
    levels = math.gcd(depth, 4)
    cells = pl.BlockSpec((levels, band, columns), lambda i: (i, 0, 0))
    flat = pl.BlockSpec((levels, turned.length, LANES), lambda i: (i, 0, 0))
    return pl.pallas_call(
        functools.partial(fresh_kernel, turned),
        grid=(depth // levels,),
        out_shape=jax.ShapeDtypeStruct(volume.shape, jnp.float32),
        in_specs=[cells, flat],
        out_specs=cells,
        name="fresh_volume",
        **kernel_options(volume.size, 12 * volume.size),
    )(volume, update)


def local(
    obj_re, obj_im, probe_re, probe_im, intensity, positions, counts, row_shift, slope, volume
):
    tile = (obj_re[0], obj_im[0])
    height, width = tile[0].shape
    depth, band, columns = volume.shape
    axes = ("tilt", "tile")
    devices = lax.axis_size("tilt") * lax.axis_size("tile")
    turned = Turned(band, columns, width)
    probe = (probe_re, probe_im)

    within = (counts, jnp.swapaxes(positions, 1, 2), row_shift)

    def exchanged(blocks):
        return lax.all_to_all(blocks, axes, split_axis=0, concat_axis=0, tiled=True)

    edge = passed_along(margins(*tile), "tile", -1)
    grad_left, begun, left = probe_phase(*within, tile, None, None, probe, intensity[0])
    left = exchanged(left.reshape(devices, band, LANES))
    grad_right, early, late, right = probe_phase(*within, tile, edge, begun, probe, intensity[0])
    right, left, slope = lax.optimization_barrier((right, left, slope))
    whole, frac = shift_tables(slope, depth)
    right = exchanged(right.reshape(devices, band, width))
    old = old_projection(turned, whole, frac, volume)
    straight = passed_by(late, "tile", 0, 1)
    back = passed_by(late, "tile", 1, -1)
    right, early, old, straight, back = lax.optimization_barrier(
        (right, early, old, straight, back)
    )
    early = passed_along(early, "tile", 1)
    relayed = passed_by(back, "tile", 0, 2)
    parts, update = volume_step(turned, whole, frac, left, right, old)
    parts, early, relayed = lax.optimization_barrier((parts, early, relayed))
    returned = exchanged(parts)
    fresh = fresh_volume(turned, volume, update)
    spill = jnp.concatenate([early, straight + relayed], axis=1)
    grad = jnp.concatenate([grad_left + spill, grad_right], axis=2)[:, None]
    reprojection = jnp.roll(returned.reshape(height, width), -row_shift[0], axis=0)[None]
    return (fresh, reprojection, grad)


def solution(mesh):
    placed = (
        P("tilt", None, "tile"),
        P("tilt", None, "tile"),
        P(),
        P(),
        P("tilt", "tile", None, None),
        P("tilt", "tile", None),
        P("tilt", "tile"),
        P("tilt"),
        P(),
        P(None, ("tilt", "tile"), None),
    )
    return jax.shard_map(
        local,
        mesh=mesh,
        in_specs=placed,
        out_specs=(
            P(None, ("tilt", "tile"), None),
            P("tilt", None, "tile"),
            P(None, "tilt", None, "tile"),
        ),
        check_vma=False,
    )
```

```python
import functools
import math

import jax
import jax.numpy as jnp
import ml_dtypes
import numpy as np
from jax import lax
from jax.experimental import pallas as pl
from jax.experimental.pallas import tpu as pltpu
from jax.sharding import PartitionSpec as P

LANES = 128
SUBLANES = 8
VMEM_BYTES = 60 * 1024 * 1024
PROBE_SCRATCH = 15
SPLIT = jnp.bfloat16
ANY = pl.BlockSpec(memory_space=pl.ANY)
HBM = pl.BlockSpec(memory_space=pltpu.HBM)
SMEM = pl.BlockSpec(memory_space=pltpu.SMEM)
VMEM = pl.BlockSpec(memory_space=pltpu.VMEM)


def passed_along(block, axis, distance):
    devices = range(lax.axis_size(axis))
    route = [(i - distance, i) for i in devices if i - distance in devices]
    return lax.ppermute(block, axis, route)


def passed_by(block, axis, first, step):
    count = lax.axis_size(axis)
    route = [(i, i + step) for i in range(first, count, 2) if 0 <= i + step < count]
    return lax.ppermute(block, axis, route)


def halves(table):
    high = table.astype(ml_dtypes.bfloat16)
    low = (table - high.astype(np.float64)).astype(ml_dtypes.bfloat16)
    return high, low


def dft_tables(length):
    half = length // 2
    index = np.arange(length)
    angle = (index[:, None] * index[None, :] % length) * (-2.0 * math.pi / length)
    wave = (np.cos(angle) + 1j * np.sin(angle)) / math.sqrt(length)
    tables = []
    for parity in (0, 1):
        part = wave[parity::2, :half]
        pair = np.block([[part.real, -part.imag], [part.imag, part.real]])
        tables += [*halves(pair), *halves(pair.T)]
    order = np.concatenate([index[0::2], index[1::2]])
    spread = np.zeros((length, length))
    spread[order, index] = 1.0
    return np.stack(tables), spread.astype(ml_dtypes.bfloat16)


def split(x):
    high = x.astype(SPLIT)
    return high, (x - high.astype(jnp.float32)).astype(SPLIT)


def dot(a, b):
    return jnp.dot(a, b, preferred_element_type=jnp.float32)


def dot3(ah, al, bh, bl):
    return dot(ah, bh) + dot(ah, bl) + dot(al, bh)


def lanes_of(shape):
    return lax.broadcasted_iota(jnp.int32, shape, len(shape) - 1)


def rows_of(shape):
    return lax.broadcasted_iota(jnp.int32, shape, len(shape) - 2)


def rolled(x, row, lane):
    size = x.shape[0]
    tiles = x.shape[1] // LANES
    cut = []
    for tile in range(tiles):
        part = x[:, tile * LANES : (tile + 1) * LANES].reshape(-1, SUBLANES, LANES)
        turned = pltpu.roll(part, row, axis=1)
        before = jnp.concatenate([turned[-1:], turned[:-1]], axis=0)
        part = jnp.where(rows_of(part.shape) < row, before, turned).reshape(size, LANES)
        cut.append(pltpu.roll(part, lane, axis=1))
    keep = lanes_of(cut[0].shape) >= lane
    return [jnp.where(keep, cut[tile], cut[tile - 1]) for tile in range(tiles)]


def probe_kernel(
    used_ref, positions_ref, shift_ref,
    *refs, base, beyond,
):
    if beyond:
        (tile_re, tile_im, edge, begun, probe_re, probe_im, intensity, tables_from, spread_from,
         grad_ref, *spill_refs, routed_ref) = refs[: len(refs) - PROBE_SCRATCH]
    else:
        (tile_re, tile_im, probe_re, probe_im, intensity, tables_from, spread_from,
         grad_ref, begun_ref, routed_ref) = refs[: len(refs) - PROBE_SCRATCH]
    (ext, acc, measured, probes, tables, spread, turned, planes, residual, routed,
     prior, listed, sems, slot_sems, out_sems) = refs[len(refs) - PROBE_SCRATCH :]
    height = ext.shape[2]
    tiles = ext.shape[1]
    size = probes.shape[1]
    half = size // 2
    used = used_ref[0, 0]
    copies = [
        pltpu.make_async_copy(probe_re, probes.at[0], sems.at[0, 2 * tiles]),
        pltpu.make_async_copy(probe_im, probes.at[1], sems.at[0, 2 * tiles + 1]),
        pltpu.make_async_copy(tables_from, tables, sems.at[1, 0]),
        pltpu.make_async_copy(spread_from, spread, sems.at[1, 1]),
    ]
    for part, tile in enumerate((tile_re, tile_im)):
        for column in range(tiles):
            if beyond and column == tiles - 1:
                source = edge.at[part]
            else:
                source = tile.at[:, pl.ds(base + column * LANES, LANES)]
            sem = sems.at[0, part * tiles + column]
            copies.append(pltpu.make_async_copy(source, ext.at[part, column], sem))
    for copy in copies:
        copy.start()

    def fetch(slot):
        return [
            pltpu.make_async_copy(
                intensity.at[slot, :, pl.ds(tile * LANES, LANES)],
                measured.at[slot, tile],
                slot_sems.at[slot, tile],
            )
            for tile in range(2)
        ]

    def mine(slot):
        past = positions_ref[0, 1, slot] + size > base + tiles * LANES
        return past if not beyond else positions_ref[0, 1, slot] + size > base + (tiles - 1) * LANES

    def live(slot):
        return mine(slot) if beyond else jnp.logical_not(mine(slot))

    slots = measured.shape[0]
    for slot in range(slots):
        @pl.when(jnp.logical_and(slot < used, live(slot)))
        def _():
            for copy in fetch(slot):
                copy.start()

    @pl.loop(0, height // size)
    def _(chunk):
        rows = pl.ds(chunk * size, size)
        for part in range(2):
            for column in range(tiles):
                acc[part, column, rows, :] = jnp.zeros((size, LANES), jnp.float32)

    for copy in copies:
        copy.wait()
    if beyond:
        earlier = pltpu.make_async_copy(begun, prior, sems.at[1, 2])
        earlier.start()

    le, let, lo, lot = 0, 2, 4, 6

    def table(which):
        return tables[which], tables[which + 1]

    def visit(slot, turned, uh, ul, vh, vl):
        row = positions_ref[0, 0, slot]
        col = positions_ref[0, 1, slot] - base
        first = pl.multiple_of(row // SUBLANES * SUBLANES, SUBLANES)
        row_rest = row - first
        wrap = pl.multiple_of(jnp.minimum(first + size, height - SUBLANES), SUBLANES)
        column = col // LANES
        lane_rest = col - column * LANES
        wrap_column = jnp.minimum(column + 2, tiles - 1)
        body = pl.ds(first, size)
        tail = pl.ds(wrap, SUBLANES)
        low_rows = rows_of((SUBLANES, LANES)) < row_rest
        low_lanes = lanes_of((size, LANES)) < lane_rest

        for part in range(2):
            for tile, piece in enumerate(rolled(probes[part], row_rest, lane_rest)):
                turned[part, tile] = piece

        def window(part, at):
            block = ext[part, at, body, :]
            top = jnp.where(low_rows, ext[part, at, tail, :], block[:SUBLANES])
            return jnp.concatenate([top, block[SUBLANES:]], axis=0)

        psi = []
        for tile in range(2):
            if tile == 0:
                o_re, o_im = (
                    jnp.where(low_lanes, window(part, wrap_column), window(part, column))
                    for part in range(2)
                )
            else:
                o_re, o_im = (window(part, column + 1) for part in range(2))
            p_re, p_im = turned[0, tile], turned[1, tile]
            psi.append((p_re * o_re - p_im * o_im, p_re * o_im + p_im * o_re))
        for part in range(2):
            lanes = slice(part * LANES, (part + 1) * LANES)
            uh[:, lanes], ul[:, lanes] = split(psi[0][part] + psi[1][part])
            vh[:, lanes], vl[:, lanes] = split(psi[0][part] - psi[1][part])
        yield
        even = dot3(uh[...], ul[...], *table(let))
        odd = dot3(vh[...], vl[...], *table(lot))
        for part in range(2):
            rows = slice(part * half, (part + 1) * half)
            for tile, y in enumerate((even, odd)):
                lanes = slice(tile * LANES, (tile + 1) * LANES)
                y = y[:, part * LANES : (part + 1) * LANES]
                uh[rows, lanes], ul[rows, lanes] = split(y[:half] + y[half:])
                vh[rows, lanes], vl[rows, lanes] = split(y[:half] - y[half:])
        yield
        for copy in fetch(slot):
            copy.wait()
        for parity, (h, l, which) in enumerate(((uh, ul, le), (vh, vl, lo))):
            th, tl = table(which)
            far = dot(th, h[...]) + dot(tl, h[...]) + dot(th, l[...])
            f_re, f_im = far[:half], far[half:]
            m = [measured[slot, tile, pl.ds(parity, half, stride=2), :] for tile in range(2)]
            mh, ml = split(jnp.concatenate(m, axis=1))
            excess = f_re * f_re + f_im * f_im - (dot(mh, spread[...]) + dot(ml, spread[...]))
            h[:half, :], l[:half, :] = split(excess * f_re)
            h[half:, :], l[half:, :] = split(excess * f_im)
        yield
        th, tl = table(let)
        even = dot(th, uh[...]) + dot(tl, uh[...]) + dot(th, ul[...])
        th, tl = table(lot)
        odd = dot(th, vh[...]) + dot(tl, vh[...]) + dot(th, vl[...])
        for part in range(2):
            rows = slice(part * half, (part + 1) * half)
            lanes = slice(part * LANES, (part + 1) * LANES)
            for sign in range(2):
                out = slice(sign * half, (sign + 1) * half)
                t = even[rows] + odd[rows] if sign == 0 else even[rows] - odd[rows]
                uh[out, lanes], ul[out, lanes] = split(t[:, :LANES])
                vh[out, lanes], vl[out, lanes] = split(t[:, LANES:])
        yield
        even = dot3(uh[...], ul[...], *table(le))
        odd = dot3(vh[...], vl[...], *table(lo))
        for tile in range(2):
            chi = even + odd if tile == 0 else even - odd
            c_re, c_im = chi[:, :LANES], chi[:, LANES:]
            p_re, p_im = turned[0, tile], turned[1, tile]
            for part, g in enumerate((p_re * c_re + p_im * c_im, p_re * c_im - p_im * c_re)):
                if tile == 0:
                    places = (
                        (column, jnp.where(low_lanes, 0.0, g)),
                        (wrap_column, jnp.where(low_lanes, g, 0.0)),
                    )
                else:
                    places = ((column + 1, g),)
                for at, value in places:
                    top = value[:SUBLANES]
                    kept = jnp.where(low_rows, 0.0, top)
                    acc[part, at, body, :] += jnp.concatenate([kept, value[SUBLANES:]], axis=0)
                    acc[part, at, tail, :] += jnp.where(low_rows, top, 0.0)
        yield

    def buffers(which):
        return (turned.at[which], *(planes.at[which, n] for n in range(4)))

    def together(*slots):
        for _ in zip(*(visit(slot, *buffers(which)) for which, slot in enumerate(slots))):
            pass

    def enlist(slot, count):
        @pl.when(live(slot))
        def _():
            listed[count] = slot

        return count + live(slot).astype(jnp.int32)

    count = lax.fori_loop(0, used, enlist, 0)

    threes = jnp.logical_and(count % 2 == 1, count >= 3)

    @pl.loop(0, count // 2 - threes.astype(jnp.int32))
    def _(pair):
        together(listed[2 * pair], listed[2 * pair + 1])

    @pl.when(threes)
    def _():
        together(listed[count - 3], listed[count - 2], listed[count - 1])

    @pl.when(count == 1)
    def _():
        together(listed[0])

    sent = []

    def send(source, target):
        sent.append(pltpu.make_async_copy(source, target, out_sems.at[len(sent)]))
        sent[-1].start()

    last = tiles - 1
    for part in range(2):
        if beyond:
            first_row = 0
            for spill_ref in spill_refs:
                rows = pl.ds(first_row, spill_ref.shape[1])
                send(acc.at[part, last, rows], spill_ref.at[part])
                first_row += spill_ref.shape[1]
        else:
            send(acc.at[part, 0], grad_ref.at[part])
            for column in range(1, tiles):
                send(acc.at[part, column], begun_ref.at[part, column - 1])
    if beyond:
        earlier.wait()
    routing = tiles if beyond else 1

    for chunk in range(height // size):
        rows = pl.ds(chunk * size, size)
        for column in range(routing):
            g_re, g_im = acc[0, column, rows, :], acc[1, column, rows, :]
            if beyond and column < last:
                g_re = g_re + prior[0, column, rows, :]
                g_im = g_im + prior[1, column, rows, :]
                lanes = pl.ds(column * LANES, LANES)
                for part, g in enumerate((g_re, g_im)):
                    acc[part, column, rows, :] = g
                    send(acc.at[part, column, rows], grad_ref.at[part, rows, lanes])
            value = ext[0, column, rows, :] * g_im - ext[1, column, rows, :] * g_re
            residual[column, rows, :] = value
            residual[column, pl.ds(height + chunk * size, size), :] = value

    shift = shift_ref[0]
    for chunk in range(height // size):
        rows = pl.ds(chunk * size, size)
        for column in range(routing):
            lanes = slice(column * LANES, (column + 1) * LANES)
            routed[rows, lanes] = residual[column, pl.ds(height - shift + chunk * size, size), :]
        send(routed.at[rows], routed_ref.at[rows])
    for copy in sent:
        copy.wait()


def margin_kernel(tile_re, tile_im, out, held, sems):
    height = tile_re.shape[0]
    first, second = [], []
    for n, tile in enumerate((tile_re, tile_im)):
        for part in range(2):
            rows = pl.ds(part * height // 2, height // 2)
            source = tile.at[rows, pl.ds(0, LANES)]
            sem = sems.at[2 * n + part]
            first.append(pltpu.make_async_copy(source, held.at[n, rows], sem))
            second.append(pltpu.make_async_copy(held.at[n, rows], out.at[n, rows], sem))
    for copy in first:
        copy.start()
    for before, after in zip(first, second):
        before.wait()
        after.start()
    for copy in second:
        copy.wait()


def margins(tile_re, tile_im):
    shape = (2, tile_re.shape[0], LANES)
    return pl.pallas_call(
        margin_kernel,
        out_shape=jax.ShapeDtypeStruct(shape, jnp.float32),
        in_specs=[HBM, HBM],
        out_specs=HBM,
        scratch_shapes=[pltpu.VMEM(shape, jnp.float32), pltpu.SemaphoreType.DMA((4,))],
        compiler_params=pltpu.CompilerParams(vmem_limit_bytes=VMEM_BYTES),
        name="margins",
    )(tile_re, tile_im)


def probe_phase(used, positions, shift, tile, edge, begun, probe, intensity):
    height, width = tile[0].shape
    size = probe[0].shape[0]
    slots = intensity.shape[0]
    columns = width // LANES
    beyond = edge is not None
    tables, spread = dft_tables(size)
    plane = pltpu.VMEM((size, size), SPLIT)
    planes = pltpu.VMEM((2, columns, height, LANES), jnp.float32)
    routing = columns if beyond else 1

    def out(*shape):
        return jax.ShapeDtypeStruct(shape, jnp.float32)

    if beyond:
        operands = (*tile, edge, begun)
        early = height * 9 // 16 // SUBLANES * SUBLANES
        spills = [out(2, rows, LANES) for rows in (early, height - early)]
        outs = (out(2, height, width - LANES), *spills, out(height, width))
        base = LANES
    else:
        operands = tile
        outs = (out(2, height, LANES), out(2, columns - 1, height, LANES), out(height, LANES))
        base = 0
    return pl.pallas_call(
        functools.partial(probe_kernel, base=base, beyond=beyond),
        out_shape=outs,
        in_specs=[SMEM, SMEM, SMEM, *[HBM if x is not edge else ANY for x in operands], *[HBM] * 5],
        out_specs=(HBM,) * len(outs),
        scratch_shapes=[
            planes, planes,
            pltpu.VMEM((slots, 2, size, LANES), jnp.float32),
            pltpu.VMEM((2, size, size), jnp.float32),
            pltpu.VMEM(tables.shape, SPLIT),
            plane,
            pltpu.VMEM((3, 2, 2, size, LANES), jnp.float32),
            pltpu.VMEM((3, 4, size, size), SPLIT),
            pltpu.VMEM((routing, 2 * height, LANES), jnp.float32),
            pltpu.VMEM((height, outs[-1].shape[1]), jnp.float32),
            pltpu.VMEM((2, columns - 1, height, LANES), jnp.float32),
            pltpu.SMEM((slots,), jnp.int32),
            pltpu.SemaphoreType.DMA((2, 2 * columns + 2)),
            pltpu.SemaphoreType.DMA((slots, 2)),
            pltpu.SemaphoreType.DMA((3 * columns + (2 * columns + 1) * (height // size),)),
        ],
        compiler_params=pltpu.CompilerParams(vmem_limit_bytes=VMEM_BYTES * 21 // 20),
        cost_estimate=pl.CostEstimate(
            flops=26 * slots * size**3, bytes_accessed=16 * height * width, transcendentals=0
        ),
        name="probes_beyond" if beyond else "probes_within",
    )(used, positions, shift, *operands, *probe, intensity, jnp.asarray(tables), jnp.asarray(spread))


def shift_tables(slope, depth):
    numer = jnp.arange(depth, dtype=jnp.int32)[None, :] * slope[:, None]
    whole = jnp.floor_divide(numer, depth)
    return whole, (numer - whole * depth).astype(jnp.float32) / depth


class Turned:
    def __init__(self, band, columns, margin):
        self.band = band
        self.segments = LANES // band
        self.length = columns // self.segments
        self.blocks = self.length // LANES
        self.margin = margin
        self.rows = self.length + 2 * margin

    def scratch(self, count):
        return pltpu.VMEM((count, self.rows, LANES), jnp.float32)

    def store(self, ref, lead, at, value):
        rows = value.shape[0]
        ref[lead, pl.ds(self.margin + at, rows), :] = value
        if at < self.margin:
            ref[lead, pl.ds(self.margin + self.length + at, rows), :] = pltpu.roll(
                value, LANES - self.band, axis=1
            )
        if at >= self.length - self.margin:
            ref[lead, pl.ds(at - self.length + self.margin, rows), :] = pltpu.roll(
                value, self.band, axis=1
            )

    def project(self, whole, frac, ref, tilt, at, rows):
        depth = ref.shape[0]

        def add_level(level, totals):
            plain, weighted = totals
            start = self.margin + at - whole[tilt, level] - SUBLANES
            x = ref[level, pl.ds(start, rows + SUBLANES), :]
            return plain + x[SUBLANES:], weighted + frac[tilt, level] * x

        zero = jnp.zeros((rows + SUBLANES, LANES), jnp.float32)
        plain, weighted = lax.fori_loop(
            0, depth, add_level, (zero[SUBLANES:], zero), unroll=16
        )
        return plain - weighted[SUBLANES:] + weighted[SUBLANES - 1 : SUBLANES - 1 + rows]


def old_kernel(turned, whole, frac, volume, old, cells):
    depth = volume.shape[0]

    @pl.loop(0, depth)
    def _(level):
        for block in range(turned.blocks):
            cut = []
            for segment in range(turned.segments):
                start = segment * turned.length + block * LANES
                cut.append(volume[level, :, start : start + LANES])
            turned.store(cells, level, block * LANES, jnp.concatenate(cut, axis=0).T)

    @pl.loop(0, whole.shape[0])
    def _(tilt):
        for block in range(turned.blocks):
            at = block * LANES
            old[tilt, at : at + LANES, :] = turned.project(whole, frac, cells, tilt, at, LANES)


def step_kernel(
    turned, whole, frac, left, right, old, parts, update,
    near, cells, before, after, sems, level_sems,
):
    old_copy = pltpu.make_async_copy(old, before, sems.at[0, 0])
    depth = cells.shape[0]
    tilts = near.shape[0]
    tiles = right.shape[0] // tilts
    own = right.shape[2] // LANES
    band = turned.band

    old_copy.start()

    def place(block, segment):
        return divmod(segment * turned.blocks + block, own)

    @pl.loop(0, tilts)
    def _(tilt):
        for block in range(turned.blocks):
            cut = []
            for segment in range(turned.segments):
                tile, column = place(block, segment)
                source = tilt * tiles + tile
                if column > 0:
                    value = right[source, :, (column - 1) * LANES : column * LANES]
                elif tile > 0:
                    value = left[source] + right[source - 1, :, (own - 1) * LANES :]
                else:
                    value = left[source]
                cut.append(value)
            value = jnp.concatenate(cut, axis=0).T * (1.0 / tilts)
            turned.store(near, tilt, block * LANES, value)

    rows = LANES // 2

    def keep(level):
        main = cells.at[level, pl.ds(turned.margin, turned.length), :]
        return pltpu.make_async_copy(main, update.at[level], level_sems.at[level])

    @pl.loop(0, depth, unroll=2)
    def _(level):
        for at in range(0, turned.length, rows):
            plain = weighted = None
            for tilt in range(tilts):
                start = turned.margin + at + whole[tilt, level]
                x = near[tilt, pl.ds(start, rows + SUBLANES), :]
                y = frac[tilt, level] * x
                plain = x[:rows] if plain is None else plain + x[:rows]
                weighted = y if weighted is None else weighted + y
            value = plain - weighted[:rows] + weighted[1 : 1 + rows]
            turned.store(cells, level, at, value)
        keep(level).start()

    old_copy.wait()

    def send(tilt):
        block = pl.ds(tilt * tiles, tiles)
        return pltpu.make_async_copy(after.at[block], parts.at[block], sems.at[1, tilt])

    @pl.loop(0, tilts)
    def _(tilt):
        for block in range(turned.blocks):
            at = block * LANES
            before[tilt, at : at + LANES, :] += turned.project(whole, frac, cells, tilt, at, LANES)
        for block in range(turned.blocks):
            total = before[tilt, block * LANES : (block + 1) * LANES, :].T
            for segment in range(turned.segments):
                tile, column = place(block, segment)
                after[tilt * tiles + tile, :, column * LANES : (column + 1) * LANES] = total[
                    segment * band : (segment + 1) * band
                ]

        send(tilt).start()

    for tilt in range(tilts):
        send(tilt).wait()
    for level in range(depth):
        keep(level).wait()


def fresh_kernel(turned, volume, update, fresh):
    for level in range(volume.shape[0]):
        for block in range(turned.blocks):
            value = update[level, block * LANES : (block + 1) * LANES, :].T
            for segment in range(turned.segments):
                start = segment * turned.length + block * LANES
                lanes = slice(start, start + LANES)
                rows = slice(segment * turned.band, (segment + 1) * turned.band)
                fresh[level, :, lanes] = volume[level, :, lanes] + value[rows]


def kernel_options(flops, size, share=1):
    return dict(
        compiler_params=pltpu.CompilerParams(vmem_limit_bytes=int(VMEM_BYTES * share)),
        cost_estimate=pl.CostEstimate(flops=flops, bytes_accessed=size, transcendentals=0),
    )


def old_projection(turned, whole, frac, volume):
    tilts = whole.shape[0]
    return pl.pallas_call(
        functools.partial(old_kernel, turned),
        out_shape=jax.ShapeDtypeStruct((tilts, turned.length, LANES), jnp.float32),
        in_specs=[SMEM, SMEM, VMEM],
        out_specs=VMEM,
        scratch_shapes=[turned.scratch(volume.shape[0])],
        name="old_projection",
        **kernel_options(8 * tilts * volume.size, 4 * volume.size),
    )(whole, frac, volume)


def volume_step(turned, whole, frac, left, right, old):
    tilts, depth = whole.shape
    return pl.pallas_call(
        functools.partial(step_kernel, turned),
        out_shape=(
            jax.ShapeDtypeStruct(right.shape, jnp.float32),
            jax.ShapeDtypeStruct((depth, turned.length, LANES), jnp.float32),
        ),
        in_specs=[SMEM, SMEM, VMEM, VMEM, HBM],
        out_specs=(HBM, HBM),
        scratch_shapes=[
            turned.scratch(tilts), turned.scratch(depth),
            pltpu.VMEM(old.shape, jnp.float32),
            pltpu.VMEM(right.shape, jnp.float32),
            pltpu.SemaphoreType.DMA((2, tilts)),
            pltpu.SemaphoreType.DMA((depth,)),
        ],
        name="volume_step",
        **kernel_options(16 * depth * old.size, 4 * depth * turned.length * LANES, 1),
    )(whole, frac, left, right, old)


def fresh_volume(turned, volume, update):
    depth, band, columns = volume.shape
    levels = math.gcd(depth, 4)
    cells = pl.BlockSpec((levels, band, columns), lambda i: (i, 0, 0))
    flat = pl.BlockSpec((levels, turned.length, LANES), lambda i: (i, 0, 0))
    return pl.pallas_call(
        functools.partial(fresh_kernel, turned),
        grid=(depth // levels,),
        out_shape=jax.ShapeDtypeStruct(volume.shape, jnp.float32),
        in_specs=[cells, flat],
        out_specs=cells,
        name="fresh_volume",
        **kernel_options(volume.size, 12 * volume.size),
    )(volume, update)


def local(
    obj_re, obj_im, probe_re, probe_im, intensity, positions, counts, row_shift, slope, volume
):
    tile = (obj_re[0], obj_im[0])
    height, width = tile[0].shape
    depth, band, columns = volume.shape
    axes = ("tilt", "tile")
    devices = lax.axis_size("tilt") * lax.axis_size("tile")
    turned = Turned(band, columns, width)
    probe = (probe_re, probe_im)

    within = (counts, jnp.swapaxes(positions, 1, 2), row_shift)

    def exchanged(blocks):
        return lax.all_to_all(blocks, axes, split_axis=0, concat_axis=0, tiled=True)

    edge = passed_along(margins(*tile), "tile", -1)
    grad_left, begun, left = probe_phase(*within, tile, None, None, probe, intensity[0])
    left = exchanged(left.reshape(devices, band, LANES))
    grad_right, early, late, right = probe_phase(*within, tile, edge, begun, probe, intensity[0])
    right, left, slope = lax.optimization_barrier((right, left, slope))
    whole, frac = shift_tables(slope, depth)
    right = exchanged(right.reshape(devices, band, width))
    old = old_projection(turned, whole, frac, volume)
    straight = passed_by(late, "tile", 0, 1)
    back = passed_by(late, "tile", 1, -1)
    right, early, old, straight, back = lax.optimization_barrier(
        (right, early, old, straight, back)
    )
    early = passed_along(early, "tile", 1)
    relayed = passed_by(back, "tile", 0, 2)
    parts, update = volume_step(turned, whole, frac, left, right, old)
    parts, early, relayed = lax.optimization_barrier((parts, early, relayed))
    returned = exchanged(parts)
    fresh = fresh_volume(turned, volume, update)
    spill = jnp.concatenate([early, straight + relayed], axis=1)
    grad = jnp.concatenate([grad_left + spill, grad_right], axis=2)[:, None]
    reprojection = jnp.roll(returned.reshape(height, width), -row_shift[0], axis=0)[None]
    return (fresh, reprojection, grad)


def solution(mesh):
    placed = (
        P("tilt", None, "tile"),
        P("tilt", None, "tile"),
        P(),
        P(),
        P("tilt", "tile", None, None),
        P("tilt", "tile", None),
        P("tilt", "tile"),
        P("tilt"),
        P(),
        P(None, ("tilt", "tile"), None),
    )
    return jax.shard_map(
        local,
        mesh=mesh,
        in_specs=placed,
        out_specs=(
            P(None, ("tilt", "tile"), None),
            P("tilt", None, "tile"),
            P(None, "tilt", None, "tile"),
        ),
        check_vma=False,
    )
```

```python
import functools
import math

import jax
import jax.numpy as jnp
import ml_dtypes
import numpy as np
from jax import lax
from jax.experimental import pallas as pl
from jax.experimental.pallas import tpu as pltpu
from jax.sharding import PartitionSpec as P

LANES = 128
SUBLANES = 8
VMEM_BYTES = 60 * 1024 * 1024
PROBE_SCRATCH = 15
SPLIT = jnp.bfloat16
ANY = pl.BlockSpec(memory_space=pl.ANY)
HBM = pl.BlockSpec(memory_space=pltpu.HBM)
SMEM = pl.BlockSpec(memory_space=pltpu.SMEM)
VMEM = pl.BlockSpec(memory_space=pltpu.VMEM)


def passed_along(block, axis, distance):
    devices = range(lax.axis_size(axis))
    route = [(i - distance, i) for i in devices if i - distance in devices]
    return lax.ppermute(block, axis, route)


def passed_by(block, axis, first, step):
    count = lax.axis_size(axis)
    route = [(i, i + step) for i in range(first, count, 2) if 0 <= i + step < count]
    return lax.ppermute(block, axis, route)


def halves(table):
    high = table.astype(ml_dtypes.bfloat16)
    low = (table - high.astype(np.float64)).astype(ml_dtypes.bfloat16)
    return high, low


def dft_tables(length):
    half = length // 2
    index = np.arange(length)
    angle = (index[:, None] * index[None, :] % length) * (-2.0 * math.pi / length)
    wave = (np.cos(angle) + 1j * np.sin(angle)) / math.sqrt(length)
    tables = []
    for parity in (0, 1):
        part = wave[parity::2, :half]
        pair = np.block([[part.real, -part.imag], [part.imag, part.real]])
        tables += [*halves(pair), *halves(pair.T)]
    order = np.concatenate([index[0::2], index[1::2]])
    spread = np.zeros((length, length))
    spread[order, index] = 1.0
    return np.stack(tables), spread.astype(ml_dtypes.bfloat16)


def split(x):
    high = x.astype(SPLIT)
    return high, (x - high.astype(jnp.float32)).astype(SPLIT)


def dot(a, b):
    return jnp.dot(a, b, preferred_element_type=jnp.float32)


def dot3(ah, al, bh, bl):
    return dot(ah, bh) + dot(ah, bl) + dot(al, bh)


def lanes_of(shape):
    return lax.broadcasted_iota(jnp.int32, shape, len(shape) - 1)


def rows_of(shape):
    return lax.broadcasted_iota(jnp.int32, shape, len(shape) - 2)


def rolled(x, row, lane):
    size = x.shape[0]
    tiles = x.shape[1] // LANES
    cut = []
    for tile in range(tiles):
        part = x[:, tile * LANES : (tile + 1) * LANES].reshape(-1, SUBLANES, LANES)
        turned = pltpu.roll(part, row, axis=1)
        before = jnp.concatenate([turned[-1:], turned[:-1]], axis=0)
        part = jnp.where(rows_of(part.shape) < row, before, turned).reshape(size, LANES)
        cut.append(pltpu.roll(part, lane, axis=1))
    keep = lanes_of(cut[0].shape) >= lane
    return [jnp.where(keep, cut[tile], cut[tile - 1]) for tile in range(tiles)]


def probe_kernel(
    used_ref, positions_ref, shift_ref,
    *refs, base, beyond,
):
    if beyond:
        (tile_re, tile_im, edge, begun, probe_re, probe_im, intensity, tables_from, spread_from,
         grad_ref, *spill_refs, routed_ref) = refs[: len(refs) - PROBE_SCRATCH]
    else:
        (tile_re, tile_im, probe_re, probe_im, intensity, tables_from, spread_from,
         grad_ref, begun_ref, routed_ref) = refs[: len(refs) - PROBE_SCRATCH]
    (ext, acc, measured, probes, tables, spread, turned, planes, residual, routed,
     prior, listed, sems, slot_sems, out_sems) = refs[len(refs) - PROBE_SCRATCH :]
    height = ext.shape[2]
    tiles = ext.shape[1]
    size = probes.shape[1]
    half = size // 2
    used = used_ref[0, 0]
    copies = [
        pltpu.make_async_copy(probe_re, probes.at[0], sems.at[0, 2 * tiles]),
        pltpu.make_async_copy(probe_im, probes.at[1], sems.at[0, 2 * tiles + 1]),
        pltpu.make_async_copy(tables_from, tables, sems.at[1, 0]),
        pltpu.make_async_copy(spread_from, spread, sems.at[1, 1]),
    ]
    for part, tile in enumerate((tile_re, tile_im)):
        for column in range(tiles):
            if beyond and column == tiles - 1:
                source = edge.at[part]
            else:
                source = tile.at[:, pl.ds(base + column * LANES, LANES)]
            sem = sems.at[0, part * tiles + column]
            copies.append(pltpu.make_async_copy(source, ext.at[part, column], sem))
    for copy in copies:
        copy.start()

    def fetch(slot):
        return [
            pltpu.make_async_copy(
                intensity.at[slot, :, pl.ds(tile * LANES, LANES)],
                measured.at[slot, tile],
                slot_sems.at[slot, tile],
            )
            for tile in range(2)
        ]

    def mine(slot):
        past = positions_ref[0, 1, slot] + size > base + tiles * LANES
        return past if not beyond else positions_ref[0, 1, slot] + size > base + (tiles - 1) * LANES

    def live(slot):
        return mine(slot) if beyond else jnp.logical_not(mine(slot))

    slots = measured.shape[0]
    for slot in range(slots):
        @pl.when(jnp.logical_and(slot < used, live(slot)))
        def _():
            for copy in fetch(slot):
                copy.start()

    @pl.loop(0, height // size)
    def _(chunk):
        rows = pl.ds(chunk * size, size)
        for part in range(2):
            for column in range(tiles):
                acc[part, column, rows, :] = jnp.zeros((size, LANES), jnp.float32)

    for copy in copies:
        copy.wait()
    if beyond:
        earlier = pltpu.make_async_copy(begun, prior, sems.at[1, 2])
        earlier.start()

    le, let, lo, lot = 0, 2, 4, 6

    def table(which):
        return tables[which], tables[which + 1]

    def visit(slot, turned, uh, ul, vh, vl):
        row = positions_ref[0, 0, slot]
        col = positions_ref[0, 1, slot] - base
        first = pl.multiple_of(row // SUBLANES * SUBLANES, SUBLANES)
        row_rest = row - first
        wrap = pl.multiple_of(jnp.minimum(first + size, height - SUBLANES), SUBLANES)
        column = col // LANES
        lane_rest = col - column * LANES
        wrap_column = jnp.minimum(column + 2, tiles - 1)
        body = pl.ds(first, size)
        tail = pl.ds(wrap, SUBLANES)
        low_rows = rows_of((SUBLANES, LANES)) < row_rest
        low_lanes = lanes_of((size, LANES)) < lane_rest

        for part in range(2):
            for tile, piece in enumerate(rolled(probes[part], row_rest, lane_rest)):
                turned[part, tile] = piece

        def window(part, at):
            block = ext[part, at, body, :]
            top = jnp.where(low_rows, ext[part, at, tail, :], block[:SUBLANES])
            return jnp.concatenate([top, block[SUBLANES:]], axis=0)

        psi = []
        for tile in range(2):
            if tile == 0:
                o_re, o_im = (
                    jnp.where(low_lanes, window(part, wrap_column), window(part, column))
                    for part in range(2)
                )
            else:
                o_re, o_im = (window(part, column + 1) for part in range(2))
            p_re, p_im = turned[0, tile], turned[1, tile]
            psi.append((p_re * o_re - p_im * o_im, p_re * o_im + p_im * o_re))
        for part in range(2):
            lanes = slice(part * LANES, (part + 1) * LANES)
            uh[:, lanes], ul[:, lanes] = split(psi[0][part] + psi[1][part])
            vh[:, lanes], vl[:, lanes] = split(psi[0][part] - psi[1][part])
        yield
        even = dot3(uh[...], ul[...], *table(let))
        odd = dot3(vh[...], vl[...], *table(lot))
        for part in range(2):
            rows = slice(part * half, (part + 1) * half)
            for tile, y in enumerate((even, odd)):
                lanes = slice(tile * LANES, (tile + 1) * LANES)
                y = y[:, part * LANES : (part + 1) * LANES]
                uh[rows, lanes], ul[rows, lanes] = split(y[:half] + y[half:])
                vh[rows, lanes], vl[rows, lanes] = split(y[:half] - y[half:])
        yield
        for copy in fetch(slot):
            copy.wait()
        for parity, (h, l, which) in enumerate(((uh, ul, le), (vh, vl, lo))):
            th, tl = table(which)
            far = dot(th, h[...]) + dot(tl, h[...]) + dot(th, l[...])
            f_re, f_im = far[:half], far[half:]
            m = [measured[slot, tile, pl.ds(parity, half, stride=2), :] for tile in range(2)]
            mh, ml = split(jnp.concatenate(m, axis=1))
            excess = f_re * f_re + f_im * f_im - (dot(mh, spread[...]) + dot(ml, spread[...]))
            h[:half, :], l[:half, :] = split(excess * f_re)
            h[half:, :], l[half:, :] = split(excess * f_im)
        yield
        th, tl = table(let)
        even = dot(th, uh[...]) + dot(tl, uh[...]) + dot(th, ul[...])
        th, tl = table(lot)
        odd = dot(th, vh[...]) + dot(tl, vh[...]) + dot(th, vl[...])
        for part in range(2):
            rows = slice(part * half, (part + 1) * half)
            lanes = slice(part * LANES, (part + 1) * LANES)
            for sign in range(2):
                out = slice(sign * half, (sign + 1) * half)
                t = even[rows] + odd[rows] if sign == 0 else even[rows] - odd[rows]
                uh[out, lanes], ul[out, lanes] = split(t[:, :LANES])
                vh[out, lanes], vl[out, lanes] = split(t[:, LANES:])
        yield
        even = dot3(uh[...], ul[...], *table(le))
        odd = dot3(vh[...], vl[...], *table(lo))
        for tile in range(2):
            chi = even + odd if tile == 0 else even - odd
            c_re, c_im = chi[:, :LANES], chi[:, LANES:]
            p_re, p_im = turned[0, tile], turned[1, tile]
            for part, g in enumerate((p_re * c_re + p_im * c_im, p_re * c_im - p_im * c_re)):
                if tile == 0:
                    places = (
                        (column, jnp.where(low_lanes, 0.0, g)),
                        (wrap_column, jnp.where(low_lanes, g, 0.0)),
                    )
                else:
                    places = ((column + 1, g),)
                for at, value in places:
                    top = value[:SUBLANES]
                    kept = jnp.where(low_rows, 0.0, top)
                    acc[part, at, body, :] += jnp.concatenate([kept, value[SUBLANES:]], axis=0)
                    acc[part, at, tail, :] += jnp.where(low_rows, top, 0.0)
        yield

    def buffers(which):
        return (turned.at[which], *(planes.at[which, n] for n in range(4)))

    def together(*slots):
        for _ in zip(*(visit(slot, *buffers(which)) for which, slot in enumerate(slots))):
            pass

    def enlist(slot, count):
        @pl.when(live(slot))
        def _():
            listed[count] = slot

        return count + live(slot).astype(jnp.int32)

    count = lax.fori_loop(0, used, enlist, 0)

    threes = jnp.logical_and(count % 2 == 1, count >= 3)

    @pl.loop(0, count // 2 - threes.astype(jnp.int32))
    def _(pair):
        together(listed[2 * pair], listed[2 * pair + 1])

    @pl.when(threes)
    def _():
        together(listed[count - 3], listed[count - 2], listed[count - 1])

    @pl.when(count == 1)
    def _():
        together(listed[0])

    sent = []

    def send(source, target):
        sent.append(pltpu.make_async_copy(source, target, out_sems.at[len(sent)]))
        sent[-1].start()

    last = tiles - 1
    for part in range(2):
        if beyond:
            first_row = 0
            for spill_ref in spill_refs:
                rows = pl.ds(first_row, spill_ref.shape[1])
                send(acc.at[part, last, rows], spill_ref.at[part])
                first_row += spill_ref.shape[1]
        else:
            send(acc.at[part, 0], grad_ref.at[part])
            for column in range(1, tiles):
                send(acc.at[part, column], begun_ref.at[part, column - 1])
    if beyond:
        earlier.wait()
    routing = tiles if beyond else 1

    for chunk in range(height // size):
        rows = pl.ds(chunk * size, size)
        for column in range(routing):
            g_re, g_im = acc[0, column, rows, :], acc[1, column, rows, :]
            if beyond and column < last:
                g_re = g_re + prior[0, column, rows, :]
                g_im = g_im + prior[1, column, rows, :]
                lanes = pl.ds(column * LANES, LANES)
                for part, g in enumerate((g_re, g_im)):
                    acc[part, column, rows, :] = g
                    send(acc.at[part, column, rows], grad_ref.at[part, rows, lanes])
            value = ext[0, column, rows, :] * g_im - ext[1, column, rows, :] * g_re
            residual[column, rows, :] = value
            residual[column, pl.ds(height + chunk * size, size), :] = value

    shift = shift_ref[0]
    for chunk in range(height // size):
        rows = pl.ds(chunk * size, size)
        for column in range(routing):
            lanes = slice(column * LANES, (column + 1) * LANES)
            routed[rows, lanes] = residual[column, pl.ds(height - shift + chunk * size, size), :]
        send(routed.at[rows], routed_ref.at[rows])
    for copy in sent:
        copy.wait()


def margin_kernel(tile_re, tile_im, out, held, sems):
    height = tile_re.shape[0]
    first, second = [], []
    for n, tile in enumerate((tile_re, tile_im)):
        for part in range(2):
            rows = pl.ds(part * height // 2, height // 2)
            source = tile.at[rows, pl.ds(0, LANES)]
            sem = sems.at[2 * n + part]
            first.append(pltpu.make_async_copy(source, held.at[n, rows], sem))
            second.append(pltpu.make_async_copy(held.at[n, rows], out.at[n, rows], sem))
    for copy in first:
        copy.start()
    for before, after in zip(first, second):
        before.wait()
        after.start()
    for copy in second:
        copy.wait()


def margins(tile_re, tile_im):
    shape = (2, tile_re.shape[0], LANES)
    return pl.pallas_call(
        margin_kernel,
        out_shape=jax.ShapeDtypeStruct(shape, jnp.float32),
        in_specs=[HBM, HBM],
        out_specs=HBM,
        scratch_shapes=[pltpu.VMEM(shape, jnp.float32), pltpu.SemaphoreType.DMA((4,))],
        compiler_params=pltpu.CompilerParams(vmem_limit_bytes=VMEM_BYTES),
        name="margins",
    )(tile_re, tile_im)


def probe_phase(used, positions, shift, tile, edge, begun, probe, intensity):
    height, width = tile[0].shape
    size = probe[0].shape[0]
    slots = intensity.shape[0]
    columns = width // LANES
    beyond = edge is not None
    tables, spread = dft_tables(size)
    plane = pltpu.VMEM((size, size), SPLIT)
    planes = pltpu.VMEM((2, columns, height, LANES), jnp.float32)
    routing = columns if beyond else 1

    def out(*shape):
        return jax.ShapeDtypeStruct(shape, jnp.float32)

    if beyond:
        operands = (*tile, edge, begun)
        early = height // 2 // SUBLANES * SUBLANES
        spills = [out(2, rows, LANES) for rows in (early, height - early)]
        outs = (out(2, height, width - LANES), *spills, out(height, width))
        base = LANES
    else:
        operands = tile
        outs = (out(2, height, LANES), out(2, columns - 1, height, LANES), out(height, LANES))
        base = 0
    return pl.pallas_call(
        functools.partial(probe_kernel, base=base, beyond=beyond),
        out_shape=outs,
        in_specs=[SMEM, SMEM, SMEM, *[HBM if x is not edge else ANY for x in operands], *[HBM] * 5],
        out_specs=(HBM,) * len(outs),
        scratch_shapes=[
            planes, planes,
            pltpu.VMEM((slots, 2, size, LANES), jnp.float32),
            pltpu.VMEM((2, size, size), jnp.float32),
            pltpu.VMEM(tables.shape, SPLIT),
            plane,
            pltpu.VMEM((3, 2, 2, size, LANES), jnp.float32),
            pltpu.VMEM((3, 4, size, size), SPLIT),
            pltpu.VMEM((routing, 2 * height, LANES), jnp.float32),
            pltpu.VMEM((height, outs[-1].shape[1]), jnp.float32),
            pltpu.VMEM((2, columns - 1, height, LANES), jnp.float32),
            pltpu.SMEM((slots,), jnp.int32),
            pltpu.SemaphoreType.DMA((2, 2 * columns + 2)),
            pltpu.SemaphoreType.DMA((slots, 2)),
            pltpu.SemaphoreType.DMA((3 * columns + (2 * columns + 1) * (height // size),)),
        ],
        compiler_params=pltpu.CompilerParams(vmem_limit_bytes=VMEM_BYTES * 21 // 20),
        cost_estimate=pl.CostEstimate(
            flops=26 * slots * size**3, bytes_accessed=16 * height * width, transcendentals=0
        ),
        name="probes_beyond" if beyond else "probes_within",
    )(used, positions, shift, *operands, *probe, intensity, jnp.asarray(tables), jnp.asarray(spread))


def shift_tables(slope, depth):
    numer = jnp.arange(depth, dtype=jnp.int32)[None, :] * slope[:, None]
    whole = jnp.floor_divide(numer, depth)
    return whole, (numer - whole * depth).astype(jnp.float32) / depth


class Turned:
    def __init__(self, band, columns, margin):
        self.band = band
        self.segments = LANES // band
        self.length = columns // self.segments
        self.blocks = self.length // LANES
        self.margin = margin
        self.rows = self.length + 2 * margin

    def scratch(self, count):
        return pltpu.VMEM((count, self.rows, LANES), jnp.float32)

    def store(self, ref, lead, at, value):
        rows = value.shape[0]
        ref[lead, pl.ds(self.margin + at, rows), :] = value
        if at < self.margin:
            ref[lead, pl.ds(self.margin + self.length + at, rows), :] = pltpu.roll(
                value, LANES - self.band, axis=1
            )
        if at >= self.length - self.margin:
            ref[lead, pl.ds(at - self.length + self.margin, rows), :] = pltpu.roll(
                value, self.band, axis=1
            )

    def project(self, whole, frac, ref, tilt, at, rows):
        depth = ref.shape[0]

        def add_level(level, totals):
            plain, weighted = totals
            start = self.margin + at - whole[tilt, level] - SUBLANES
            x = ref[level, pl.ds(start, rows + SUBLANES), :]
            return plain + x[SUBLANES:], weighted + frac[tilt, level] * x

        zero = jnp.zeros((rows + SUBLANES, LANES), jnp.float32)
        plain, weighted = lax.fori_loop(
            0, depth, add_level, (zero[SUBLANES:], zero), unroll=16
        )
        return plain - weighted[SUBLANES:] + weighted[SUBLANES - 1 : SUBLANES - 1 + rows]


def old_kernel(turned, whole, frac, volume, old, cells):
    depth = volume.shape[0]

    @pl.loop(0, depth)
    def _(level):
        for block in range(turned.blocks):
            cut = []
            for segment in range(turned.segments):
                start = segment * turned.length + block * LANES
                cut.append(volume[level, :, start : start + LANES])
            turned.store(cells, level, block * LANES, jnp.concatenate(cut, axis=0).T)

    @pl.loop(0, whole.shape[0])
    def _(tilt):
        for block in range(turned.blocks):
            at = block * LANES
            old[tilt, at : at + LANES, :] = turned.project(whole, frac, cells, tilt, at, LANES)


def step_kernel(
    turned, whole, frac, left, right, old, parts, update,
    near, cells, before, after, sems, level_sems,
):
    old_copy = pltpu.make_async_copy(old, before, sems.at[0, 0])
    depth = cells.shape[0]
    tilts = near.shape[0]
    tiles = right.shape[0] // tilts
    own = right.shape[2] // LANES
    band = turned.band

    old_copy.start()

    def place(block, segment):
        return divmod(segment * turned.blocks + block, own)

    @pl.loop(0, tilts)
    def _(tilt):
        for block in range(turned.blocks):
            cut = []
            for segment in range(turned.segments):
                tile, column = place(block, segment)
                source = tilt * tiles + tile
                if column > 0:
                    value = right[source, :, (column - 1) * LANES : column * LANES]
                elif tile > 0:
                    value = left[source] + right[source - 1, :, (own - 1) * LANES :]
                else:
                    value = left[source]
                cut.append(value)
            value = jnp.concatenate(cut, axis=0).T * (1.0 / tilts)
            turned.store(near, tilt, block * LANES, value)

    rows = LANES // 2

    def keep(level):
        main = cells.at[level, pl.ds(turned.margin, turned.length), :]
        return pltpu.make_async_copy(main, update.at[level], level_sems.at[level])

    @pl.loop(0, depth, unroll=2)
    def _(level):
        for at in range(0, turned.length, rows):
            plain = weighted = None
            for tilt in range(tilts):
                start = turned.margin + at + whole[tilt, level]
                x = near[tilt, pl.ds(start, rows + SUBLANES), :]
                y = frac[tilt, level] * x
                plain = x[:rows] if plain is None else plain + x[:rows]
                weighted = y if weighted is None else weighted + y
            value = plain - weighted[:rows] + weighted[1 : 1 + rows]
            turned.store(cells, level, at, value)
        keep(level).start()

    old_copy.wait()

    def send(tilt):
        block = pl.ds(tilt * tiles, tiles)
        return pltpu.make_async_copy(after.at[block], parts.at[block], sems.at[1, tilt])

    @pl.loop(0, tilts)
    def _(tilt):
        for block in range(turned.blocks):
            at = block * LANES
            before[tilt, at : at + LANES, :] += turned.project(whole, frac, cells, tilt, at, LANES)
        for block in range(turned.blocks):
            total = before[tilt, block * LANES : (block + 1) * LANES, :].T
            for segment in range(turned.segments):
                tile, column = place(block, segment)
                after[tilt * tiles + tile, :, column * LANES : (column + 1) * LANES] = total[
                    segment * band : (segment + 1) * band
                ]

        send(tilt).start()

    for tilt in range(tilts):
        send(tilt).wait()
    for level in range(depth):
        keep(level).wait()


def fresh_kernel(turned, volume, update, fresh):
    for level in range(volume.shape[0]):
        for block in range(turned.blocks):
            value = update[level, block * LANES : (block + 1) * LANES, :].T
            for segment in range(turned.segments):
                start = segment * turned.length + block * LANES
                lanes = slice(start, start + LANES)
                rows = slice(segment * turned.band, (segment + 1) * turned.band)
                fresh[level, :, lanes] = volume[level, :, lanes] + value[rows]


def kernel_options(flops, size, share=1):
    return dict(
        compiler_params=pltpu.CompilerParams(vmem_limit_bytes=int(VMEM_BYTES * share)),
        cost_estimate=pl.CostEstimate(flops=flops, bytes_accessed=size, transcendentals=0),
    )


def old_projection(turned, whole, frac, volume):
    tilts = whole.shape[0]
    return pl.pallas_call(
        functools.partial(old_kernel, turned),
        out_shape=jax.ShapeDtypeStruct((tilts, turned.length, LANES), jnp.float32),
        in_specs=[SMEM, SMEM, VMEM],
        out_specs=VMEM,
        scratch_shapes=[turned.scratch(volume.shape[0])],
        name="old_projection",
        **kernel_options(8 * tilts * volume.size, 4 * volume.size),
    )(whole, frac, volume)


def volume_step(turned, whole, frac, left, right, old):
    tilts, depth = whole.shape
    return pl.pallas_call(
        functools.partial(step_kernel, turned),
        out_shape=(
            jax.ShapeDtypeStruct(right.shape, jnp.float32),
            jax.ShapeDtypeStruct((depth, turned.length, LANES), jnp.float32),
        ),
        in_specs=[SMEM, SMEM, VMEM, VMEM, HBM],
        out_specs=(HBM, HBM),
        scratch_shapes=[
            turned.scratch(tilts), turned.scratch(depth),
            pltpu.VMEM(old.shape, jnp.float32),
            pltpu.VMEM(right.shape, jnp.float32),
            pltpu.SemaphoreType.DMA((2, tilts)),
            pltpu.SemaphoreType.DMA((depth,)),
        ],
        name="volume_step",
        **kernel_options(16 * depth * old.size, 4 * depth * turned.length * LANES, 1),
    )(whole, frac, left, right, old)


def fresh_volume(turned, volume, update):
    depth, band, columns = volume.shape
    levels = math.gcd(depth, 4)
    cells = pl.BlockSpec((levels, band, columns), lambda i: (i, 0, 0))
    flat = pl.BlockSpec((levels, turned.length, LANES), lambda i: (i, 0, 0))
    return pl.pallas_call(
        functools.partial(fresh_kernel, turned),
        grid=(depth // levels,),
        out_shape=jax.ShapeDtypeStruct(volume.shape, jnp.float32),
        in_specs=[cells, flat],
        out_specs=cells,
        name="fresh_volume",
        **kernel_options(volume.size, 12 * volume.size),
    )(volume, update)


def local(
    obj_re, obj_im, probe_re, probe_im, intensity, positions, counts, row_shift, slope, volume
):
    tile = (obj_re[0], obj_im[0])
    height, width = tile[0].shape
    depth, band, columns = volume.shape
    axes = ("tilt", "tile")
    devices = lax.axis_size("tilt") * lax.axis_size("tile")
    turned = Turned(band, columns, width)
    probe = (probe_re, probe_im)

    within = (counts, jnp.swapaxes(positions, 1, 2), row_shift)

    def exchanged(blocks):
        return lax.all_to_all(blocks, axes, split_axis=0, concat_axis=0, tiled=True)

    edge = passed_along(margins(*tile), "tile", -1)
    grad_left, begun, left = probe_phase(*within, tile, None, None, probe, intensity[0])
    left = exchanged(left.reshape(devices, band, LANES))
    grad_right, early, late, right = probe_phase(*within, tile, edge, begun, probe, intensity[0])
    right, left, slope = lax.optimization_barrier((right, left, slope))
    whole, frac = shift_tables(slope, depth)
    right = exchanged(right.reshape(devices, band, width))
    old = old_projection(turned, whole, frac, volume)
    straight = passed_by(late, "tile", 0, 1)
    back = passed_by(late, "tile", 1, -1)
    right, early, old, straight, back = lax.optimization_barrier(
        (right, early, old, straight, back)
    )
    early = passed_along(early, "tile", 1)
    relayed = passed_by(back, "tile", 0, 2)
    parts, update = volume_step(turned, whole, frac, left, right, old)
    parts, early, relayed = lax.optimization_barrier((parts, early, relayed))
    returned = exchanged(parts)
    fresh = fresh_volume(turned, volume, update)
    spill = jnp.concatenate([early, straight + relayed], axis=1)
    grad = jnp.concatenate([grad_left + spill, grad_right], axis=2)[:, None]
    reprojection = jnp.roll(returned.reshape(height, width), -row_shift[0], axis=0)[None]
    return (fresh, reprojection, grad)


def solution(mesh):
    placed = (
        P("tilt", None, "tile"),
        P("tilt", None, "tile"),
        P(),
        P(),
        P("tilt", "tile", None, None),
        P("tilt", "tile", None),
        P("tilt", "tile"),
        P("tilt"),
        P(),
        P(None, ("tilt", "tile"), None),
    )
    return jax.shard_map(
        local,
        mesh=mesh,
        in_specs=placed,
        out_specs=(
            P(None, ("tilt", "tile"), None),
            P("tilt", None, "tile"),
            P(None, "tilt", None, "tile"),
        ),
        check_vma=False,
    )
```
